128 devices in a mesh: rows: 32 (over y, x_lo, z), cols: 4 (over x_hi, core).
Axes of the slice: x: 4 (x_hi: 2, x_lo: 2; x = x_hi * 2 + x_lo), y: 4, z: 4, core: 2. Of those that a mesh axis runs over, the one named last changes fastest.
Arguments:
- features_in: bfloat16 [1024, 512, 128], P('rows', 'cols'), may hold values from -6 to 6
- cotangent: bfloat16 [1024, 512, 128], P('rows', 'cols'), may hold values from -6 to 6
- depth_kernels: bfloat16 [8, 9, 128], replicated, may hold values from -2 to 2
- point_weights: bfloat16 [8, 128, 128], replicated, may hold values from -0.5 to 0.5
- coarse_weight: bfloat16 [128, 128], replicated, may hold values from -4 to 4
Outputs:
- output: bfloat16 [1024, 512, 128], P('rows', 'cols')
- input_grad: bfloat16 [1024, 512, 128], P('rows', 'cols')
- weight_grads: float32 [9, 128, 128], P(None, 'rows')
The draws below stay inside these ranges and needn't reach their ends.
All inputs are finite; a program needn't handle non-finite values.
Results may differ from the reference program's by a relative error of at most 0.039.
Values may be sent and summed in bfloat16 or wider, within the bound.
No kernel may reach another device: no remote copies, remote signals or barrier semaphores. Data moves between devices by JAX's collectives and lax.ppermute only.
A program may use at most 128 MiB of HBM per device.

```python
import jax
import jax.numpy as jnp
from jax import lax

C = 128
L = 8
STRIDE = 8
H = 1024
W = 512


def level_of(rng, dims, pieces, low, largest):
    def one(position, parts):
        steps = jax.random.uniform(jax.random.fold_in(jax.random.fold_in(rng, 6), position), (parts,), jnp.float32, low / len(pieces), largest / len(pieces))
        return jnp.repeat(jnp.exp(steps), dims[position] // parts).reshape((-1,) + (1,) * (len(dims) - position - 1))

    factor_of = one(*pieces[0])
    for cut in pieces[1:]:
        factor_of = factor_of * one(*cut)
    return factor_of


def gaussian(rng, shape, width, reach, pieces=(), kind=jnp.bfloat16):
    loudness = level_of(rng, shape, pieces, -0.22, 0.18) if pieces else 1.0
    array = jax.random.normal(rng, shape, jnp.float32) * width * loudness
    return jnp.minimum(jnp.maximum(array, -reach), reach).astype(kind)


def setup_inputs(seed: int = 0) -> dict:
    key_of = jax.random.split(jax.random.key(seed), 6)
    return {
        "features_in": gaussian(key_of[0], (H, W, C), 1.0, 6.0, ((0, 32), (1, 4))),
        "cotangent": gaussian(key_of[1], (H, W, C), 1.0, 6.0, ((0, 32), (1, 4))),
        "depth_kernels": gaussian(key_of[2], (L, 9, C), 9 ** -0.5, 2.0),
        "point_weights": gaussian(key_of[3], (L, C, C), C ** -0.5, 0.5),
        "coarse_weight": gaussian(key_of[4], (C, C), (C // 64) ** -0.5, 4.0),
    }


def gelu_tanh(value):
    return jax.nn.gelu(value, approximate=True)

def taps(padded, kernel, dilate, base, height, breadth, sign):
    total = jnp.zeros((height, breadth, padded.shape[2]), jnp.float32)
    for shift_row in (-1, 0, 1):
        for shift_col in (-1, 0, 1):
            index = (shift_row + 1) * 3 + (shift_col + 1)
            start_row = base + sign * shift_row * dilate
            start_col = base + sign * shift_col * dilate
            piece = padded[start_row:start_row + height, start_col:start_col + breadth, :]
            total = total + kernel[index].astype(jnp.float32) * piece.astype(jnp.float32)
    return total

def forward_layer(x_now, kernel, weight, dilate):
    height, breadth, channels = x_now.shape
    padded = jnp.pad(x_now, ((dilate, dilate), (dilate, dilate), (0, 0)))
    preact = taps(padded, kernel, dilate, dilate, height, breadth, 1)
    hidden = gelu_tanh(preact).astype(jnp.bfloat16)
    return (preact, hidden)

def reference(features_in, cotangent, depth_kernels, point_weights, coarse_weight):
    height, breadth, channels = features_in.shape
    contract = (((0,), (0,)), ((), ()))
    x_now = features_in
    saved = []
    for layer in range(L):
        dilate = 2 ** (layer % 4)
        saved.append(x_now)
        preact, hidden = forward_layer(x_now, depth_kernels[layer], point_weights[layer], dilate)
        mixed = jnp.dot(hidden.reshape(-1, channels), point_weights[layer], preferred_element_type=jnp.float32)
        x_now = (x_now.astype(jnp.float32) + mixed.reshape(height, breadth, channels)).astype(jnp.bfloat16)
    blocks = (height // STRIDE, STRIDE, breadth // STRIDE, STRIDE, channels)
    pooled = features_in.astype(jnp.float32).reshape(blocks).mean(axis=(1, 3)).astype(jnp.bfloat16)
    coarse = jnp.dot(pooled.reshape(-1, channels), coarse_weight, preferred_element_type=jnp.float32)
    coarse = coarse.reshape(height // STRIDE, 1, breadth // STRIDE, 1, channels)
    output = (x_now.astype(jnp.float32).reshape(blocks) + coarse).reshape(height, breadth, channels).astype(jnp.bfloat16)
    block_cot = cotangent.astype(jnp.float32).reshape(blocks).sum(axis=(1, 3)).astype(jnp.bfloat16)
    coarse_grad = lax.dot_general(pooled.reshape(-1, channels), block_cot.reshape(-1, channels), contract, preferred_element_type=jnp.float32)
    back = jnp.dot(block_cot.reshape(-1, channels), coarse_weight.T, preferred_element_type=jnp.float32) / (STRIDE * STRIDE)
    back = back.reshape(height // STRIDE, 1, breadth // STRIDE, 1, channels)
    upstream = cotangent.astype(jnp.float32)
    grads = [None] * L
    for layer in range(L - 1, -1, -1):
        dilate = 2 ** (layer % 4)
        preact, hidden = forward_layer(saved[layer], depth_kernels[layer], point_weights[layer], dilate)
        up_b = upstream.astype(jnp.bfloat16).reshape(-1, channels)
        grads[layer] = lax.dot_general(hidden.reshape(-1, channels), up_b, contract, preferred_element_type=jnp.float32)
        hid_grad = jnp.dot(up_b, point_weights[layer].T, preferred_element_type=jnp.float32).reshape(height, breadth, channels)
        pull = jax.vjp(gelu_tanh, preact)[1]
        pre_grad = pull(hid_grad)[0]
        padded = jnp.pad(pre_grad, ((dilate, dilate), (dilate, dilate), (0, 0)))
        upstream = upstream + taps(padded, depth_kernels[layer], dilate, dilate, height, breadth, -1)
    input_grad = (upstream.reshape(blocks) + back).reshape(height, breadth, channels).astype(jnp.bfloat16)
    weight_grads = jnp.stack(grads + [coarse_grad])
    return (output, input_grad, weight_grads)
```

```python
import functools

import jax
import jax.numpy as jnp
from jax import lax
from jax.experimental import pallas as pl
from jax.experimental.pallas import tpu as pltpu
from jax.sharding import PartitionSpec as P

STRIDE = 8
F32 = jnp.float32
BF = jnp.bfloat16
C0 = 0.7978845608028654
C1 = 0.7978845608028654 * 0.044715

ROWS, COLS, CH = 32, 128, 128
RH, CHALO = 15, 16
WIDE = COLS + 2 * CHALO
PAD = 8

HALO = (14, 12, 8, 0)
SPAN = ((0, 160), (0, 160), (8, 152), (16, 144))
DHALO = (2, 4, 8, 0)
DSPAN = ((8, 152), (8, 152), (8, 152), (16, 144))
BLOCK = (15, 14, 16, 16)

VMEM = pl.BlockSpec(memory_space=pltpu.VMEM)
SMEM = pl.BlockSpec(memory_space=pltpu.SMEM)
ANY = pl.BlockSpec(memory_space=pl.ANY)


def sds(shape, dtype):
    return jax.ShapeDtypeStruct(shape, dtype)


def gelu_parts(half, want_slope):
    square = half * half
    t = jnp.tanh(half * (2 * C0 + 8 * C1 * square))
    half_t = half * t
    hidden = half + half_t
    if not want_slope:
        return hidden, None
    slope = (0.5 + 0.5 * t) + (half - half_t * t) * (C0 + 12 * C1 * square)
    return hidden, slope


def rows_of(kernel, scale):
    return [jnp.broadcast_to(kernel[t : t + 1, :] * scale, (8, CH))[None] for t in range(9)]


def tap_sum(src, row, col, width, dilate, sign, taps, which, start=None):
    total = start
    for i in which:
        for j in (-1, 0, 1):
            at = col + sign * j * dilate
            piece = src[row + sign * i * dilate, at : at + width, :].reshape(width // 8, 8, CH)
            piece = piece * taps[(i + 1) * 3 + j + 1]
            total = piece if total is None else total + piece
    return total


def chunks(low, high, size):
    out = []
    while low < high:
        out.append((low, min(size, high - low)))
        low += size
    return out


def clear_outside(ref, edges, rows_top, rows_bottom, col_left, col_right):
    count = ref.shape[0]
    breadth = ref.shape[1]

    @pl.when(edges[0] == 1)
    def _():
        ref[0:rows_top] = jnp.zeros((rows_top, breadth, CH), F32)

    @pl.when(edges[1] == 1)
    def _():
        ref[count - rows_bottom : count] = jnp.zeros((rows_bottom, breadth, CH), F32)

    @pl.when(edges[2] == 1)
    def _():
        ref[:, col_left : col_left + CHALO] = jnp.zeros((count, CHALO, CH), F32)

    @pl.when(edges[3] == 1)
    def _():
        ref[:, col_right : col_right + CHALO] = jnp.zeros((count, CHALO, CH), F32)


def grad_of(hidden, upstream):
    return lax.dot_general(
        hidden.reshape(-1, CH),
        upstream.reshape(-1, CH),
        (((0,), (0,)), ((), ())),
        preferred_element_type=F32,
    )


def forward_kernel(last, *refs):
    refs = list(refs)
    take = lambda n: [refs.pop(0) for _ in range(n)]
    edges, own, left, right, top, bottom, kernels, weights = take(8)
    if last:
        coarse, cot, back_weight = take(3)
        out, pre, pre_left, pre_right, grad = take(5)
        kept = take(3 + 3)
    else:
        x_out, x_left, x_right = take(3)
        kept = take(4 + 4)
    count = len(kept) // 2
    hid_out, slope_out = kept[:count], kept[count:]
    x_bufs = take(2)
    h_bufs = take(4)
    hid_two = take(1)[0]
    slopes = take(4)
    sem = take(1)[0]
    own_buf = take(1)[0]

    def build(r, _):
        x_bufs[0][RH + r, PAD : PAD + 16] = left[r].astype(F32)
        x_bufs[0][RH + r, PAD + 16 : PAD + 144] = own[r].astype(F32)
        x_bufs[0][RH + r, PAD + 144 : PAD + 160] = right[r].astype(F32)
        return 0

    lax.fori_loop(0, ROWS, build, 0)

    def build_ends(r, _):
        x_bufs[0][r, PAD : PAD + WIDE] = top[r].astype(F32)
        x_bufs[0][RH + ROWS + r, PAD : PAD + WIDE] = bottom[r].astype(F32)
        return 0

    lax.fori_loop(0, RH, build_ends, 0)

    copies = []
    for layer in range(4):
        dilate = 2**layer
        halo = HALO[layer]
        low, high = SPAN[layer]
        breadth = high - low
        dhalo = DHALO[layer]
        dlow, dhigh = DSPAN[layer]
        src, dst = x_bufs[layer % 2], x_bufs[(layer + 1) % 2]
        h_buf, slope_buf = h_bufs[layer], slopes[layer]
        taps = rows_of(kernels[layer], 0.5)

        def act_rows(r, number, want_slope, own_rows):
            for q in range(number):
                hid_parts, slope_parts = [], []
                for c, width in chunks(low, high, 32):
                    half = tap_sum(
                        src, RH + r + q, PAD + c, width, dilate, 1, taps, (-1, 0, 1)
                    )
                    hidden, slope = gelu_parts(half, want_slope)
                    hid_parts.append(hidden.reshape(width, CH))
                    if want_slope:
                        slope_parts.append(slope.reshape(width, CH))
                hidden = jnp.concatenate(hid_parts, 0)
                h_buf[halo + r + q] = hidden.astype(BF)
                if layer == 2 and own_rows:
                    hid_two[r + q] = hidden[8:136].astype(BF)
                if want_slope:
                    slope = jnp.concatenate(slope_parts, 0)
                    slope_buf[dhalo + r + q] = slope[dlow - low : dhigh - low].astype(BF)

        number = 4
        outer = halo - dhalo
        if outer:
            each = outer // number

            def outer_body(it, _):
                r = jnp.where(it < each, it * number - halo, ROWS + dhalo + (it - each) * number)
                act_rows(r, number, False, False)
                return 0

            lax.fori_loop(0, 2 * each, outer_body, 0)
        if layer == 2:

            def ring_body(it, _):
                r = jnp.where(it < 2, it * number - halo, ROWS + (it - 2) * number)
                act_rows(r, number, True, False)
                return 0

            lax.fori_loop(0, 4, ring_body, 0)
            first, rows_here = 0, ROWS
        else:
            first, rows_here = -dhalo, ROWS + 2 * dhalo

        def inner_body(it, _):
            act_rows(first + it * number, number, True, True)
            return 0

        lax.fori_loop(0, rows_here // number, inner_body, 0)

        if layer < count:
            if layer == 2:
                hid_src = hid_two
            else:
                hid_src = h_buf.at[pl.ds(halo, ROWS), pl.ds(16 - low, COLS)]
            copies.append(pltpu.make_async_copy(hid_src, hid_out[layer], sem.at[layer]))
            copies.append(pltpu.make_async_copy(slope_buf, slope_out[layer], sem.at[4 + layer]))
            copies[-1].start()
            copies[-2].start()

        step = BLOCK[layer]
        total = ROWS + 2 * halo

        def mix_body(it, _):
            at = it * step
            mixed = jnp.dot(
                h_buf[pl.ds(at, step)].reshape(step * breadth, CH),
                weights[layer],
                preferred_element_type=F32,
            ).reshape(step, breadth, CH)
            rows = pl.ds(RH - halo + at, step)
            value = src[rows, PAD + low : PAD + high] + mixed
            if layer < 3:
                dst[rows, PAD + low : PAD + high] = value
            elif last:
                for q in range(step // STRIDE):
                    extra = coarse[it * (step // STRIDE) + q][:, None, :]
                    part = value[q * STRIDE : (q + 1) * STRIDE].reshape(STRIDE, -1, STRIDE, CH)
                    part = (part + extra[None]).reshape(STRIDE, COLS, CH)
                    own_buf[pl.ds(at + q * STRIDE, STRIDE)] = part.astype(BF)
            else:
                value = value.astype(BF)
                own_buf[pl.ds(at, step)] = value
                x_left[pl.ds(at, step)] = value[:, :CHALO]
                x_right[pl.ds(at, step)] = value[:, COLS - CHALO :]
            return 0

        lax.fori_loop(0, total // step, mix_body, 0)
        if layer < 3:
            clear_outside(dst, edges, RH, RH, PAD, PAD + 16 + COLS)

    result = out if last else x_out
    copies.append(pltpu.make_async_copy(own_buf, result, sem.at[8]))
    copies[-1].start()
    if last:
        total = jnp.zeros((CH, CH), F32)
        for b in range(2):
            rows = slice(16 * b, 16 * b + 16)
            up = cot[rows]
            total = total + grad_of(h_bufs[3][rows], up)
            pulled = jnp.dot(up.reshape(-1, CH), back_weight[...], preferred_element_type=F32)
            value = pulled.reshape(16, COLS, CH) * slopes[3][rows].astype(F32)
            value = value.astype(BF)
            pre[rows] = value
            pre_left[rows] = value[:, :CHALO]
            pre_right[rows] = value[:, COLS - CHALO :]
        grad[...] = total
    for copy in copies:
        copy.wait()


def forward(last, edges, own, left, right, top, bottom, kernels, weights, extra=()):
    count = 3 if last else 4
    block = sds((ROWS, COLS, CH), BF)
    strip = sds((ROWS, CHALO, CH), BF)
    hid_shapes = [block] * count
    slope_shapes = [
        sds((ROWS + 2 * DHALO[k], DSPAN[k][1] - DSPAN[k][0], CH), BF) for k in range(4)
    ]
    if last:
        outs = [block, block, strip, strip, sds((CH, CH), F32)]
        specs = [ANY] + [VMEM] * 4
    else:
        outs = [block, strip, strip]
        specs = [ANY, VMEM, VMEM]
    outs = outs + hid_shapes + slope_shapes[:count]
    specs = specs + [ANY] * (2 * count)
    scratch = [pltpu.VMEM((ROWS + 2 * RH, WIDE + 2 * PAD, CH), F32)] * 2
    scratch += [
        pltpu.VMEM((ROWS + 2 * HALO[k], SPAN[k][1] - SPAN[k][0], CH), BF) for k in range(4)
    ]
    scratch += [pltpu.VMEM((ROWS, COLS, CH), BF)]
    scratch += [pltpu.VMEM(s.shape, BF) for s in slope_shapes]
    scratch += [pltpu.SemaphoreType.DMA((9,)), pltpu.VMEM((ROWS, COLS, CH), BF)]
    return pl.pallas_call(
        functools.partial(forward_kernel, last),
        out_shape=outs,
        in_specs=[SMEM] + [VMEM] * (7 + len(extra)),
        out_specs=specs,
        scratch_shapes=scratch,
        compiler_params=pltpu.CompilerParams(vmem_limit_bytes=52 * 2**20),
        cost_estimate=pl.CostEstimate(
            flops=4 * 2 * 8000 * CH * CH, bytes_accessed=12 * 2**20, transcendentals=0
        ),
        name="forward_last" if last else "forward_first",
    )(edges, own, left, right, top, bottom, kernels, weights, *extra)


def pool_kernel(feature, cot, weight, weight_t, coarse, back, grad):
    total = None
    for b in range(ROWS // STRIDE):
        rows = slice(STRIDE * b, STRIDE * (b + 1))

        def block_sum(ref):
            value = ref[STRIDE * b].astype(F32)
            for r in range(1, STRIDE):
                value = value + ref[STRIDE * b + r].astype(F32)
            return value.reshape(COLS // STRIDE, STRIDE, CH).sum(axis=1)

        pooled = (block_sum(feature) * (1.0 / (STRIDE * STRIDE))).astype(BF)
        block_cot = block_sum(cot).astype(BF)
        coarse[b] = jnp.dot(pooled, weight[...], preferred_element_type=F32)
        back[b] = jnp.dot(block_cot, weight_t[...], preferred_element_type=F32) * (
            1.0 / (STRIDE * STRIDE)
        )
        part = grad_of(pooled, block_cot)
        total = part if total is None else total + part
    grad[...] = total


def pool(feature, cot, weight):
    small = sds((ROWS // STRIDE, COLS // STRIDE, CH), F32)
    return pl.pallas_call(
        pool_kernel,
        out_shape=[small, small, sds((CH, CH), F32)],
        in_specs=[VMEM] * 4,
        out_specs=[VMEM] * 3,
        compiler_params=pltpu.CompilerParams(vmem_limit_bytes=16 * 2**20),
        cost_estimate=pl.CostEstimate(flops=10**8, bytes_accessed=2 * 2**20, transcendentals=0),
        name="pool",
    )(feature, cot, weight, weight.T)


BASE = 8


def ends_kernel(pre, pre_left, pre_right, base, base_left, base_right, kernel, up, down, buf):
    taps = rows_of(kernel, 1.0)

    def build(r, _):
        buf[r, 0:16] = pre_left[r].astype(F32)
        buf[r, 16:144] = pre[r].astype(F32)
        buf[r, 144:160] = pre_right[r].astype(F32)
        return 0

    lax.fori_loop(0, ROWS, build, 0)
    zeros = jnp.zeros((8, CH), F32)

    def one(r, which):
        parts = []
        for c, width in chunks(8, 152, 32):
            parts.append(tap_sum(buf, r, c, width, 8, -1, taps, which).reshape(width, CH))
        middle = jnp.concatenate(parts, 0)
        ends = jnp.concatenate(
            [
                base_left[r].astype(F32)[8:16],
                base[r].astype(F32),
                base_right[r].astype(F32)[0:8],
            ],
            0,
        )
        return jnp.concatenate([zeros, middle + ends, zeros], 0).astype(BF)

    def body(r, _):
        up[r] = one(r, (-1, 0))
        down[r] = one(ROWS - 7 + r, (0, 1))
        return 0

    lax.fori_loop(0, 7, body, 0)

    def body_pre(r, _):
        up[7 + r] = buf[r].astype(BF)
        down[7 + r] = buf[ROWS - 8 + r].astype(BF)
        return 0

    lax.fori_loop(0, 8, body_pre, 0)


def ends(pre, pre_left, pre_right, base, base_left, base_right, kernel):
    strip = sds((RH, WIDE, CH), BF)
    return pl.pallas_call(
        ends_kernel,
        out_shape=[strip, strip],
        in_specs=[VMEM] * 7,
        out_specs=[VMEM] * 2,
        scratch_shapes=[pltpu.VMEM((ROWS, WIDE, CH), F32)],
        compiler_params=pltpu.CompilerParams(vmem_limit_bytes=24 * 2**20),
        cost_estimate=pl.CostEstimate(flops=10**8, bytes_accessed=6 * 2**20, transcendentals=0),
        name="ends",
    )(pre, pre_left, pre_right, base, base_left, base_right, kernel)


UHALO = 7
UWIDE = COLS + 16


def backward_kernel(last, *refs):
    refs = list(refs)
    take = lambda n: [refs.pop(0) for _ in range(n)]
    edges, pre, pre_left, pre_right, base, base_left, base_right, top, bottom = take(9)
    kernels, weights_t = take(2)
    count = 3 if last else 4
    if last:
        back = take(1)[0]
    slope_in = take(count)
    hid_in = take(count)
    if last:
        out, grads = take(2)
    else:
        up_out, pre_out, strip_left, strip_right, grads = take(5)
    buf, ups = take(2)
    slopes = take(count)
    hids = take(count)
    sem = take(1)[0]

    copies = []
    for k in range(count):
        copies.append(
            (
                pltpu.make_async_copy(slope_in[k], slopes[k], sem.at[2 * k]),
                pltpu.make_async_copy(hid_in[k], hids[k], sem.at[2 * k + 1]),
            )
        )
        copies[-1][0].start()
        copies[-1][1].start()

    def build(r, _):
        buf[BASE + r, 0:16] = pre_left[r].astype(F32)
        buf[BASE + r, 16:144] = pre[r].astype(F32)
        buf[BASE + r, 144:160] = pre_right[r].astype(F32)
        ups[UHALO + r, 0:8] = base_left[r].astype(F32)[8:16]
        ups[UHALO + r, 8:136] = base[r].astype(F32)
        ups[UHALO + r, 136:144] = base_right[r].astype(F32)[0:8]
        return 0

    lax.fori_loop(0, ROWS, build, 0)

    def build_pre(r, _):
        buf[r] = top[7 + r].astype(F32)
        buf[BASE + ROWS + r] = bottom[7 + r].astype(F32)
        return 0

    lax.fori_loop(0, 8, build_pre, 0)

    def build_ups(r, _):
        ups[r] = top[r].astype(F32)[8:152]
        ups[UHALO + ROWS + r] = bottom[r].astype(F32)[8:152]
        return 0

    lax.fori_loop(0, 7, build_ups, 0)

    def add_taps(r, low, high, dilate, taps, which, extra=None):
        for c, width in chunks(low, high, 32):
            start = ups[UHALO + r, c - 8 : c - 8 + width].reshape(width // 8, 8, CH)
            total = tap_sum(buf, BASE + r, c, width, dilate, -1, taps, which, start)
            if extra is not None:
                total = total + extra[(c - low) // 8 : (c - low + width) // 8][:, None, :]
                out[r, c - low : c - low + width] = total.reshape(width, CH).astype(BF)
            else:
                ups[UHALO + r, c - 8 : c - 8 + width] = total.reshape(width, CH)

    taps = rows_of(kernels[3], 1.0)

    def first_body(it, _):
        for q in range(2):
            add_taps(2 * it + q, 8, 152, 8, taps, (-1, 0, 1))
        return 0

    lax.fori_loop(0, ROWS // 2, first_body, 0)

    def first_ends(r, _):
        add_taps(r - 7, 8, 152, 8, taps, (-1,))
        add_taps(ROWS + r, 8, 152, 8, taps, (1,))
        return 0

    lax.fori_loop(0, 7, first_ends, 0)

    for k, layer in enumerate((2, 1, 0)):
        dilate = 2**layer
        halo = (1, 3, 7)[layer]
        copies[k][0].wait()
        copies[k][1].wait()
        step = (ROWS + 2 * halo) // 2
        skip = DHALO[layer] - halo

        def pull_body(it, _):
            at = it * step
            up = ups[pl.ds(UHALO - halo + at, step)].astype(BF)
            pulled = jnp.dot(
                up.reshape(step * UWIDE, CH), weights_t[layer], preferred_element_type=F32
            ).reshape(step, UWIDE, CH)
            slope = slopes[k][pl.ds(skip + at, step)].astype(F32)
            buf[pl.ds(BASE - halo + at, step), 8:152] = pulled * slope
            return 0

        lax.fori_loop(0, 2, pull_body, 0)
        clear_outside(buf, edges, 8, 8, 0, 16 + COLS)
        total = jnp.zeros((CH, CH), F32)
        for b in range(2):
            up = ups[UHALO + 16 * b : UHALO + 16 * b + 16, 8:136].astype(BF)
            total = total + grad_of(hids[k][16 * b : 16 * b + 16], up)
        grads[k] = total

        taps = rows_of(kernels[layer], 1.0)
        reach = (0, 1, 3)[layer]
        low, high = ((16, 144), (8, 152), (8, 152))[layer]

        def tap_body(it, _):
            for q in range(2):
                r = 2 * it + q - reach
                if last and layer == 0:
                    add_taps(r, low, high, dilate, taps, (-1, 0, 1), back[r // STRIDE])
                else:
                    add_taps(r, low, high, dilate, taps, (-1, 0, 1))
            return 0

        if layer == 1:
            lax.fori_loop(0, (ROWS + 2) // 2, tap_body, 0)
        else:
            lax.fori_loop(0, (ROWS + 2 * reach) // 2, tap_body, 0)

    if not last:
        copies[3][0].wait()
        copies[3][1].wait()
        total = jnp.zeros((CH, CH), F32)
        for b in range(2):
            rows = slice(16 * b, 16 * b + 16)
            value = ups[UHALO + 16 * b : UHALO + 16 * b + 16, 8:136]
            up_out[rows] = value
            up = value.astype(BF)
            total = total + grad_of(hids[3][rows], up)
            pulled = jnp.dot(up.reshape(-1, CH), weights_t[3], preferred_element_type=F32)
            value = (pulled.reshape(16, COLS, CH) * slopes[3][rows].astype(F32)).astype(BF)
            pre_out[rows] = value
            strip_left[rows, 0:16] = value[:, :CHALO]
            strip_left[rows, 16:32] = up[:, :CHALO]
            strip_right[rows, 0:16] = value[:, COLS - CHALO :]
            strip_right[rows, 16:32] = up[:, COLS - CHALO :]
        grads[3] = total


def backward(last, edges, pre, sides, base, base_sides, ends_in, kernels, weights_t, slopes, hids, back=()):
    count = len(slopes)
    block = sds((ROWS, COLS, CH), BF)
    if last:
        outs = [block, sds((count, CH, CH), F32)]
    else:
        strip = sds((ROWS, 2 * CHALO, CH), BF)
        outs = [sds((ROWS, COLS, CH), F32), block, strip, strip, sds((count, CH, CH), F32)]
    scratch = [
        pltpu.VMEM((ROWS + 16, WIDE, CH), F32),
        pltpu.VMEM((ROWS + 2 * UHALO, UWIDE, CH), F32),
    ]
    scratch += [pltpu.VMEM(a.shape, BF) for a in slopes]
    scratch += [pltpu.VMEM(a.shape, BF) for a in hids]
    scratch += [pltpu.SemaphoreType.DMA((2 * count,))]
    args = (edges, pre, *sides, base, *base_sides, *ends_in, kernels, weights_t, *back)
    return pl.pallas_call(
        functools.partial(backward_kernel, last),
        out_shape=outs,
        in_specs=[SMEM] + [VMEM] * (len(args) - 1) + [ANY] * (2 * count),
        out_specs=[VMEM] * len(outs),
        scratch_shapes=scratch,
        compiler_params=pltpu.CompilerParams(vmem_limit_bytes=52 * 2**20),
        cost_estimate=pl.CostEstimate(
            flops=7 * 2 * 5000 * CH * CH, bytes_accessed=14 * 2**20, transcendentals=0
        ),
        name="backward_last" if last else "backward_first",
    )(*args, *slopes, *hids)


def exchange(to_before, to_after, axis):
    ends_at = lax.axis_size(axis) - 1
    forth = [(i, i + 1) for i in range(ends_at)]
    back = [(i + 1, i) for i in range(ends_at)]
    return lax.ppermute(to_after, axis, forth), lax.ppermute(to_before, axis, back)


def row_strips(own, left, right):
    wide = lambda s: jnp.concatenate([left[s], own[s], right[s]], axis=1)
    return wide(slice(0, RH)), wide(slice(ROWS - RH, ROWS))


def local(features_in, cotangent, depth_kernels, point_weights, coarse_weight):
    row, col = lax.axis_index("rows"), lax.axis_index("cols")
    row_end, col_end = lax.axis_size("rows") - 1, lax.axis_size("cols") - 1
    edges = jnp.stack([row == 0, row == row_end, col == 0, col == col_end]).astype(jnp.int32)
    kernels = depth_kernels.astype(F32)
    weights_t = jnp.swapaxes(point_weights, 1, 2)

    side = lambda s: jnp.concatenate([features_in[:, s], cotangent[:, s]], axis=1)
    from_left, from_right = exchange(
        side(slice(0, CHALO)), side(slice(COLS - CHALO, COLS)), "cols"
    )
    left, right = from_left[:, :CHALO], from_right[:, :CHALO]
    cot_left, cot_right = from_left[:, CHALO:], from_right[:, CHALO:]
    top, bottom = exchange(*row_strips(features_in, left, right), "rows")
    coarse, back, coarse_grad = pool(features_in, cotangent, coarse_weight)
    x_mid, x_left, x_right, *kept = forward(
        False, edges, features_in, left, right, top, bottom, kernels[:4], point_weights[:4]
    )
    hid_low, slope_low = kept[:4], kept[4:]
    left, right = exchange(x_left, x_right, "cols")
    top, bottom = exchange(*row_strips(x_mid, left, right), "rows")
    output, pre, pre_left, pre_right, grad_top, *kept = forward(
        True, edges, x_mid, left, right, top, bottom, kernels[4:], point_weights[4:],
        (coarse, cotangent, weights_t[7]),
    )
    hid_high, slope_high = kept[:3], kept[3:]

    sides = exchange(pre_left, pre_right, "cols")
    base_sides = (cot_left, cot_right)
    rows_in = exchange(*ends(pre, *sides, cotangent, *base_sides, kernels[7]), "rows")
    order = lambda things: [things[2], things[1], things[0]]
    upstream, pre, strip_left, strip_right, grad_mid = backward(
        False, edges, pre, sides, cotangent, base_sides, rows_in,
        kernels[4:], jnp.concatenate([weights_t[4:7], weights_t[3:4]]),
        order(slope_high) + [slope_low[3]], order(hid_high) + [hid_low[3]],
    )
    got_left, got_right = exchange(strip_left, strip_right, "cols")
    sides = (got_left[:, :CHALO], got_right[:, :CHALO])
    base_sides = (got_left[:, CHALO:], got_right[:, CHALO:])
    rows_in = exchange(*ends(pre, *sides, upstream, *base_sides, kernels[3]), "rows")
    input_grad, grad_low = backward(
        True, edges, pre, sides, upstream, base_sides, rows_in,
        kernels[:4], weights_t[:3], order(slope_low), order(hid_low), (back,),
    )

    grads = [grad_low[2], grad_low[1], grad_low[0], grad_mid[3], grad_mid[2], grad_mid[1]]
    grads = jnp.stack(grads + [grad_mid[0], grad_top, coarse_grad], axis=1).astype(BF)
    shares = lax.all_to_all(grads, ("rows", "cols"), 0, 0, tiled=True)
    summed = shares.astype(F32).sum(axis=0)
    weight_grads = lax.all_gather(summed[:, None, :], "cols", axis=1, tiled=True)
    return (output, input_grad, weight_grads)


def solution(mesh):
    in_specs = (P("rows", "cols", None), P("rows", "cols", None), P(), P(), P())
    out_specs = (P("rows", "cols", None), P("rows", "cols", None), P(None, "rows", None))
    return jax.shard_map(local, mesh=mesh, in_specs=in_specs, out_specs=out_specs, check_vma=False)
```

```python
import functools

import jax
import jax.numpy as jnp
from jax import lax
from jax.experimental import pallas as pl
from jax.experimental.pallas import tpu as pltpu
from jax.sharding import PartitionSpec as P

STRIDE = 8
F32 = jnp.float32
BF = jnp.bfloat16
C0 = 0.7978845608028654
C1 = 0.7978845608028654 * 0.044715

ROWS, COLS, CH = 32, 128, 128
RH, CHALO = 15, 16
WIDE = COLS + 2 * CHALO
PAD = 8

HALO = (14, 12, 8, 0)
SPAN = ((0, 160), (0, 160), (8, 152), (16, 144))
DHALO = (2, 3, 8, 0)
DSPAN = ((8, 152), (8, 152), (8, 152), (16, 144))

VMEM = pl.BlockSpec(memory_space=pltpu.VMEM)
SMEM = pl.BlockSpec(memory_space=pltpu.SMEM)
ANY = pl.BlockSpec(memory_space=pl.ANY)


def sds(shape, dtype):
    return jax.ShapeDtypeStruct(shape, dtype)


def gelu_parts(half, want_slope):
    square = half * half
    t = jnp.tanh(half * (2 * C0 + 8 * C1 * square))
    half_t = half * t
    hidden = half + half_t
    if not want_slope:
        return hidden, None
    slope = (0.5 + 0.5 * t) + (half - half_t * t) * (C0 + 12 * C1 * square)
    return hidden, slope


def rows_of(kernel, scale):
    return [jnp.broadcast_to(kernel[t : t + 1, :] * scale, (8, CH))[None] for t in range(9)]


def tap_sum(src, row, col, width, dilate, sign, taps, which, start=None):
    total = start
    for i in which:
        for j in (-1, 0, 1):
            at = col + sign * j * dilate
            piece = src[row + sign * i * dilate, at : at + width, :].reshape(width // 8, 8, CH)
            piece = piece * taps[(i + 1) * 3 + j + 1]
            total = piece if total is None else total + piece
    return total


def chunks(low, high, size):
    out = []
    while low < high:
        out.append((low, min(size, high - low)))
        low += size
    return out


def clear_outside(ref, edges, rows_top, rows_bottom, col_left, col_right):
    count = ref.shape[0]
    breadth = ref.shape[1]

    if rows_top:

        @pl.when(edges[0] == 1)
        def _():
            ref[0:rows_top] = jnp.zeros((rows_top, breadth, CH), F32)

    if rows_bottom:

        @pl.when(edges[1] == 1)
        def _():
            ref[count - rows_bottom : count] = jnp.zeros((rows_bottom, breadth, CH), F32)

    @pl.when(edges[2] == 1)
    def _():
        ref[:, col_left : col_left + CHALO] = jnp.zeros((count, CHALO, CH), F32)

    @pl.when(edges[3] == 1)
    def _():
        ref[:, col_right : col_right + CHALO] = jnp.zeros((count, CHALO, CH), F32)


def grad_of(hidden, upstream):
    return lax.dot_general(
        hidden.reshape(-1, CH),
        upstream.reshape(-1, CH),
        (((0,), (0,)), ((), ())),
        preferred_element_type=F32,
    )


INNER = (0, 2, 6)
DSKIP = (4, 3, 0)


def act_rows(src, taps, layer, r, number, want_slope, h_buf, h_at, slope_buf, slope_at, hid_own, own_at):
    low, high = SPAN[layer]
    dlow, dhigh = DSPAN[layer]
    for q in range(number):
        hid_parts, slope_parts = [], []
        for c, width in chunks(low, high, 32):
            half = tap_sum(src, RH + r + q, PAD + c, width, 2**layer, 1, taps, (-1, 0, 1))
            hidden, slope = gelu_parts(half, want_slope)
            hid_parts.append(hidden.reshape(width, CH))
            if want_slope:
                slope_parts.append(slope.reshape(width, CH))
        hidden = jnp.concatenate(hid_parts, 0)
        h_buf[h_at + q] = hidden.astype(BF)
        if hid_own is not None:
            hid_own[own_at + q] = hidden[8:136].astype(BF)
        if want_slope:
            slope = jnp.concatenate(slope_parts, 0)
            slope_buf[slope_at + q] = slope[dlow - low : dhigh - low].astype(BF)


def mixed_rows(h_buf, h_at, src, r, step, layer, weights):
    low, high = SPAN[layer]
    mixed = jnp.dot(
        h_buf[pl.ds(h_at, step)].reshape(step * (high - low), CH),
        weights[layer],
        preferred_element_type=F32,
    ).reshape(step, high - low, CH)
    return src[pl.ds(RH + r, step), PAD + low : PAD + high] + mixed


def inner_kernel(*refs):
    refs = list(refs)
    take = lambda n: [refs.pop(0) for _ in range(n)]
    edges, own, left, right, kernels, weights = take(6)
    hid_out, slope_out, x_out = take(3), take(3), take(3)
    x_bufs, h_bufs, slopes = take(4), take(3), take(3)
    hid_two, sem = take(2)

    def build(r, _):
        x_bufs[0][RH + r, PAD : PAD + 16] = left[r].astype(F32)
        x_bufs[0][RH + r, PAD + 16 : PAD + 144] = own[r].astype(F32)
        x_bufs[0][RH + r, PAD + 144 : PAD + 160] = right[r].astype(F32)
        return 0

    lax.fori_loop(0, ROWS, build, 0)
    copies = []

    def send(src, dst, slot):
        copies.append(pltpu.make_async_copy(src, dst, sem.at[slot]))
        copies[-1].start()

    for layer in range(3):
        src, dst = x_bufs[layer], x_bufs[layer + 1]
        h_buf, slope_buf = h_bufs[layer], slopes[layer]
        low, high = SPAN[layer]
        edge = INNER[layer]
        first, number = edge + 1, ROWS - 2 - 2 * edge
        taps = rows_of(kernels[layer], 0.5)
        hid_own = hid_two if layer == 2 else None

        def body(it, _):
            act_rows(
                src, taps, layer, first + 2 * it, 2, True,
                h_buf, 2 * it, slope_buf, 2 * it, hid_own, 2 * it,
            )
            return 0

        lax.fori_loop(0, number // 2, body, 0)
        rows = pl.ds(first, number)
        hid_src = hid_two if layer == 2 else h_buf.at[:, pl.ds(16 - low, COLS)]
        send(hid_src, hid_out[layer].at[rows], layer)
        send(slope_buf, slope_out[layer].at[pl.ds(DHALO[layer] + first, number)], 3 + layer)

        step = (15, 13, 18)[layer]

        def mix_body(it, _):
            at = it * step
            dst[pl.ds(RH + first + at, step), PAD + low : PAD + high] = mixed_rows(
                h_buf, at, src, first + at, step, layer, weights
            )
            return 0

        lax.fori_loop(0, number // step, mix_body, 0)
        clear_outside(dst, edges, 0, 0, PAD, PAD + 16 + COLS)
        depth = (4, 8, 18)[layer]
        send(dst.at[pl.ds(RH + first, depth)], x_out[layer].at[pl.ds(0, depth)], 6 + layer)
        if layer < 2:
            send(
                dst.at[pl.ds(RH + first + number - depth, depth)],
                x_out[layer].at[pl.ds(depth, depth)],
                9 + layer,
            )
    for copy in copies:
        copy.wait()


XWIDE = WIDE + 2 * PAD
SLOPE_SHAPES = [(ROWS + 2 * DHALO[k], DSPAN[k][1] - DSPAN[k][0], CH) for k in range(4)]


def inner(edges, own, left, right, kernels, weights):
    outs = [sds((ROWS, COLS, CH), BF)] * 3
    outs += [sds(s, BF) for s in SLOPE_SHAPES[:3]]
    outs += [sds((n, XWIDE, CH), F32) for n in (8, 16, 18)]
    numbers = [ROWS - 2 - 2 * e for e in INNER]
    scratch = [pltpu.VMEM((ROWS + 2 * RH, XWIDE, CH), F32)] * 4
    scratch += [pltpu.VMEM((numbers[k], SPAN[k][1] - SPAN[k][0], CH), BF) for k in range(3)]
    scratch += [pltpu.VMEM((numbers[k], SLOPE_SHAPES[k][1], CH), BF) for k in range(3)]
    scratch += [pltpu.VMEM((numbers[2], COLS, CH), BF), pltpu.SemaphoreType.DMA((11,))]
    return pl.pallas_call(
        inner_kernel,
        out_shape=outs,
        in_specs=[SMEM] + [VMEM] * 5,
        out_specs=[ANY] * 9,
        scratch_shapes=scratch,
        compiler_params=pltpu.CompilerParams(vmem_limit_bytes=52 * 2**20),
        cost_estimate=pl.CostEstimate(
            flops=4 * 2 * 3000 * CH * CH, bytes_accessed=12 * 2**20, transcendentals=0
        ),
        name="forward_inner",
    )(edges, own, left, right, kernels, weights)


def outer_kernel(last, *refs):
    refs = list(refs)
    take = lambda n: [refs.pop(0) for _ in range(n)]
    edges, own, left, right, top, bottom, kernels, weights = take(8)
    if last:
        coarse, cot, back_weight = take(3)
    x_in = take(3)
    take(6)
    if last:
        out, pre, pre_left, pre_right, grad = take(5)
    else:
        x_out, x_left, x_right, hid_three, slope_three = take(5)
    hid_out, slope_out = take(3), take(3)
    x_bufs, h_bufs, slopes = take(4), take(4), take(4)
    hid_two, own_buf, sem = take(3)

    loads = []
    for layer in range(3):
        first = INNER[layer] + 1
        depth = (4, 8, 18)[layer]
        spots = [(first, 0)] if layer == 2 else [(first, 0), (ROWS - first - depth, depth)]
        for k, (r, at) in enumerate(spots):
            copy = pltpu.make_async_copy(
                x_in[layer].at[pl.ds(at, depth)],
                x_bufs[layer + 1].at[pl.ds(RH + r, depth)],
                sem.at[20 + 2 * layer + k],
            )
            copy.start()
            loads.append((layer, copy))

    for r in (0, 1, ROWS - 2, ROWS - 1):
        x_bufs[0][RH + r, PAD : PAD + 16] = left[r].astype(F32)
        x_bufs[0][RH + r, PAD + 16 : PAD + 144] = own[r].astype(F32)
        x_bufs[0][RH + r, PAD + 144 : PAD + 160] = right[r].astype(F32)

    def build_ends(r, _):
        x_bufs[0][r, PAD : PAD + WIDE] = top[r].astype(F32)
        x_bufs[0][RH + ROWS + r, PAD : PAD + WIDE] = bottom[r].astype(F32)
        return 0

    lax.fori_loop(0, RH, build_ends, 0)
    copies = []

    def send(src, dst, slot):
        copies.append(pltpu.make_async_copy(src, dst, sem.at[slot]))
        copies[-1].start()

    for layer in range(3):
        src, dst = x_bufs[layer], x_bufs[layer + 1]
        h_buf, slope_buf = h_bufs[layer], slopes[layer]
        halo, edge, dhalo = HALO[layer], INNER[layer], DHALO[layer]
        low, high = SPAN[layer]
        taps = rows_of(kernels[layer], 0.5)
        hid_own = hid_two if layer == 2 else None
        skip = DSKIP[layer]
        kept = 5 - skip

        if skip:

            def far_body(it, _):
                low_side = it >= skip
                at = jnp.where(low_side, 15 + 3 * kept + 3 * (it - skip), 3 * it)
                r = jnp.where(low_side, ROWS - 1 - edge - 15, -halo) + at
                act_rows(src, taps, layer, r, 3, False, h_buf, at, None, 0, None, 0)
                return 0

            lax.fori_loop(0, 2 * skip, far_body, 0)

        def near_body(it, _):
            low_side = it >= kept
            at = jnp.where(low_side, 15 + 3 * (it - kept), 3 * skip + 3 * it)
            r = jnp.where(low_side, ROWS - 1 - edge - 15, -halo) + at
            act_rows(src, taps, layer, r, 3, True, h_buf, at, slope_buf, 3 * it, hid_own, at)
            return 0

        lax.fori_loop(0, 2 * kept, near_body, 0)

        whole = hid_two if layer == 2 else h_buf
        cols = pl.ds(0, COLS) if layer == 2 else pl.ds(16 - low, COLS)
        send(whole.at[pl.ds(halo, edge + 1), cols], hid_out[layer].at[pl.ds(0, edge + 1)], layer)
        send(
            whole.at[pl.ds(15, edge + 1), cols],
            hid_out[layer].at[pl.ds(ROWS - 1 - edge, edge + 1)],
            3 + layer,
        )
        number = 3 * kept
        send(slope_buf.at[pl.ds(0, number)], slope_out[layer].at[pl.ds(0, number)], 6 + layer)
        send(
            slope_buf.at[pl.ds(number, number)],
            slope_out[layer].at[pl.ds(dhalo + ROWS - 1 - edge, number)],
            9 + layer,
        )
        for which, copy in loads:
            if which == layer:
                copy.wait()

        def mix_body(it, _):
            r = jnp.where(it == 0, -halo, ROWS - 1 - edge)
            dst[pl.ds(RH + r, 15), PAD + low : PAD + high] = mixed_rows(
                h_buf, 15 * it, src, r, 15, layer, weights
            )
            return 0

        lax.fori_loop(0, 2, mix_body, 0)
        clear_outside(dst, edges, RH, RH, PAD, PAD + 16 + COLS)

    taps = rows_of(kernels[3], 0.5)

    def last_body(it, _):
        act_rows(
            x_bufs[3], taps, 3, 4 * it, 4, True, h_bufs[3], 4 * it, slopes[3], 4 * it, None, 0
        )
        return 0

    lax.fori_loop(0, ROWS // 4, last_body, 0)
    if not last:
        send(h_bufs[3], hid_three, 12)
        send(slopes[3], slope_three, 13)

    def last_mix(it, _):
        at = 16 * it
        value = mixed_rows(h_bufs[3], at, x_bufs[3], at, 16, 3, weights)
        if last:
            for q in range(2):
                extra = coarse[2 * it + q][:, None, :]
                part = value[q * STRIDE : (q + 1) * STRIDE].reshape(STRIDE, -1, STRIDE, CH)
                part = (part + extra[None]).reshape(STRIDE, COLS, CH)
                own_buf[pl.ds(at + q * STRIDE, STRIDE)] = part.astype(BF)
        else:
            value = value.astype(BF)
            own_buf[pl.ds(at, 16)] = value
            x_left[pl.ds(at, 16)] = value[:, :CHALO]
            x_right[pl.ds(at, 16)] = value[:, COLS - CHALO :]
        return 0

    lax.fori_loop(0, 2, last_mix, 0)
    send(own_buf, out if last else x_out, 14)
    if last:
        total = jnp.zeros((CH, CH), F32)
        for b in range(2):
            rows = slice(16 * b, 16 * b + 16)
            up = cot[rows]
            total = total + grad_of(h_bufs[3][rows], up)
            pulled = jnp.dot(up.reshape(-1, CH), back_weight[...], preferred_element_type=F32)
            value = pulled.reshape(16, COLS, CH) * slopes[3][rows].astype(F32)
            value = value.astype(BF)
            pre[rows] = value
            pre_left[rows] = value[:, :CHALO]
            pre_right[rows] = value[:, COLS - CHALO :]
        grad[...] = total
    for copy in copies:
        copy.wait()


def outer(last, edges, own, left, right, top, bottom, kernels, weights, begun, extra=()):
    block = sds((ROWS, COLS, CH), BF)
    strip = sds((ROWS, CHALO, CH), BF)
    if last:
        outs = [block, block, strip, strip, sds((CH, CH), F32)]
        specs = [ANY] + [VMEM] * 4
    else:
        outs = [block, strip, strip, block, block]
        specs = [ANY, VMEM, VMEM, ANY, ANY]
    outs = outs + [sds(a.shape, BF) for a in begun[:6]]
    specs = specs + [ANY] * 6
    args = (edges, own, left, right, top, bottom, kernels, weights, *extra, *begun[6:], *begun[:6])
    scratch = [pltpu.VMEM((ROWS + 2 * RH, XWIDE, CH), F32)] * 4
    heights = [30, 30, 30, ROWS]
    scratch += [pltpu.VMEM((heights[k], SPAN[k][1] - SPAN[k][0], CH), BF) for k in range(4)]
    tall = [6 * (5 - DSKIP[k]) for k in range(3)] + [ROWS]
    scratch += [pltpu.VMEM((tall[k], SLOPE_SHAPES[k][1], CH), BF) for k in range(4)]
    scratch += [pltpu.VMEM((30, COLS, CH), BF), pltpu.VMEM((ROWS, COLS, CH), BF)]
    scratch += [pltpu.SemaphoreType.DMA((26,))]
    return pl.pallas_call(
        functools.partial(outer_kernel, last),
        out_shape=outs,
        in_specs=[SMEM] + [VMEM] * (7 + len(extra)) + [ANY] * 9,
        out_specs=specs,
        scratch_shapes=scratch,
        input_output_aliases={len(args) - 6 + k: 5 + k for k in range(6)},
        compiler_params=pltpu.CompilerParams(vmem_limit_bytes=52 * 2**20),
        cost_estimate=pl.CostEstimate(
            flops=4 * 2 * 5000 * CH * CH, bytes_accessed=12 * 2**20, transcendentals=0
        ),
        name="forward_last" if last else "forward_first",
    )(*args)


def pool_kernel(feature, cot, weight, weight_t, coarse, back, grad):
    total = None
    for b in range(ROWS // STRIDE):
        rows = slice(STRIDE * b, STRIDE * (b + 1))

        def block_sum(ref):
            value = ref[STRIDE * b].astype(F32)
            for r in range(1, STRIDE):
                value = value + ref[STRIDE * b + r].astype(F32)
            return value.reshape(COLS // STRIDE, STRIDE, CH).sum(axis=1)

        pooled = (block_sum(feature) * (1.0 / (STRIDE * STRIDE))).astype(BF)
        block_cot = block_sum(cot).astype(BF)
        coarse[b] = jnp.dot(pooled, weight[...], preferred_element_type=F32)
        back[b] = jnp.dot(block_cot, weight_t[...], preferred_element_type=F32) * (
            1.0 / (STRIDE * STRIDE)
        )
        part = grad_of(pooled, block_cot)
        total = part if total is None else total + part
    grad[...] = total


def pool(feature, cot, weight):
    small = sds((ROWS // STRIDE, COLS // STRIDE, CH), F32)
    return pl.pallas_call(
        pool_kernel,
        out_shape=[small, small, sds((CH, CH), F32)],
        in_specs=[VMEM] * 4,
        out_specs=[VMEM] * 3,
        compiler_params=pltpu.CompilerParams(vmem_limit_bytes=16 * 2**20),
        cost_estimate=pl.CostEstimate(flops=10**8, bytes_accessed=2 * 2**20, transcendentals=0),
        name="pool",
    )(feature, cot, weight, weight.T)


BASE = 8


def ends_kernel(pre, pre_left, pre_right, base, base_left, base_right, kernel, up, down, buf):
    taps = rows_of(kernel, 1.0)

    def build(r, _):
        buf[r, 0:16] = pre_left[r].astype(F32)
        buf[r, 16:144] = pre[r].astype(F32)
        buf[r, 144:160] = pre_right[r].astype(F32)
        return 0

    lax.fori_loop(0, ROWS, build, 0)
    zeros = jnp.zeros((8, CH), F32)

    def one(r, which):
        parts = []
        for c, width in chunks(8, 152, 32):
            parts.append(tap_sum(buf, r, c, width, 8, -1, taps, which).reshape(width, CH))
        middle = jnp.concatenate(parts, 0)
        ends = jnp.concatenate(
            [
                base_left[r].astype(F32)[8:16],
                base[r].astype(F32),
                base_right[r].astype(F32)[0:8],
            ],
            0,
        )
        return jnp.concatenate([zeros, middle + ends, zeros], 0).astype(BF)

    def body(r, _):
        up[r] = one(r, (-1, 0))
        down[r] = one(ROWS - 7 + r, (0, 1))
        return 0

    lax.fori_loop(0, 7, body, 0)

    def body_pre(r, _):
        up[7 + r] = buf[r].astype(BF)
        down[7 + r] = buf[ROWS - 8 + r].astype(BF)
        return 0

    lax.fori_loop(0, 8, body_pre, 0)


def ends(pre, pre_left, pre_right, base, base_left, base_right, kernel):
    strip = sds((RH, WIDE, CH), BF)
    return pl.pallas_call(
        ends_kernel,
        out_shape=[strip, strip],
        in_specs=[VMEM] * 7,
        out_specs=[VMEM] * 2,
        scratch_shapes=[pltpu.VMEM((ROWS, WIDE, CH), F32)],
        compiler_params=pltpu.CompilerParams(vmem_limit_bytes=24 * 2**20),
        cost_estimate=pl.CostEstimate(flops=10**8, bytes_accessed=6 * 2**20, transcendentals=0),
        name="ends",
    )(pre, pre_left, pre_right, base, base_left, base_right, kernel)


UHALO = 7
UWIDE = COLS + 16


def backward_kernel(last, *refs):
    refs = list(refs)
    take = lambda n: [refs.pop(0) for _ in range(n)]
    edges, pre, pre_left, pre_right, base, base_left, base_right, top, bottom = take(9)
    kernels, weights_t = take(2)
    count = 3 if last else 4
    if last:
        back = take(1)[0]
    slope_in = take(count)
    hid_in = take(count)
    if last:
        out, grads = take(2)
    else:
        up_out, pre_out, strip_left, strip_right, grads = take(5)
    buf, ups = take(2)
    slopes = take(count)
    hids = take(count)
    sem = take(1)[0]

    copies = []
    for k in range(count):
        copies.append(
            (
                pltpu.make_async_copy(slope_in[k], slopes[k], sem.at[2 * k]),
                pltpu.make_async_copy(hid_in[k], hids[k], sem.at[2 * k + 1]),
            )
        )
        copies[-1][0].start()
        copies[-1][1].start()

    def build(r, _):
        buf[BASE + r, 0:16] = pre_left[r].astype(F32)
        buf[BASE + r, 16:144] = pre[r].astype(F32)
        buf[BASE + r, 144:160] = pre_right[r].astype(F32)
        ups[UHALO + r, 0:8] = base_left[r].astype(F32)[8:16]
        ups[UHALO + r, 8:136] = base[r].astype(F32)
        ups[UHALO + r, 136:144] = base_right[r].astype(F32)[0:8]
        return 0

    lax.fori_loop(0, ROWS, build, 0)

    def build_pre(r, _):
        buf[r] = top[7 + r].astype(F32)
        buf[BASE + ROWS + r] = bottom[7 + r].astype(F32)
        return 0

    lax.fori_loop(0, 8, build_pre, 0)

    def build_ups(r, _):
        ups[r] = top[r].astype(F32)[8:152]
        ups[UHALO + ROWS + r] = bottom[r].astype(F32)[8:152]
        return 0

    lax.fori_loop(0, 7, build_ups, 0)

    def add_taps(r, low, high, dilate, taps, which, extra=None):
        for c, width in chunks(low, high, 32):
            start = ups[UHALO + r, c - 8 : c - 8 + width].reshape(width // 8, 8, CH)
            total = tap_sum(buf, BASE + r, c, width, dilate, -1, taps, which, start)
            if extra is not None:
                total = total + extra[(c - low) // 8 : (c - low + width) // 8][:, None, :]
                out[r, c - low : c - low + width] = total.reshape(width, CH).astype(BF)
            else:
                ups[UHALO + r, c - 8 : c - 8 + width] = total.reshape(width, CH)

    taps = rows_of(kernels[3], 1.0)

    def first_body(it, _):
        for q in range(2):
            add_taps(2 * it + q, 8, 152, 8, taps, (-1, 0, 1))
        return 0

    lax.fori_loop(0, ROWS // 2, first_body, 0)

    def first_ends(r, _):
        add_taps(r - 7, 8, 152, 8, taps, (-1,))
        add_taps(ROWS + r, 8, 152, 8, taps, (1,))
        return 0

    lax.fori_loop(0, 7, first_ends, 0)

    for k, layer in enumerate((2, 1, 0)):
        dilate = 2**layer
        halo = (1, 3, 7)[layer]
        copies[k][0].wait()
        copies[k][1].wait()
        step = (ROWS + 2 * halo) // 2
        skip = DHALO[layer] - halo

        def pull_body(it, _):
            at = it * step
            up = ups[pl.ds(UHALO - halo + at, step)].astype(BF)
            pulled = jnp.dot(
                up.reshape(step * UWIDE, CH), weights_t[layer], preferred_element_type=F32
            ).reshape(step, UWIDE, CH)
            slope = slopes[k][pl.ds(skip + at, step)].astype(F32)
            buf[pl.ds(BASE - halo + at, step), 8:152] = pulled * slope
            return 0

        lax.fori_loop(0, 2, pull_body, 0)
        clear_outside(buf, edges, 8, 8, 0, 16 + COLS)
        total = jnp.zeros((CH, CH), F32)
        for b in range(2):
            up = ups[UHALO + 16 * b : UHALO + 16 * b + 16, 8:136].astype(BF)
            total = total + grad_of(hids[k][16 * b : 16 * b + 16], up)
        grads[k] = total

        taps = rows_of(kernels[layer], 1.0)
        reach = (0, 1, 3)[layer]
        low, high = ((16, 144), (8, 152), (8, 152))[layer]

        def tap_body(it, _):
            for q in range(2):
                r = 2 * it + q - reach
                if last and layer == 0:
                    add_taps(r, low, high, dilate, taps, (-1, 0, 1), back[r // STRIDE])
                else:
                    add_taps(r, low, high, dilate, taps, (-1, 0, 1))
            return 0

        if layer == 1:
            lax.fori_loop(0, (ROWS + 2) // 2, tap_body, 0)
        else:
            lax.fori_loop(0, (ROWS + 2 * reach) // 2, tap_body, 0)

    if not last:
        copies[3][0].wait()
        copies[3][1].wait()
        total = jnp.zeros((CH, CH), F32)
        for b in range(2):
            rows = slice(16 * b, 16 * b + 16)
            value = ups[UHALO + 16 * b : UHALO + 16 * b + 16, 8:136]
            up_out[rows] = value
            up = value.astype(BF)
            total = total + grad_of(hids[3][rows], up)
            pulled = jnp.dot(up.reshape(-1, CH), weights_t[3], preferred_element_type=F32)
            value = (pulled.reshape(16, COLS, CH) * slopes[3][rows].astype(F32)).astype(BF)
            pre_out[rows] = value
            strip_left[rows, 0:16] = value[:, :CHALO]
            strip_left[rows, 16:32] = up[:, :CHALO]
            strip_right[rows, 0:16] = value[:, COLS - CHALO :]
            strip_right[rows, 16:32] = up[:, COLS - CHALO :]
        grads[3] = total


def backward(last, edges, pre, sides, base, base_sides, ends_in, kernels, weights_t, slopes, hids, back=()):
    count = len(slopes)
    block = sds((ROWS, COLS, CH), BF)
    if last:
        outs = [block, sds((count, CH, CH), F32)]
    else:
        strip = sds((ROWS, 2 * CHALO, CH), BF)
        outs = [sds((ROWS, COLS, CH), F32), block, strip, strip, sds((count, CH, CH), F32)]
    scratch = [
        pltpu.VMEM((ROWS + 16, WIDE, CH), F32),
        pltpu.VMEM((ROWS + 2 * UHALO, UWIDE, CH), F32),
    ]
    scratch += [pltpu.VMEM(a.shape, BF) for a in slopes]
    scratch += [pltpu.VMEM(a.shape, BF) for a in hids]
    scratch += [pltpu.SemaphoreType.DMA((2 * count,))]
    args = (edges, pre, *sides, base, *base_sides, *ends_in, kernels, weights_t, *back)
    return pl.pallas_call(
        functools.partial(backward_kernel, last),
        out_shape=outs,
        in_specs=[SMEM] + [VMEM] * (len(args) - 1) + [ANY] * (2 * count),
        out_specs=[VMEM] * len(outs),
        scratch_shapes=scratch,
        compiler_params=pltpu.CompilerParams(vmem_limit_bytes=52 * 2**20),
        cost_estimate=pl.CostEstimate(
            flops=7 * 2 * 5000 * CH * CH, bytes_accessed=14 * 2**20, transcendentals=0
        ),
        name="backward_last" if last else "backward_first",
    )(*args, *slopes, *hids)


def exchange(to_before, to_after, axis):
    ends_at = lax.axis_size(axis) - 1
    forth = [(i, i + 1) for i in range(ends_at)]
    back = [(i + 1, i) for i in range(ends_at)]
    return lax.ppermute(to_after, axis, forth), lax.ppermute(to_before, axis, back)


def row_strips(own, left, right):
    wide = lambda s: jnp.concatenate([left[s], own[s], right[s]], axis=1)
    return wide(slice(0, RH)), wide(slice(ROWS - RH, ROWS))


def local(features_in, cotangent, depth_kernels, point_weights, coarse_weight):
    row, col = lax.axis_index("rows"), lax.axis_index("cols")
    row_end, col_end = lax.axis_size("rows") - 1, lax.axis_size("cols") - 1
    edges = jnp.stack([row == 0, row == row_end, col == 0, col == col_end]).astype(jnp.int32)
    kernels = depth_kernels.astype(F32)
    weights_t = jnp.swapaxes(point_weights, 1, 2)

    side = lambda s: jnp.concatenate([features_in[:, s], cotangent[:, s]], axis=1)
    from_left, from_right = exchange(
        side(slice(0, CHALO)), side(slice(COLS - CHALO, COLS)), "cols"
    )
    left, right = from_left[:, :CHALO], from_right[:, :CHALO]
    cot_left, cot_right = from_left[:, CHALO:], from_right[:, CHALO:]
    top, bottom = exchange(*row_strips(features_in, left, right), "rows")
    coarse, back, coarse_grad = pool(features_in, cotangent, coarse_weight)
    begun = inner(edges, features_in, left, right, kernels[:3], point_weights[:3])
    x_mid, x_left, x_right, hid_three, slope_three, *kept = outer(
        False, edges, features_in, left, right, top, bottom, kernels[:4], point_weights[:4], begun
    )
    hid_low, slope_low = kept[:3] + [hid_three], kept[3:] + [slope_three]
    left, right = exchange(x_left, x_right, "cols")
    top, bottom = exchange(*row_strips(x_mid, left, right), "rows")
    begun = inner(edges, x_mid, left, right, kernels[4:7], point_weights[4:7])
    output, pre, pre_left, pre_right, grad_top, *kept = outer(
        True, edges, x_mid, left, right, top, bottom, kernels[4:], point_weights[4:], begun,
        (coarse, cotangent, weights_t[7]),
    )
    hid_high, slope_high = kept[:3], kept[3:]

    sides = exchange(pre_left, pre_right, "cols")
    base_sides = (cot_left, cot_right)
    rows_in = exchange(*ends(pre, *sides, cotangent, *base_sides, kernels[7]), "rows")
    order = lambda things: [things[2], things[1], things[0]]
    upstream, pre, strip_left, strip_right, grad_mid = backward(
        False, edges, pre, sides, cotangent, base_sides, rows_in,
        kernels[4:], jnp.concatenate([weights_t[4:7], weights_t[3:4]]),
        order(slope_high) + [slope_low[3]], order(hid_high) + [hid_low[3]],
    )
    got_left, got_right = exchange(strip_left, strip_right, "cols")
    sides = (got_left[:, :CHALO], got_right[:, :CHALO])
    base_sides = (got_left[:, CHALO:], got_right[:, CHALO:])
    rows_in = exchange(*ends(pre, *sides, upstream, *base_sides, kernels[3]), "rows")
    input_grad, grad_low = backward(
        True, edges, pre, sides, upstream, base_sides, rows_in,
        kernels[:4], weights_t[:3], order(slope_low), order(hid_low), (back,),
    )

    grads = [grad_low[2], grad_low[1], grad_low[0], grad_mid[3], grad_mid[2], grad_mid[1]]
    grads = jnp.stack(grads + [grad_mid[0], grad_top, coarse_grad]).astype(BF)
    shares = lax.all_to_all(grads, "rows", 1, 0, tiled=True)
    summed = shares.reshape(-1, grads.shape[0], CH * 4).astype(F32).sum(axis=0)
    parts = lax.all_gather(summed, "cols", axis=0, tiled=False)
    weight_grads = parts.sum(axis=0).reshape(grads.shape[0], 4, CH)
    return (output, input_grad, weight_grads)


def solution(mesh):
    in_specs = (P("rows", "cols", None), P("rows", "cols", None), P(), P(), P())
    out_specs = (P("rows", "cols", None), P("rows", "cols", None), P(None, "rows", None))
    return jax.shard_map(local, mesh=mesh, in_specs=in_specs, out_specs=out_specs, check_vma=False)
```

```python
import functools

import jax
import jax.numpy as jnp
from jax import lax
from jax.experimental import pallas as pl
from jax.experimental.pallas import tpu as pltpu
from jax.sharding import PartitionSpec as P

STRIDE = 8
F32 = jnp.float32
BF = jnp.bfloat16
C0 = 0.7978845608028654
C1 = 0.7978845608028654 * 0.044715

ROWS, COLS, CH = 32, 128, 128
RH, CHALO = 15, 16
WIDE = COLS + 2 * CHALO
PAD = 8

HALO = (14, 12, 8, 0)
SIDES = (32, 16)
SPANS = (
    ((0, 192), (0, 192), (8, 184), (16, 176)),
    ((0, 160), (0, 160), (8, 152), (16, 144)),
)
DHALO = (2, 3, 8, 0)
DSIDE = (16, 16, 8, 0)

VMEM = pl.BlockSpec(memory_space=pltpu.VMEM)
SMEM = pl.BlockSpec(memory_space=pltpu.SMEM)
ANY = pl.BlockSpec(memory_space=pl.ANY)


def sds(shape, dtype):
    return jax.ShapeDtypeStruct(shape, dtype)


def gelu_parts(half, want_slope):
    square = half * half
    t = jnp.tanh(half * (BF(2 * C0) + BF(8 * C1) * square))
    half_t = half * t
    hidden = half + half_t
    if not want_slope:
        return hidden, None
    slope = (BF(0.5) + BF(0.5) * t) + (half - half_t * t) * (BF(C0) + BF(12 * C1) * square)
    return hidden, slope


def rows_of(kernel, scale):
    return [jnp.broadcast_to(kernel[t : t + 1, :] * scale, (8, CH))[None] for t in range(9)]


def tap_sum(src, row, col, width, dilate, sign, taps, which, start=None):
    total = start
    for i in which:
        for j in (-1, 0, 1):
            at = col + sign * j * dilate
            piece = src[row + sign * i * dilate, at : at + width, :].reshape(width // 8, 8, CH)
            piece = piece * taps[(i + 1) * 3 + j + 1]
            total = piece if total is None else total + piece
    return total


def chunks(low, high, size):
    out = []
    while low < high:
        out.append((low, min(size, high - low)))
        low += size
    return out


def grad_of(hidden, upstream):
    return lax.dot_general(
        hidden.reshape(-1, CH),
        upstream.reshape(-1, CH),
        (((0,), (0,)), ((), ())),
        preferred_element_type=F32,
    )


INNER = (0, 2, 6)
DSKIP = (4, 3, 0)


def act_rows(src, taps, seg, layer, r, number, want_slope, h_buf, h_at, slope_buf, slope_at, hid_own):
    low, high = SPANS[seg][layer]
    first = SIDES[seg] - DSIDE[layer] - low
    for q in range(number):
        parts = []
        for c, width in chunks(low, high, 32):
            half = tap_sum(src, RH + r + q, PAD + c, width, 2**layer, 1, taps, (-1, 0, 1))
            parts.append(gelu_parts(half.reshape(width, CH).astype(BF), want_slope))
        hidden = jnp.concatenate([p[0] for p in parts], 0)
        h_buf[h_at + q] = hidden
        if hid_own is not None:
            own = hidden.astype(F32)[SIDES[seg] - low : SIDES[seg] - low + COLS]
            hid_own[h_at + q] = own.astype(BF)
        if want_slope:
            slope = jnp.concatenate([p[1] for p in parts], 0)
            slope_buf[slope_at + q] = slope[first : first + COLS + 2 * DSIDE[layer]]


def mixed_rows(h_buf, h_at, src, r, step, seg, layer, weights):
    low, high = SPANS[seg][layer]
    mixed = jnp.dot(
        h_buf[pl.ds(h_at, step)].reshape(step * (high - low), CH),
        weights[layer],
        preferred_element_type=F32,
    ).reshape(step, high - low, CH)
    return src[pl.ds(RH + r, step), PAD + low : PAD + high] + mixed


def fill_row(buf, row, at, pieces, r):
    for piece in pieces:
        width = piece.shape[1]
        buf[row, at : at + width] = piece[r].astype(F32)
        at += width


def clear_columns(ref, edges, seg):
    side = SIDES[seg]
    count = ref.shape[0]

    @pl.when(edges[2] == 1)
    def _():
        ref[:, PAD : PAD + side] = jnp.zeros((count, side, CH), F32)

    @pl.when(edges[3] == 1)
    def _():
        ref[:, PAD + side + COLS : PAD + 2 * side + COLS] = jnp.zeros((count, side, CH), F32)


def clear_rows(ref, edges, number):
    count, breadth = ref.shape[0], ref.shape[1]

    @pl.when(edges[0] == 1)
    def _():
        ref[0:number] = jnp.zeros((number, breadth, CH), F32)

    @pl.when(edges[1] == 1)
    def _():
        ref[count - number : count] = jnp.zeros((number, breadth, CH), F32)


def inner_kernel(seg, *refs):
    refs = list(refs)
    take = lambda n: [refs.pop(0) for _ in range(n)]
    edges = take(1)[0]
    pieces = take(1 if seg else 3)
    kernels, weights = take(2)
    hid_out, slope_out, x_out = take(3), take(3), take(3)
    x_bufs, h_bufs, slopes = take(4), take(3), take(3)
    hid_two, sem = take(2)

    def build(r, _):
        fill_row(x_bufs[0], RH + r, PAD, pieces, r)
        return 0

    lax.fori_loop(0, ROWS, build, 0)
    copies = []

    def send(src, dst, slot):
        copies.append(pltpu.make_async_copy(src, dst, sem.at[slot]))
        copies[-1].start()

    for layer in range(3):
        src, dst = x_bufs[layer], x_bufs[layer + 1]
        h_buf, slope_buf = h_bufs[layer], slopes[layer]
        low, high = SPANS[seg][layer]
        edge = INNER[layer]
        first, number = edge + 1, ROWS - 2 - 2 * edge
        taps = rows_of(kernels[layer], 0.5)
        hid_own = hid_two if layer == 2 else None

        def body(it, _):
            act_rows(
                src, taps, seg, layer, first + 2 * it, 2, True,
                h_buf, 2 * it, slope_buf, 2 * it, hid_own,
            )
            return 0

        lax.fori_loop(0, number // 2, body, 0)
        rows = pl.ds(first, number)
        hid_src = hid_two if layer == 2 else h_buf.at[:, pl.ds(SIDES[seg] - low, COLS)]
        send(hid_src, hid_out[layer].at[rows], layer)
        send(slope_buf, slope_out[layer].at[pl.ds(DHALO[layer] + first, number)], 3 + layer)

        step = (15, 13, 9)[layer]

        def mix_body(it, _):
            at = it * step
            dst[pl.ds(RH + first + at, step), PAD + low : PAD + high] = mixed_rows(
                h_buf, at, src, first + at, step, seg, layer, weights
            )
            return 0

        lax.fori_loop(0, number // step, mix_body, 0)
        clear_columns(dst, edges, seg)
        depth = (4, 8, 18)[layer]
        send(dst.at[pl.ds(RH + first, depth)], x_out[layer].at[pl.ds(0, depth)], 6 + layer)
        if layer < 2:
            send(
                dst.at[pl.ds(RH + first + number - depth, depth)],
                x_out[layer].at[pl.ds(depth, depth)],
                9 + layer,
            )
    for copy in copies:
        copy.wait()


SLOPE_SHAPES = [(ROWS + 2 * DHALO[k], COLS + 2 * DSIDE[k], CH) for k in range(4)]


def x_wide(seg):
    return COLS + 2 * SIDES[seg] + 2 * PAD


def inner(seg, edges, pieces, kernels, weights):
    outs = [sds((ROWS, COLS, CH), BF)] * 3
    outs += [sds(s, BF) for s in SLOPE_SHAPES[:3]]
    outs += [sds((n, x_wide(seg), CH), F32) for n in (8, 16, 18)]
    numbers = [ROWS - 2 - 2 * e for e in INNER]
    breadth = [b - a for a, b in SPANS[seg]]
    scratch = [pltpu.VMEM((ROWS + 2 * RH, x_wide(seg), CH), F32)] * 4
    scratch += [pltpu.VMEM((numbers[k], breadth[k], CH), BF) for k in range(3)]
    scratch += [pltpu.VMEM((numbers[k], SLOPE_SHAPES[k][1], CH), BF) for k in range(3)]
    scratch += [pltpu.VMEM((numbers[2], COLS, CH), BF), pltpu.SemaphoreType.DMA((11,))]
    return pl.pallas_call(
        functools.partial(inner_kernel, seg),
        out_shape=outs,
        in_specs=[SMEM] + [VMEM] * (2 + len(pieces)),
        out_specs=[ANY] * 9,
        scratch_shapes=scratch,
        compiler_params=pltpu.CompilerParams(vmem_limit_bytes=52 * 2**20),
        cost_estimate=pl.CostEstimate(
            flops=4 * 2 * 3000 * CH * CH, bytes_accessed=12 * 2**20, transcendentals=0
        ),
        name="inner_last" if seg else "inner_first",
    )(edges, *pieces, kernels, weights)


def outer_kernel(seg, *refs):
    refs = list(refs)
    take = lambda n: [refs.pop(0) for _ in range(n)]
    edges = take(1)[0]
    pieces = take(1 if seg else 3)
    top, bottom, kernels, weights = take(4)
    if seg:
        coarse, cot, back_weight = take(3)
    x_in = take(3)
    take(6)
    if seg:
        out, pre, strip_left, strip_right, grad = take(5)
    else:
        x_out, hid_three, slope_three = take(3)
    hid_out, slope_out = take(3), take(3)
    x_bufs, h_bufs, slopes = take(4), take(4), take(4)
    hid_two, own_buf, sem = take(3)
    side = SIDES[seg]

    loads = []
    for layer in range(3):
        first = INNER[layer] + 1
        depth = (4, 8, 18)[layer]
        spots = [(first, 0)] if layer == 2 else [(first, 0), (ROWS - first - depth, depth)]
        for k, (r, at) in enumerate(spots):
            copy = pltpu.make_async_copy(
                x_in[layer].at[pl.ds(at, depth)],
                x_bufs[layer + 1].at[pl.ds(RH + r, depth)],
                sem.at[20 + 2 * layer + k],
            )
            copy.start()
            loads.append((layer, copy))

    for r in (0, 1, ROWS - 2, ROWS - 1):
        fill_row(x_bufs[0], RH + r, PAD, pieces, r)

    def build_ends(r, _):
        fill_row(x_bufs[0], r, PAD, [top], r)
        fill_row(x_bufs[0], RH + ROWS + r, PAD, [bottom], r)
        return 0

    lax.fori_loop(0, RH, build_ends, 0)
    copies = []

    def send(src, dst, slot):
        copies.append(pltpu.make_async_copy(src, dst, sem.at[slot]))
        copies[-1].start()

    for layer in range(3):
        src, dst = x_bufs[layer], x_bufs[layer + 1]
        h_buf, slope_buf = h_bufs[layer], slopes[layer]
        halo, edge, dhalo = HALO[layer], INNER[layer], DHALO[layer]
        low, high = SPANS[seg][layer]
        taps = rows_of(kernels[layer], 0.5)
        hid_own = hid_two if layer == 2 else None
        skip = DSKIP[layer]
        kept = 5 - skip

        if skip:

            def far_body(it, _):
                low_side = it >= skip
                at = jnp.where(low_side, 15 + 3 * kept + 3 * (it - skip), 3 * it)
                r = jnp.where(low_side, ROWS - 1 - edge - 15, -halo) + at
                act_rows(src, taps, seg, layer, r, 3, False, h_buf, at, None, 0, None)
                return 0

            lax.fori_loop(0, 2 * skip, far_body, 0)

        def near_body(it, _):
            low_side = it >= kept
            at = jnp.where(low_side, 15 + 3 * (it - kept), 3 * skip + 3 * it)
            r = jnp.where(low_side, ROWS - 1 - edge - 15, -halo) + at
            act_rows(src, taps, seg, layer, r, 3, True, h_buf, at, slope_buf, 3 * it, hid_own)
            return 0

        lax.fori_loop(0, 2 * kept, near_body, 0)

        whole = hid_two if layer == 2 else h_buf
        cols = pl.ds(0, COLS) if layer == 2 else pl.ds(side - low, COLS)
        send(whole.at[pl.ds(halo, edge + 1), cols], hid_out[layer].at[pl.ds(0, edge + 1)], layer)
        send(
            whole.at[pl.ds(15, edge + 1), cols],
            hid_out[layer].at[pl.ds(ROWS - 1 - edge, edge + 1)],
            3 + layer,
        )
        number = 3 * kept
        send(slope_buf.at[pl.ds(0, number)], slope_out[layer].at[pl.ds(0, number)], 6 + layer)
        send(
            slope_buf.at[pl.ds(number, number)],
            slope_out[layer].at[pl.ds(dhalo + ROWS - 1 - edge, number)],
            9 + layer,
        )
        for which, copy in loads:
            if which == layer:
                copy.wait()

        def mix_body(it, _):
            r = jnp.where(it == 0, -halo, ROWS - 1 - edge)
            dst[pl.ds(RH + r, 15), PAD + low : PAD + high] = mixed_rows(
                h_buf, 15 * it, src, r, 15, seg, layer, weights
            )
            return 0

        lax.fori_loop(0, 2, mix_body, 0)
        clear_rows(dst, edges, RH)
        clear_columns(dst, edges, seg)

    taps = rows_of(kernels[3], 0.5)

    def last_body(it, _):
        act_rows(
            x_bufs[3], taps, seg, 3, 4 * it, 4, True, h_bufs[3], 4 * it, slopes[3], 4 * it, None
        )
        return 0

    lax.fori_loop(0, ROWS // 4, last_body, 0)
    if not seg:
        send(h_bufs[3].at[:, pl.ds(CHALO, COLS)], hid_three, 12)
        send(slopes[3], slope_three, 13)

    def last_mix(it, _):
        at = 16 * it
        value = mixed_rows(h_bufs[3], at, x_bufs[3], at, 16, seg, 3, weights)
        if seg:
            for q in range(2):
                extra = coarse[2 * it + q][:, None, :]
                part = value[q * STRIDE : (q + 1) * STRIDE].reshape(STRIDE, -1, STRIDE, CH)
                part = (part + extra[None]).reshape(STRIDE, COLS, CH)
                own_buf[pl.ds(at + q * STRIDE, STRIDE)] = part.astype(BF)
        else:
            own_buf[pl.ds(at, 16)] = value.astype(BF)
        return 0

    lax.fori_loop(0, 2, last_mix, 0)
    if seg:
        send(own_buf, out, 14)
        total = jnp.zeros((CH, CH), F32)
        edge_cols = []
        for b in range(2):
            rows = slice(16 * b, 16 * b + 16)
            up = cot[rows]
            total = total + grad_of(h_bufs[3][rows], up)
            pulled = jnp.dot(up.reshape(-1, CH), back_weight[...], preferred_element_type=F32)
            value = pulled.reshape(16, COLS, CH) * slopes[3][rows].astype(F32)
            value = value.astype(BF)
            pre[rows] = value
            strip_left[rows] = value[:, :CHALO]
            strip_right[rows] = value[:, COLS - CHALO :]
            edge_cols.append(up.astype(F32))
        pack_edges(strip_left, strip_right, edge_cols)
        grad[...] = total
    else:
        zeros = jnp.zeros((ROWS, CHALO, CH), BF)

        @pl.when(edges[2] == 1)
        def _():
            own_buf[:, 0:CHALO] = zeros

        @pl.when(edges[3] == 1)
        def _():
            own_buf[:, CHALO + COLS : WIDE] = zeros

        send(own_buf, x_out, 14)
    for copy in copies:
        copy.wait()


def pack_edges(strip_left, strip_right, halves):
    first, second = halves
    strip_left[ROWS : ROWS + 16] = jnp.concatenate([first[:, :8], second[:, :8]], 1).astype(BF)
    strip_right[ROWS : ROWS + 16] = jnp.concatenate(
        [first[:, COLS - 8 :], second[:, COLS - 8 :]], 1
    ).astype(BF)


def outer(seg, edges, pieces, top, bottom, kernels, weights, begun, extra=()):
    block = sds((ROWS, COLS, CH), BF)
    strip = sds((ROWS + 16, CHALO, CH), BF)
    if seg:
        outs = [block, block, strip, strip, sds((CH, CH), F32)]
        specs = [ANY] + [VMEM] * 4
    else:
        outs = [sds((ROWS, WIDE, CH), BF), block, block]
        specs = [ANY, ANY, ANY]
    shift = len(outs)
    outs = outs + [sds(a.shape, BF) for a in begun[:6]]
    specs = specs + [ANY] * 6
    args = (edges, *pieces, top, bottom, kernels, weights, *extra, *begun[6:], *begun[:6])
    breadth = [b - a for a, b in SPANS[seg]]
    scratch = [pltpu.VMEM((ROWS + 2 * RH, x_wide(seg), CH), F32)] * 4
    heights = [30, 30, 30, ROWS]
    scratch += [pltpu.VMEM((heights[k], breadth[k], CH), BF) for k in range(4)]
    tall = [6 * (5 - DSKIP[k]) for k in range(3)] + [ROWS]
    scratch += [pltpu.VMEM((tall[k], SLOPE_SHAPES[k][1], CH), BF) for k in range(4)]
    scratch += [pltpu.VMEM((30, COLS, CH), BF), pltpu.VMEM((ROWS, breadth[3], CH), BF)]
    scratch += [pltpu.SemaphoreType.DMA((26,))]
    return pl.pallas_call(
        functools.partial(outer_kernel, seg),
        out_shape=outs,
        in_specs=[SMEM] + [VMEM] * (len(args) - 10) + [ANY] * 9,
        out_specs=specs,
        scratch_shapes=scratch,
        input_output_aliases={len(args) - 6 + k: shift + k for k in range(6)},
        compiler_params=pltpu.CompilerParams(vmem_limit_bytes=52 * 2**20),
        cost_estimate=pl.CostEstimate(
            flops=4 * 2 * 5000 * CH * CH, bytes_accessed=12 * 2**20, transcendentals=0
        ),
        name="outer_last" if seg else "outer_first",
    )(*args)


def pool_kernel(feature, cot, weight, weight_t, coarse, back, grad):
    total = None
    for b in range(ROWS // STRIDE):
        rows = slice(STRIDE * b, STRIDE * (b + 1))

        def block_sum(ref):
            value = ref[STRIDE * b].astype(F32)
            for r in range(1, STRIDE):
                value = value + ref[STRIDE * b + r].astype(F32)
            return value.reshape(COLS // STRIDE, STRIDE, CH).sum(axis=1)

        pooled = (block_sum(feature) * (1.0 / (STRIDE * STRIDE))).astype(BF)
        block_cot = block_sum(cot).astype(BF)
        coarse[b] = jnp.dot(pooled, weight[...], preferred_element_type=F32)
        back[b] = jnp.dot(block_cot, weight_t[...], preferred_element_type=F32) * (
            1.0 / (STRIDE * STRIDE)
        )
        part = grad_of(pooled, block_cot)
        total = part if total is None else total + part
    grad[...] = total


def pool(feature, cot, weight):
    small = sds((ROWS // STRIDE, COLS // STRIDE, CH), F32)
    return pl.pallas_call(
        pool_kernel,
        out_shape=[small, small, sds((CH, CH), F32)],
        in_specs=[VMEM] * 4,
        out_specs=[VMEM] * 3,
        compiler_params=pltpu.CompilerParams(vmem_limit_bytes=16 * 2**20),
        cost_estimate=pl.CostEstimate(flops=10**8, bytes_accessed=2 * 2**20, transcendentals=0),
        name="pool",
    )(feature, cot, weight, weight.T)


BASE = 8


def fill_pre(buf, row, pre, from_left, from_right, r):
    buf[row, 0:16] = from_left[r].astype(F32)
    buf[row, 16:144] = pre[r].astype(F32)
    buf[row, 144:160] = from_right[r].astype(F32)


def base_row(base, from_left, from_right, r, half):
    side = slice(8 * half, 8 * half + 8)
    return jnp.concatenate(
        [
            from_left[ROWS + r].astype(F32)[side],
            base[r + 16 * half].astype(F32),
            from_right[ROWS + r].astype(F32)[side],
        ],
        0,
    )


def row_taps(buf, r, taps, which, low=8, high=152):
    parts = []
    for c, width in chunks(low, high, 32):
        parts.append(tap_sum(buf, r, c, width, 8, -1, taps, which).reshape(width, CH))
    return jnp.concatenate(parts, 0)


def ends_kernel(pre, from_left, from_right, base, kernel, up, down, buf):
    taps = rows_of(kernel, 1.0)

    def build(r, _):
        fill_pre(buf, r, pre, from_left, from_right, r)
        fill_pre(buf, 16 + r, pre, from_left, from_right, 16 + r)
        return 0

    lax.fori_loop(0, 16, build, 0)
    zeros = jnp.zeros((8, CH), F32)

    def one(r, half, which):
        value = row_taps(buf, r + 16 * half, taps, which)
        value = value + base_row(base, from_left, from_right, r, half)
        return jnp.concatenate([zeros, value, zeros], 0).astype(BF)

    def body(r, _):
        up[r] = one(r, 0, (-1, 0))
        down[r] = one(ROWS - 23 + r, 1, (0, 1))
        return 0

    lax.fori_loop(0, 7, body, 0)

    def body_pre(r, _):
        up[7 + r] = buf[r].astype(BF)
        down[7 + r] = buf[ROWS - 8 + r].astype(BF)
        return 0

    lax.fori_loop(0, 8, body_pre, 0)


def ends(pre, from_left, from_right, base, kernel):
    strip = sds((RH, WIDE, CH), BF)
    return pl.pallas_call(
        ends_kernel,
        out_shape=[strip, strip],
        in_specs=[VMEM] * 5,
        out_specs=[VMEM] * 2,
        scratch_shapes=[pltpu.VMEM((ROWS, WIDE, CH), F32)],
        compiler_params=pltpu.CompilerParams(vmem_limit_bytes=20 * 2**20),
        cost_estimate=pl.CostEstimate(flops=10**8, bytes_accessed=6 * 2**20, transcendentals=0),
        name="ends",
    )(pre, from_left, from_right, base, kernel)


def own_kernel(pre, from_left, from_right, base, kernel, out, buf):
    taps = rows_of(kernel, 1.0)

    def build(r, _):
        fill_pre(buf, r, pre, from_left, from_right, r)
        fill_pre(buf, 16 + r, pre, from_left, from_right, 16 + r)
        return 0

    lax.fori_loop(0, 16, build, 0)

    def one(r, half, which):
        value = row_taps(buf, r + 16 * half, taps, which)
        out[r + 16 * half] = value + base_row(base, from_left, from_right, r, half)

    def body_edge(r, _):
        one(r, 0, (-1, 0))
        one(r + 8, 1, (0, 1))
        return 0

    def body_middle(r, _):
        one(r + 8, 0, (-1, 0, 1))
        one(r, 1, (-1, 0, 1))
        return 0

    lax.fori_loop(0, 8, body_edge, 0)
    lax.fori_loop(0, 8, body_middle, 0)


def own_part(pre, from_left, from_right, base, kernel):
    return pl.pallas_call(
        own_kernel,
        out_shape=sds((ROWS, UWIDE, CH), F32),
        in_specs=[VMEM] * 5,
        out_specs=VMEM,
        scratch_shapes=[pltpu.VMEM((ROWS, WIDE, CH), F32)],
        compiler_params=pltpu.CompilerParams(vmem_limit_bytes=20 * 2**20),
        cost_estimate=pl.CostEstimate(
            flops=2 * 10**9, bytes_accessed=6 * 2**20, transcendentals=0
        ),
        name="own_part",
    )(pre, from_left, from_right, base, kernel)


UHALO = 7
UWIDE = COLS + 16


def backward_kernel(last, *refs):
    refs = list(refs)
    take = lambda n: [refs.pop(0) for _ in range(n)]
    edges, pre, from_left, from_right, top, bottom = take(6)
    kernels, weights_t = take(2)
    count = 3 if last else 4
    if last:
        back = take(1)[0]
    part_in = take(1)[0]
    slope_in = take(count)
    hid_in = take(count)
    if last:
        out, grads = take(2)
    else:
        up_out, pre_out, strip_left, strip_right, grads = take(5)
    buf, ups = take(2)
    slopes = take(count)
    hids = take(count)
    sem = take(1)[0]

    copies = []
    for k in range(count):
        copies.append(
            (
                pltpu.make_async_copy(slope_in[k], slopes[k], sem.at[2 * k]),
                pltpu.make_async_copy(hid_in[k], hids[k], sem.at[2 * k + 1]),
            )
        )
        copies[-1][0].start()
        copies[-1][1].start()

    part_copy = pltpu.make_async_copy(
        part_in, ups.at[pl.ds(UHALO, ROWS)], sem.at[2 * count]
    )
    part_copy.start()

    def build(r, _):
        fill_pre(buf, BASE + r, pre, from_left, from_right, r)
        fill_pre(buf, BASE + 24 + r, pre, from_left, from_right, 24 + r)
        return 0

    lax.fori_loop(0, 8, build, 0)

    def build_pre(r, _):
        buf[r] = top[7 + r].astype(F32)
        buf[BASE + ROWS + r] = bottom[7 + r].astype(F32)
        return 0

    lax.fori_loop(0, 8, build_pre, 0)

    def build_ups(r, _):
        ups[r] = top[r].astype(F32)[8:152]
        ups[UHALO + ROWS + r] = bottom[r].astype(F32)[8:152]
        return 0

    lax.fori_loop(0, 7, build_ups, 0)

    def add_taps(r, low, high, dilate, taps, which, extra=None):
        for c, width in chunks(low, high, 32):
            start = ups[UHALO + r, c - 8 : c - 8 + width].reshape(width // 8, 8, CH)
            total = tap_sum(buf, BASE + r, c, width, dilate, -1, taps, which, start)
            if extra is not None:
                total = total + extra[(c - low) // 8 : (c - low + width) // 8][:, None, :]
                out[r, c - low : c - low + width] = total.reshape(width, CH).astype(BF)
            else:
                ups[UHALO + r, c - 8 : c - 8 + width] = total.reshape(width, CH)

    taps = rows_of(kernels[3], 1.0)

    part_copy.wait()

    def first_upper(r, _):
        add_taps(r, 8, 152, 8, taps, (1,))
        add_taps(24 + r, 8, 152, 8, taps, (-1,))
        return 0

    lax.fori_loop(0, 8, first_upper, 0)

    def first_ends(r, _):
        add_taps(r - 7, 8, 152, 8, taps, (-1,))
        add_taps(ROWS + r, 8, 152, 8, taps, (1,))
        return 0

    lax.fori_loop(0, 7, first_ends, 0)

    for k, layer in enumerate((2, 1, 0)):
        dilate = 2**layer
        halo = (1, 3, 7)[layer]
        copies[k][0].wait()
        copies[k][1].wait()
        step = (ROWS + 2 * halo) // 2
        skip = DHALO[layer] - halo

        def pull_body(it, _):
            at = it * step
            up = ups[pl.ds(UHALO - halo + at, step)].astype(BF)
            pulled = jnp.dot(
                up.reshape(step * UWIDE, CH), weights_t[layer], preferred_element_type=F32
            ).reshape(step, UWIDE, CH)
            slope = slopes[k][pl.ds(skip + at, step)].astype(F32)
            slope = slope[:, DSIDE[layer] - 8 : DSIDE[layer] - 8 + UWIDE]
            buf[pl.ds(BASE - halo + at, step), 8:152] = pulled * slope
            return 0

        lax.fori_loop(0, 2, pull_body, 0)
        clear_rows(buf, edges, 8)
        zeros = jnp.zeros((ROWS + 16, CHALO, CH), F32)

        @pl.when(edges[2] == 1)
        def _():
            buf[:, 0:CHALO] = zeros

        @pl.when(edges[3] == 1)
        def _():
            buf[:, CHALO + COLS : WIDE] = zeros

        total = jnp.zeros((CH, CH), F32)
        for b in range(2):
            up = ups[UHALO + 16 * b : UHALO + 16 * b + 16, 8:136].astype(BF)
            total = total + grad_of(hids[k][16 * b : 16 * b + 16], up)
        grads[k] = total

        taps = rows_of(kernels[layer], 1.0)
        reach = (0, 1, 3)[layer]
        low, high = ((16, 144), (8, 152), (8, 152))[layer]

        def tap_body(it, _):
            for q in range(2):
                r = 2 * it + q - reach
                if last and layer == 0:
                    add_taps(r, low, high, dilate, taps, (-1, 0, 1), back[r // STRIDE])
                else:
                    add_taps(r, low, high, dilate, taps, (-1, 0, 1))
            return 0

        if layer == 1:
            lax.fori_loop(0, (ROWS + 2) // 2, tap_body, 0)
        else:
            lax.fori_loop(0, (ROWS + 2 * reach) // 2, tap_body, 0)

    if not last:
        copies[3][0].wait()
        copies[3][1].wait()
        total = jnp.zeros((CH, CH), F32)
        edge_cols = []
        for b in range(2):
            rows = slice(16 * b, 16 * b + 16)
            value = ups[UHALO + 16 * b : UHALO + 16 * b + 16, 8:136]
            up_out[rows] = value
            up = value.astype(BF)
            total = total + grad_of(hids[3][rows], up)
            pulled = jnp.dot(up.reshape(-1, CH), weights_t[3], preferred_element_type=F32)
            value = (pulled.reshape(16, COLS, CH) * slopes[3][rows].astype(F32)).astype(BF)
            pre_out[rows] = value
            strip_left[rows] = value[:, :CHALO]
            strip_right[rows] = value[:, COLS - CHALO :]
            edge_cols.append(ups[UHALO + 16 * b : UHALO + 16 * b + 16, 8:136])
        pack_edges(strip_left, strip_right, edge_cols)
        grads[3] = total


def backward(last, edges, pre, sides, part, ends_in, kernels, weights_t, slopes, hids, back=()):
    count = len(slopes)
    block = sds((ROWS, COLS, CH), BF)
    if last:
        outs = [block, sds((count, CH, CH), F32)]
    else:
        strip = sds((ROWS + 16, CHALO, CH), BF)
        outs = [sds((ROWS, COLS, CH), F32), block, strip, strip, sds((count, CH, CH), F32)]
    scratch = [
        pltpu.VMEM((ROWS + 16, WIDE, CH), F32),
        pltpu.VMEM((ROWS + 2 * UHALO, UWIDE, CH), F32),
    ]
    scratch += [pltpu.VMEM(a.shape, BF) for a in slopes]
    scratch += [pltpu.VMEM(a.shape, BF) for a in hids]
    scratch += [pltpu.SemaphoreType.DMA((2 * count + 1,))]
    args = (edges, pre, *sides, *ends_in, kernels, weights_t, *back)
    return pl.pallas_call(
        functools.partial(backward_kernel, last),
        out_shape=outs,
        in_specs=[SMEM] + [VMEM] * (len(args) - 1) + [ANY] * (1 + 2 * count),
        out_specs=[VMEM] * len(outs),
        scratch_shapes=scratch,
        compiler_params=pltpu.CompilerParams(vmem_limit_bytes=30 * 2**20),
        cost_estimate=pl.CostEstimate(
            flops=7 * 2 * 5000 * CH * CH, bytes_accessed=14 * 2**20, transcendentals=0
        ),
        name="backward_last" if last else "backward_first",
    )(*args, part, *slopes, *hids)


def exchange(to_before, to_after, axis):
    ends_at = lax.axis_size(axis) - 1
    forth = [(i, i + 1) for i in range(ends_at)]
    back = [(i + 1, i) for i in range(ends_at)]
    return lax.ppermute(to_after, axis, forth), lax.ppermute(to_before, axis, back)


def local(features_in, cotangent, depth_kernels, point_weights, coarse_weight):
    row, col = lax.axis_index("rows"), lax.axis_index("cols")
    row_end, col_end = lax.axis_size("rows") - 1, lax.axis_size("cols") - 1
    edges = jnp.stack([row == 0, row == row_end, col == 0, col == col_end]).astype(jnp.int32)
    kernels = depth_kernels.astype(F32)
    weights_t = jnp.swapaxes(point_weights, 1, 2)

    left, right = exchange(
        features_in[:, : SIDES[0]], features_in[:, COLS - SIDES[0] :], "cols"
    )
    wide = lambda rows: jnp.concatenate([left[rows], features_in[rows], right[rows]], axis=1)
    top, bottom = exchange(wide(slice(0, RH)), wide(slice(ROWS - RH, ROWS)), "rows")
    coarse, back, coarse_grad = pool(features_in, cotangent, coarse_weight)
    pieces = (left, features_in, right)
    begun = inner(0, edges, pieces, kernels[:3], point_weights[:3])
    x_mid, hid_three, slope_three, *kept = outer(
        0, edges, pieces, top, bottom, kernels[:4], point_weights[:4], begun
    )
    hid_low, slope_low = kept[:3] + [hid_three], kept[3:] + [slope_three]
    top, bottom = exchange(x_mid[:RH], x_mid[ROWS - RH :], "rows")
    begun = inner(1, edges, (x_mid,), kernels[4:7], point_weights[4:7])
    output, pre, strip_left, strip_right, grad_top, *kept = outer(
        1, edges, (x_mid,), top, bottom, kernels[4:], point_weights[4:], begun,
        (coarse, cotangent, weights_t[7]),
    )
    hid_high, slope_high = kept[:3], kept[3:]

    order = lambda things: [things[2], things[1], things[0]]
    sides = exchange(strip_left, strip_right, "cols")
    rows_in = exchange(*ends(pre, *sides, cotangent, kernels[7]), "rows")
    part = own_part(pre, *sides, cotangent, kernels[7])
    upstream, pre, strip_left, strip_right, grad_mid = backward(
        False, edges, pre, sides, part, rows_in,
        kernels[4:], jnp.concatenate([weights_t[4:7], weights_t[3:4]]),
        order(slope_high) + [slope_low[3]], order(hid_high) + [hid_low[3]],
    )
    sides = exchange(strip_left, strip_right, "cols")
    rows_in = exchange(*ends(pre, *sides, upstream, kernels[3]), "rows")
    part = own_part(pre, *sides, upstream, kernels[3])
    input_grad, grad_low = backward(
        True, edges, pre, sides, part, rows_in,
        kernels[:4], weights_t[:3], order(slope_low), order(hid_low), (back,),
    )

    grads = [grad_low[2], grad_low[1], grad_low[0], grad_mid[3], grad_mid[2], grad_mid[1]]
    grads = jnp.stack(grads + [grad_mid[0], grad_top, coarse_grad]).astype(BF)
    shares = lax.all_to_all(grads, "rows", 1, 0, tiled=True)
    summed = shares.reshape(-1, grads.shape[0], CH * 4).astype(F32).sum(axis=0)
    parts = lax.all_gather(summed.astype(BF), "cols", axis=0, tiled=False)
    weight_grads = parts.astype(F32).sum(axis=0).reshape(grads.shape[0], 4, CH)
    return (output, input_grad, weight_grads)


def solution(mesh):
    in_specs = (P("rows", "cols", None), P("rows", "cols", None), P(), P(), P())
    out_specs = (P("rows", "cols", None), P("rows", "cols", None), P(None, "rows", None))
    return jax.shard_map(local, mesh=mesh, in_specs=in_specs, out_specs=out_specs, check_vma=False)
```

```python
import functools

import jax
import jax.numpy as jnp
from jax import lax
from jax.experimental import pallas as pl
from jax.experimental.pallas import tpu as pltpu
from jax.sharding import PartitionSpec as P

STRIDE = 8
F32 = jnp.float32
BF = jnp.bfloat16
C0 = 0.7978845608028654
C1 = 0.7978845608028654 * 0.044715

ROWS, COLS, CH = 32, 128, 128
RH, CHALO = 15, 16
WIDE = COLS + 2 * CHALO
PAD = 8

HALO = (14, 12, 8, 0)
SIDES = (32, 16)
SPANS = (
    ((0, 192), (0, 192), (8, 184), (16, 176)),
    ((0, 160), (0, 160), (8, 152), (16, 144)),
)
DHALO = (2, 3, 8, 0)
DSIDE = (16, 16, 8, 0)

VMEM = pl.BlockSpec(memory_space=pltpu.VMEM)
SMEM = pl.BlockSpec(memory_space=pltpu.SMEM)
ANY = pl.BlockSpec(memory_space=pl.ANY)


def sds(shape, dtype):
    return jax.ShapeDtypeStruct(shape, dtype)


def gelu_parts(half, want_slope):
    square = half * half
    t = jnp.tanh(half * (BF(2 * C0) + BF(8 * C1) * square))
    half_t = half * t
    hidden = half + half_t
    if not want_slope:
        return hidden, None
    slope = (BF(0.5) + BF(0.5) * t) + (half - half_t * t) * (BF(C0) + BF(12 * C1) * square)
    return hidden, slope


def rows_of(kernel, scale):
    return [jnp.broadcast_to(kernel[t : t + 1, :] * scale, (8, CH))[None] for t in range(9)]


def tap_sum(src, row, col, width, dilate, sign, taps, which, start=None):
    total = start
    for i in which:
        for j in (-1, 0, 1):
            at = col + sign * j * dilate
            piece = src[row + sign * i * dilate, at : at + width, :].reshape(width // 8, 8, CH)
            piece = piece * taps[(i + 1) * 3 + j + 1]
            total = piece if total is None else total + piece
    return total


def chunks(low, high, size):
    out = []
    while low < high:
        out.append((low, min(size, high - low)))
        low += size
    return out


def pull_back(upstream, weight):
    return lax.dot_general(
        upstream.reshape(-1, CH), weight, (((1,), (1,)), ((), ())), preferred_element_type=F32
    )


def grad_of(hidden, upstream):
    return lax.dot_general(
        hidden.reshape(-1, CH),
        upstream.reshape(-1, CH),
        (((0,), (0,)), ((), ())),
        preferred_element_type=F32,
    )


INNER = (0, 2, 6)
DSKIP = (4, 3, 0)


def act_rows(src, taps, seg, layer, r, number, want_slope, h_buf, h_at, slope_buf, slope_at, hid_own):
    low, high = SPANS[seg][layer]
    first = SIDES[seg] - DSIDE[layer] - low
    for q in range(number):
        parts = []
        for c, width in chunks(low, high, 32):
            half = tap_sum(src, RH + r + q, PAD + c, width, 2**layer, 1, taps, (-1, 0, 1))
            parts.append(gelu_parts(half.reshape(width, CH).astype(BF), want_slope))
        hidden = jnp.concatenate([p[0] for p in parts], 0)
        h_buf[h_at + q] = hidden
        if hid_own is not None:
            own = hidden.astype(F32)[SIDES[seg] - low : SIDES[seg] - low + COLS]
            hid_own[h_at + q] = own.astype(BF)
        if want_slope:
            slope = jnp.concatenate([p[1] for p in parts], 0)
            slope_buf[slope_at + q] = slope[first : first + COLS + 2 * DSIDE[layer]]


def mixed_rows(h_buf, h_at, src, r, step, seg, layer, weights):
    low, high = SPANS[seg][layer]
    mixed = jnp.dot(
        h_buf[pl.ds(h_at, step)].reshape(step * (high - low), CH),
        weights[layer],
        preferred_element_type=F32,
    ).reshape(step, high - low, CH)
    return src[pl.ds(RH + r, step), PAD + low : PAD + high] + mixed


def fill_row(buf, row, at, pieces, r):
    for piece in pieces:
        width = piece.shape[1]
        buf[row, at : at + width] = piece[r].astype(F32)
        at += width


def clear_columns(ref, edges, seg):
    side = SIDES[seg]
    count = ref.shape[0]

    @pl.when(edges[2] == 1)
    def _():
        ref[:, PAD : PAD + side] = jnp.zeros((count, side, CH), F32)

    @pl.when(edges[3] == 1)
    def _():
        ref[:, PAD + side + COLS : PAD + 2 * side + COLS] = jnp.zeros((count, side, CH), F32)


def clear_rows(ref, edges, number):
    count, breadth = ref.shape[0], ref.shape[1]

    @pl.when(edges[0] == 1)
    def _():
        ref[0:number] = jnp.zeros((number, breadth, CH), F32)

    @pl.when(edges[1] == 1)
    def _():
        ref[count - number : count] = jnp.zeros((number, breadth, CH), F32)


def inner_kernel(seg, *refs):
    refs = list(refs)
    take = lambda n: [refs.pop(0) for _ in range(n)]
    edges = take(1)[0]
    pieces = take(1 if seg else 3)
    kernels, weights = take(2)
    hid_out, slope_out, x_out = take(3), take(3), take(3)
    x_bufs, h_bufs, slopes = take(4), take(3), take(3)
    hid_two, sem = take(2)

    def build(r, _):
        fill_row(x_bufs[0], RH + r, PAD, pieces, r)
        return 0

    lax.fori_loop(0, ROWS, build, 0)
    copies = []

    def send(src, dst, slot):
        copies.append(pltpu.make_async_copy(src, dst, sem.at[slot]))
        copies[-1].start()

    for layer in range(3):
        src, dst = x_bufs[layer], x_bufs[layer + 1]
        h_buf, slope_buf = h_bufs[layer], slopes[layer]
        low, high = SPANS[seg][layer]
        edge = INNER[layer]
        first, number = edge + 1, ROWS - 2 - 2 * edge
        taps = rows_of(kernels[layer], 0.5)
        hid_own = hid_two if layer == 2 else None

        def body(it, _):
            act_rows(
                src, taps, seg, layer, first + 2 * it, 2, True,
                h_buf, 2 * it, slope_buf, 2 * it, hid_own,
            )
            return 0

        lax.fori_loop(0, number // 2, body, 0)
        rows = pl.ds(first, number)
        hid_src = hid_two if layer == 2 else h_buf.at[:, pl.ds(SIDES[seg] - low, COLS)]
        send(hid_src, hid_out[layer].at[rows], layer)
        send(slope_buf, slope_out[layer].at[pl.ds(DHALO[layer] + first, number)], 3 + layer)

        step = (15, 13, 9)[layer]

        def mix_body(it, _):
            at = it * step
            dst[pl.ds(RH + first + at, step), PAD + low : PAD + high] = mixed_rows(
                h_buf, at, src, first + at, step, seg, layer, weights
            )
            return 0

        lax.fori_loop(0, number // step, mix_body, 0)
        clear_columns(dst, edges, seg)
        depth = (4, 8, 18)[layer]
        send(dst.at[pl.ds(RH + first, depth)], x_out[layer].at[pl.ds(0, depth)], 6 + layer)
        if layer < 2:
            send(
                dst.at[pl.ds(RH + first + number - depth, depth)],
                x_out[layer].at[pl.ds(depth, depth)],
                9 + layer,
            )
    for copy in copies:
        copy.wait()


SLOPE_SHAPES = [(ROWS + 2 * DHALO[k], COLS + 2 * DSIDE[k], CH) for k in range(4)]


def x_wide(seg):
    return COLS + 2 * SIDES[seg] + 2 * PAD


def inner(seg, edges, pieces, kernels, weights):
    outs = [sds((ROWS, COLS, CH), BF)] * 3
    outs += [sds(s, BF) for s in SLOPE_SHAPES[:3]]
    outs += [sds((n, x_wide(seg), CH), F32) for n in (8, 16, 18)]
    numbers = [ROWS - 2 - 2 * e for e in INNER]
    breadth = [b - a for a, b in SPANS[seg]]
    scratch = [pltpu.VMEM((ROWS + 2 * RH, x_wide(seg), CH), F32)] * 4
    scratch += [pltpu.VMEM((numbers[k], breadth[k], CH), BF) for k in range(3)]
    scratch += [pltpu.VMEM((numbers[k], SLOPE_SHAPES[k][1], CH), BF) for k in range(3)]
    scratch += [pltpu.VMEM((numbers[2], COLS, CH), BF), pltpu.SemaphoreType.DMA((11,))]
    return pl.pallas_call(
        functools.partial(inner_kernel, seg),
        out_shape=outs,
        in_specs=[SMEM] + [VMEM] * (2 + len(pieces)),
        out_specs=[ANY] * 9,
        scratch_shapes=scratch,
        compiler_params=pltpu.CompilerParams(vmem_limit_bytes=52 * 2**20),
        cost_estimate=pl.CostEstimate(
            flops=4 * 2 * 3000 * CH * CH, bytes_accessed=12 * 2**20, transcendentals=0
        ),
        name="inner_last" if seg else "inner_first",
    )(edges, *pieces, kernels, weights)


def outer_kernel(seg, *refs):
    refs = list(refs)
    take = lambda n: [refs.pop(0) for _ in range(n)]
    edges = take(1)[0]
    pieces = take(1 if seg else 3)
    top, bottom, kernels, weights = take(4)
    if seg:
        cot = take(1)[0]
    x_in = take(3)
    take(6)
    if seg:
        out, pre, strip_left, strip_right, grad = take(5)
    else:
        x_out, up_out, down_out, hid_three, slope_three = take(5)
    hid_out, slope_out = take(3), take(3)
    x_bufs, h_bufs, slopes = take(4), take(4), take(4)
    hid_two, own_buf, sem = take(3)
    side = SIDES[seg]

    loads = []
    for layer in range(3):
        first = INNER[layer] + 1
        depth = (4, 8, 18)[layer]
        spots = [(first, 0)] if layer == 2 else [(first, 0), (ROWS - first - depth, depth)]
        for k, (r, at) in enumerate(spots):
            copy = pltpu.make_async_copy(
                x_in[layer].at[pl.ds(at, depth)],
                x_bufs[layer + 1].at[pl.ds(RH + r, depth)],
                sem.at[20 + 2 * layer + k],
            )
            copy.start()
            loads.append((layer, copy))

    for r in (0, 1, ROWS - 2, ROWS - 1):
        fill_row(x_bufs[0], RH + r, PAD, pieces, r)

    def build_ends(r, _):
        fill_row(x_bufs[0], r, PAD, [top], r)
        fill_row(x_bufs[0], RH + ROWS + r, PAD, [bottom], r)
        return 0

    lax.fori_loop(0, RH, build_ends, 0)
    copies = []

    def send(src, dst, slot):
        copies.append(pltpu.make_async_copy(src, dst, sem.at[slot]))
        copies[-1].start()

    for layer in range(3):
        src, dst = x_bufs[layer], x_bufs[layer + 1]
        h_buf, slope_buf = h_bufs[layer], slopes[layer]
        halo, edge, dhalo = HALO[layer], INNER[layer], DHALO[layer]
        low, high = SPANS[seg][layer]
        taps = rows_of(kernels[layer], 0.5)
        hid_own = hid_two if layer == 2 else None
        skip = DSKIP[layer]
        kept = 5 - skip

        if skip:

            def far_body(it, _):
                low_side = it >= skip
                at = jnp.where(low_side, 15 + 3 * kept + 3 * (it - skip), 3 * it)
                r = jnp.where(low_side, ROWS - 1 - edge - 15, -halo) + at
                act_rows(src, taps, seg, layer, r, 3, False, h_buf, at, None, 0, None)
                return 0

            lax.fori_loop(0, 2 * skip, far_body, 0)

        def near_body(it, _):
            low_side = it >= kept
            at = jnp.where(low_side, 15 + 3 * (it - kept), 3 * skip + 3 * it)
            r = jnp.where(low_side, ROWS - 1 - edge - 15, -halo) + at
            act_rows(src, taps, seg, layer, r, 3, True, h_buf, at, slope_buf, 3 * it, hid_own)
            return 0

        lax.fori_loop(0, 2 * kept, near_body, 0)

        whole = hid_two if layer == 2 else h_buf
        cols = pl.ds(0, COLS) if layer == 2 else pl.ds(side - low, COLS)
        send(whole.at[pl.ds(halo, edge + 1), cols], hid_out[layer].at[pl.ds(0, edge + 1)], layer)
        send(
            whole.at[pl.ds(15, edge + 1), cols],
            hid_out[layer].at[pl.ds(ROWS - 1 - edge, edge + 1)],
            3 + layer,
        )
        number = 3 * kept
        send(slope_buf.at[pl.ds(0, number)], slope_out[layer].at[pl.ds(0, number)], 6 + layer)
        send(
            slope_buf.at[pl.ds(number, number)],
            slope_out[layer].at[pl.ds(dhalo + ROWS - 1 - edge, number)],
            9 + layer,
        )
        for which, copy in loads:
            if which == layer:
                copy.wait()

        def mix_body(it, _):
            r = jnp.where(it == 0, -halo, ROWS - 1 - edge)
            dst[pl.ds(RH + r, 15), PAD + low : PAD + high] = mixed_rows(
                h_buf, 15 * it, src, r, 15, seg, layer, weights
            )
            return 0

        lax.fori_loop(0, 2, mix_body, 0)
        clear_rows(dst, edges, RH)
        clear_columns(dst, edges, seg)

    taps = rows_of(kernels[3], 0.5)

    def last_body(it, _):
        act_rows(
            x_bufs[3], taps, seg, 3, 4 * it, 4, True, h_bufs[3], 4 * it, slopes[3], 4 * it, None
        )
        return 0

    lax.fori_loop(0, ROWS // 4, last_body, 0)
    if not seg:
        send(h_bufs[3].at[:, pl.ds(CHALO, COLS)], hid_three, 12)
        send(slopes[3], slope_three, 13)

    def last_mix(it, _):
        at = 16 * it
        value = mixed_rows(h_bufs[3], at, x_bufs[3], at, 16, seg, 3, weights)
        own_buf[pl.ds(at, 16)] = value.astype(BF)
        return 0

    lax.fori_loop(0, 2, last_mix, 0)
    if seg:
        send(own_buf, out, 14)
        total = jnp.zeros((CH, CH), F32)
        edge_cols = []
        for b in range(2):
            rows = slice(16 * b, 16 * b + 16)
            up = cot[rows]
            total = total + grad_of(h_bufs[3][rows], up)
            pulled = pull_back(up, weights[3])
            value = pulled.reshape(16, COLS, CH) * slopes[3][rows].astype(F32)
            value = value.astype(BF)
            pre[rows] = value
            strip_left[rows] = value[:, :CHALO]
            strip_right[rows] = value[:, COLS - CHALO :]
            edge_cols.append(up.astype(F32))
        pack_edges(strip_left, strip_right, edge_cols)
        grad[...] = total
    else:
        zeros = jnp.zeros((ROWS, CHALO, CH), BF)

        @pl.when(edges[2] == 1)
        def _():
            own_buf[:, 0:CHALO] = zeros

        @pl.when(edges[3] == 1)
        def _():
            own_buf[:, CHALO + COLS : WIDE] = zeros

        send(own_buf, x_out, 14)
        send(own_buf.at[pl.ds(0, RH)], up_out, 15)
        send(own_buf.at[pl.ds(ROWS - RH, RH)], down_out, 16)
    for copy in copies:
        copy.wait()


def pack_edges(strip_left, strip_right, halves):
    first, second = halves
    strip_left[ROWS : ROWS + 16] = jnp.concatenate([first[:, :8], second[:, :8]], 1).astype(BF)
    strip_right[ROWS : ROWS + 16] = jnp.concatenate(
        [first[:, COLS - 8 :], second[:, COLS - 8 :]], 1
    ).astype(BF)


def outer(seg, edges, pieces, top, bottom, kernels, weights, begun, extra=()):
    block = sds((ROWS, COLS, CH), BF)
    strip = sds((ROWS + 16, CHALO, CH), BF)
    if seg:
        outs = [block, block, strip, strip, sds((CH, CH), F32)]
        specs = [ANY] + [VMEM] * 4
    else:
        ends_shape = sds((RH, WIDE, CH), BF)
        outs = [sds((ROWS, WIDE, CH), BF), ends_shape, ends_shape, block, block]
        specs = [ANY] * 5
    shift = len(outs)
    outs = outs + [sds(a.shape, BF) for a in begun[:6]]
    specs = specs + [ANY] * 6
    args = (edges, *pieces, top, bottom, kernels, weights, *extra, *begun[6:], *begun[:6])
    breadth = [b - a for a, b in SPANS[seg]]
    scratch = [pltpu.VMEM((ROWS + 2 * RH, x_wide(seg), CH), F32)] * 4
    heights = [30, 30, 30, ROWS]
    scratch += [pltpu.VMEM((heights[k], breadth[k], CH), BF) for k in range(4)]
    tall = [6 * (5 - DSKIP[k]) for k in range(3)] + [ROWS]
    scratch += [pltpu.VMEM((tall[k], SLOPE_SHAPES[k][1], CH), BF) for k in range(4)]
    scratch += [pltpu.VMEM((30, COLS, CH), BF), pltpu.VMEM((ROWS, breadth[3], CH), BF)]
    scratch += [pltpu.SemaphoreType.DMA((26,))]
    return pl.pallas_call(
        functools.partial(outer_kernel, seg),
        out_shape=outs,
        in_specs=[SMEM] + [VMEM] * (len(args) - 10) + [ANY] * 9,
        out_specs=specs,
        scratch_shapes=scratch,
        input_output_aliases={len(args) - 6 + k: shift + k for k in range(6)},
        compiler_params=pltpu.CompilerParams(vmem_limit_bytes=52 * 2**20),
        cost_estimate=pl.CostEstimate(
            flops=4 * 2 * 5000 * CH * CH, bytes_accessed=12 * 2**20, transcendentals=0
        ),
        name="outer_last" if seg else "outer_first",
    )(*args)


def pool_kernel(feature, cot, x_last, weight, out, back, grad):
    total = None
    for b in range(ROWS // STRIDE):
        rows = slice(STRIDE * b, STRIDE * (b + 1))

        def block_sum(ref):
            value = ref[STRIDE * b].astype(F32)
            for r in range(1, STRIDE):
                value = value + ref[STRIDE * b + r].astype(F32)
            return value.reshape(COLS // STRIDE, STRIDE, CH).sum(axis=1)

        pooled = (block_sum(feature) * (1.0 / (STRIDE * STRIDE))).astype(BF)
        block_cot = block_sum(cot).astype(BF)
        coarse = jnp.dot(pooled, weight[...], preferred_element_type=F32)
        value = x_last[rows].astype(F32).reshape(STRIDE, COLS // STRIDE, STRIDE, CH)
        value = value + coarse[:, None, :][None]
        out[rows] = value.reshape(STRIDE, COLS, CH).astype(BF)
        back[b] = pull_back(block_cot, weight[...]) * (1.0 / (STRIDE * STRIDE))
        part = grad_of(pooled, block_cot)
        total = part if total is None else total + part
    grad[...] = total


def pool(feature, cot, x_last, weight):
    small = sds((ROWS // STRIDE, COLS // STRIDE, CH), F32)
    return pl.pallas_call(
        pool_kernel,
        out_shape=[sds((ROWS, COLS, CH), BF), small, sds((CH, CH), F32)],
        in_specs=[VMEM] * 4,
        out_specs=[VMEM] * 3,
        compiler_params=pltpu.CompilerParams(vmem_limit_bytes=16 * 2**20),
        cost_estimate=pl.CostEstimate(flops=10**9, bytes_accessed=4 * 2**20, transcendentals=0),
        name="pool",
    )(feature, cot, x_last, weight)


BASE = 8


def fill_pre(buf, row, pre, from_left, from_right, r):
    buf[row, 0:16] = from_left[r].astype(F32)
    buf[row, 16:144] = pre[r].astype(F32)
    buf[row, 144:160] = from_right[r].astype(F32)


def base_row(base, from_left, from_right, r, half):
    side = slice(8 * half, 8 * half + 8)
    return jnp.concatenate(
        [
            from_left[ROWS + r].astype(F32)[side],
            base[r + 16 * half].astype(F32),
            from_right[ROWS + r].astype(F32)[side],
        ],
        0,
    )


def row_taps(buf, r, taps, which, low=8, high=152):
    parts = []
    for c, width in chunks(low, high, 32):
        parts.append(tap_sum(buf, r, c, width, 8, -1, taps, which).reshape(width, CH))
    return jnp.concatenate(parts, 0)


def ends_kernel(pre, from_left, from_right, base, kernel, up, down, buf):
    taps = rows_of(kernel, 1.0)

    def build(r, _):
        fill_pre(buf, r, pre, from_left, from_right, r)
        fill_pre(buf, 16 + r, pre, from_left, from_right, 16 + r)
        return 0

    lax.fori_loop(0, 16, build, 0)
    zeros = jnp.zeros((8, CH), F32)

    def one(r, half, which):
        value = row_taps(buf, r + 16 * half, taps, which)
        value = value + base_row(base, from_left, from_right, r, half)
        return jnp.concatenate([zeros, value, zeros], 0).astype(BF)

    def body(r, _):
        up[r] = one(r, 0, (-1, 0))
        down[r] = one(ROWS - 23 + r, 1, (0, 1))
        return 0

    lax.fori_loop(0, 7, body, 0)

    def body_pre(r, _):
        up[7 + r] = buf[r].astype(BF)
        down[7 + r] = buf[ROWS - 8 + r].astype(BF)
        return 0

    lax.fori_loop(0, 8, body_pre, 0)


def ends(pre, from_left, from_right, base, kernel):
    strip = sds((RH, WIDE, CH), BF)
    return pl.pallas_call(
        ends_kernel,
        out_shape=[strip, strip],
        in_specs=[VMEM] * 5,
        out_specs=[VMEM] * 2,
        scratch_shapes=[pltpu.VMEM((ROWS, WIDE, CH), F32)],
        compiler_params=pltpu.CompilerParams(vmem_limit_bytes=20 * 2**20),
        cost_estimate=pl.CostEstimate(flops=10**8, bytes_accessed=6 * 2**20, transcendentals=0),
        name="ends",
    )(pre, from_left, from_right, base, kernel)


def own_kernel(pre, from_left, from_right, base, kernel, out, buf):
    taps = rows_of(kernel, 1.0)

    def build(r, _):
        fill_pre(buf, r, pre, from_left, from_right, r)
        fill_pre(buf, 16 + r, pre, from_left, from_right, 16 + r)
        return 0

    lax.fori_loop(0, 16, build, 0)

    def one(r, half, which):
        value = row_taps(buf, r + 16 * half, taps, which)
        out[r + 16 * half] = value + base_row(base, from_left, from_right, r, half)

    def body_edge(r, _):
        one(r, 0, (-1, 0))
        one(r + 8, 1, (0, 1))
        return 0

    def body_middle(r, _):
        one(r + 8, 0, (-1, 0, 1))
        one(r, 1, (-1, 0, 1))
        return 0

    lax.fori_loop(0, 8, body_edge, 0)
    lax.fori_loop(0, 8, body_middle, 0)


def own_part(pre, from_left, from_right, base, kernel):
    return pl.pallas_call(
        own_kernel,
        out_shape=sds((ROWS, UWIDE, CH), F32),
        in_specs=[VMEM] * 5,
        out_specs=VMEM,
        scratch_shapes=[pltpu.VMEM((ROWS, WIDE, CH), F32)],
        compiler_params=pltpu.CompilerParams(vmem_limit_bytes=20 * 2**20),
        cost_estimate=pl.CostEstimate(
            flops=2 * 10**9, bytes_accessed=6 * 2**20, transcendentals=0
        ),
        name="own_part",
    )(pre, from_left, from_right, base, kernel)


UHALO = 7
UWIDE = COLS + 16


def backward_kernel(last, *refs):
    refs = list(refs)
    take = lambda n: [refs.pop(0) for _ in range(n)]
    edges, pre, from_left, from_right, top, bottom = take(6)
    kernels, weights = take(2)
    count = 3 if last else 4
    if last:
        back = take(1)[0]
    part_in = take(1)[0]
    slope_in = take(count)
    hid_in = take(count)
    if last:
        out, grads = take(2)
    else:
        up_out, pre_out, strip_left, strip_right, grads = take(5)
    buf, ups = take(2)
    slopes = take(count)
    hids = take(count)
    sem = take(1)[0]

    copies = []
    for k in range(count):
        copies.append(
            (
                pltpu.make_async_copy(slope_in[k], slopes[k], sem.at[2 * k]),
                pltpu.make_async_copy(hid_in[k], hids[k], sem.at[2 * k + 1]),
            )
        )
        copies[-1][0].start()
        copies[-1][1].start()

    part_copy = pltpu.make_async_copy(
        part_in, ups.at[pl.ds(UHALO, ROWS)], sem.at[2 * count]
    )
    part_copy.start()

    def build(r, _):
        fill_pre(buf, BASE + r, pre, from_left, from_right, r)
        fill_pre(buf, BASE + 24 + r, pre, from_left, from_right, 24 + r)
        return 0

    lax.fori_loop(0, 8, build, 0)

    def build_pre(r, _):
        buf[r] = top[7 + r].astype(F32)
        buf[BASE + ROWS + r] = bottom[7 + r].astype(F32)
        return 0

    lax.fori_loop(0, 8, build_pre, 0)

    def build_ups(r, _):
        ups[r] = top[r].astype(F32)[8:152]
        ups[UHALO + ROWS + r] = bottom[r].astype(F32)[8:152]
        return 0

    lax.fori_loop(0, 7, build_ups, 0)

    def add_taps(r, low, high, dilate, taps, which, extra=None):
        for c, width in chunks(low, high, 32):
            start = ups[UHALO + r, c - 8 : c - 8 + width].reshape(width // 8, 8, CH)
            total = tap_sum(buf, BASE + r, c, width, dilate, -1, taps, which, start)
            if extra is not None:
                total = total + extra[(c - low) // 8 : (c - low + width) // 8][:, None, :]
                out[r, c - low : c - low + width] = total.reshape(width, CH).astype(BF)
            else:
                ups[UHALO + r, c - 8 : c - 8 + width] = total.reshape(width, CH)

    taps = rows_of(kernels[3], 1.0)

    part_copy.wait()

    def first_upper(r, _):
        add_taps(r, 8, 152, 8, taps, (1,))
        add_taps(24 + r, 8, 152, 8, taps, (-1,))
        return 0

    lax.fori_loop(0, 8, first_upper, 0)

    def first_ends(r, _):
        add_taps(r - 7, 8, 152, 8, taps, (-1,))
        add_taps(ROWS + r, 8, 152, 8, taps, (1,))
        return 0

    lax.fori_loop(0, 7, first_ends, 0)

    for k, layer in enumerate((2, 1, 0)):
        dilate = 2**layer
        halo = (1, 3, 7)[layer]
        copies[k][0].wait()
        copies[k][1].wait()
        step = (ROWS + 2 * halo) // 2
        skip = DHALO[layer] - halo

        def pull_body(it, _):
            at = it * step
            up = ups[pl.ds(UHALO - halo + at, step)].astype(BF)
            pulled = pull_back(up, weights[layer]).reshape(step, UWIDE, CH)
            slope = slopes[k][pl.ds(skip + at, step)].astype(F32)
            slope = slope[:, DSIDE[layer] - 8 : DSIDE[layer] - 8 + UWIDE]
            buf[pl.ds(BASE - halo + at, step), 8:152] = pulled * slope
            return 0

        lax.fori_loop(0, 2, pull_body, 0)
        clear_rows(buf, edges, 8)
        zeros = jnp.zeros((ROWS + 16, CHALO, CH), F32)

        @pl.when(edges[2] == 1)
        def _():
            buf[:, 0:CHALO] = zeros

        @pl.when(edges[3] == 1)
        def _():
            buf[:, CHALO + COLS : WIDE] = zeros

        total = jnp.zeros((CH, CH), F32)
        for b in range(2):
            up = ups[UHALO + 16 * b : UHALO + 16 * b + 16, 8:136].astype(BF)
            total = total + grad_of(hids[k][16 * b : 16 * b + 16], up)
        grads[k] = total

        taps = rows_of(kernels[layer], 1.0)
        reach = (0, 1, 3)[layer]
        low, high = ((16, 144), (8, 152), (8, 152))[layer]

        def tap_body(it, _):
            for q in range(2):
                r = 2 * it + q - reach
                if last and layer == 0:
                    add_taps(r, low, high, dilate, taps, (-1, 0, 1), back[r // STRIDE])
                else:
                    add_taps(r, low, high, dilate, taps, (-1, 0, 1))
            return 0

        if layer == 1:
            lax.fori_loop(0, (ROWS + 2) // 2, tap_body, 0)
        else:
            lax.fori_loop(0, (ROWS + 2 * reach) // 2, tap_body, 0)

    if not last:
        copies[3][0].wait()
        copies[3][1].wait()
        total = jnp.zeros((CH, CH), F32)
        edge_cols = []
        for b in range(2):
            rows = slice(16 * b, 16 * b + 16)
            value = ups[UHALO + 16 * b : UHALO + 16 * b + 16, 8:136]
            up_out[rows] = value
            up = value.astype(BF)
            total = total + grad_of(hids[3][rows], up)
            pulled = pull_back(up, weights[3])
            value = (pulled.reshape(16, COLS, CH) * slopes[3][rows].astype(F32)).astype(BF)
            pre_out[rows] = value
            strip_left[rows] = value[:, :CHALO]
            strip_right[rows] = value[:, COLS - CHALO :]
            edge_cols.append(ups[UHALO + 16 * b : UHALO + 16 * b + 16, 8:136])
        pack_edges(strip_left, strip_right, edge_cols)
        grads[3] = total


def backward(last, edges, pre, sides, part, ends_in, kernels, weights, slopes, hids, back=()):
    count = len(slopes)
    block = sds((ROWS, COLS, CH), BF)
    if last:
        outs = [block, sds((count, CH, CH), F32)]
    else:
        strip = sds((ROWS + 16, CHALO, CH), BF)
        outs = [sds((ROWS, COLS, CH), F32), block, strip, strip, sds((count, CH, CH), F32)]
    scratch = [
        pltpu.VMEM((ROWS + 16, WIDE, CH), F32),
        pltpu.VMEM((ROWS + 2 * UHALO, UWIDE, CH), F32),
    ]
    scratch += [pltpu.VMEM(a.shape, BF) for a in slopes]
    scratch += [pltpu.VMEM(a.shape, BF) for a in hids]
    scratch += [pltpu.SemaphoreType.DMA((2 * count + 1,))]
    args = (edges, pre, *sides, *ends_in, kernels, weights, *back)
    return pl.pallas_call(
        functools.partial(backward_kernel, last),
        out_shape=outs,
        in_specs=[SMEM] + [VMEM] * (len(args) - 1) + [ANY] * (1 + 2 * count),
        out_specs=[VMEM] * len(outs),
        scratch_shapes=scratch,
        compiler_params=pltpu.CompilerParams(vmem_limit_bytes=30 * 2**20),
        cost_estimate=pl.CostEstimate(
            flops=7 * 2 * 5000 * CH * CH, bytes_accessed=14 * 2**20, transcendentals=0
        ),
        name="backward_last" if last else "backward_first",
    )(*args, part, *slopes, *hids)


def exchange(to_before, to_after, axis):
    ends_at = lax.axis_size(axis) - 1
    forth = [(i, i + 1) for i in range(ends_at)]
    back = [(i + 1, i) for i in range(ends_at)]
    return lax.ppermute(to_after, axis, forth), lax.ppermute(to_before, axis, back)


def local(features_in, cotangent, depth_kernels, point_weights, coarse_weight):
    row, col = lax.axis_index("rows"), lax.axis_index("cols")
    row_end, col_end = lax.axis_size("rows") - 1, lax.axis_size("cols") - 1
    edges = jnp.stack([row == 0, row == row_end, col == 0, col == col_end]).astype(jnp.int32)
    kernels = depth_kernels.astype(F32)

    left, right = exchange(
        features_in[:, : SIDES[0]], features_in[:, COLS - SIDES[0] :], "cols"
    )
    wide = lambda rows: jnp.concatenate([left[rows], features_in[rows], right[rows]], axis=1)
    top, bottom = exchange(wide(slice(0, RH)), wide(slice(ROWS - RH, ROWS)), "rows")
    pieces = (left, features_in, right)
    begun = inner(0, edges, pieces, kernels[:3], point_weights[:3])
    x_mid, x_up, x_down, hid_three, slope_three, *kept = outer(
        0, edges, pieces, top, bottom, kernels[:4], point_weights[:4], begun
    )
    hid_low, slope_low = kept[:3] + [hid_three], kept[3:] + [slope_three]
    top, bottom = exchange(x_up, x_down, "rows")
    begun = inner(1, edges, (x_mid,), kernels[4:7], point_weights[4:7])
    x_last, pre, strip_left, strip_right, grad_top, *kept = outer(
        1, edges, (x_mid,), top, bottom, kernels[4:], point_weights[4:], begun,
        (cotangent,),
    )
    hid_high, slope_high = kept[:3], kept[3:]

    order = lambda things: [things[2], things[1], things[0]]
    sides = exchange(strip_left, strip_right, "cols")
    rows_in = exchange(*ends(pre, *sides, cotangent, kernels[7]), "rows")
    part = own_part(pre, *sides, cotangent, kernels[7])
    upstream, pre, strip_left, strip_right, grad_mid = backward(
        False, edges, pre, sides, part, rows_in,
        kernels[4:], jnp.concatenate([point_weights[4:7], point_weights[3:4]]),
        order(slope_high) + [slope_low[3]], order(hid_high) + [hid_low[3]],
    )
    sides = exchange(strip_left, strip_right, "cols")
    rows_in = exchange(*ends(pre, *sides, upstream, kernels[3]), "rows")
    output, back, coarse_grad = pool(features_in, cotangent, x_last, coarse_weight)
    later, back = lax.optimization_barrier((upstream, back))
    part = own_part(pre, *sides, later, kernels[3])
    input_grad, grad_low = backward(
        True, edges, pre, sides, part, rows_in,
        kernels[:4], point_weights[:3], order(slope_low), order(hid_low), (back,),
    )

    grads = [grad_low[2], grad_low[1], grad_low[0], grad_mid[3], grad_mid[2], grad_mid[1]]
    grads = jnp.stack(grads + [grad_mid[0], grad_top, coarse_grad]).astype(BF)
    shares = lax.all_to_all(grads, "rows", 1, 0, tiled=True)
    summed = shares.reshape(-1, grads.shape[0], CH * 4).astype(F32).sum(axis=0)
    parts = lax.all_gather(summed.astype(BF), "cols", axis=0, tiled=False)
    weight_grads = parts.astype(F32).sum(axis=0).reshape(grads.shape[0], 4, CH)
    return (output, input_grad, weight_grads)


def solution(mesh):
    in_specs = (P("rows", "cols", None), P("rows", "cols", None), P(), P(), P())
    out_specs = (P("rows", "cols", None), P("rows", "cols", None), P(None, "rows", None))
    return jax.shard_map(local, mesh=mesh, in_specs=in_specs, out_specs=out_specs, check_vma=False)
```

```python
import functools

import jax
import jax.numpy as jnp
from jax import lax
from jax.experimental import pallas as pl
from jax.experimental.pallas import tpu as pltpu
from jax.sharding import PartitionSpec as P

STRIDE = 8
F32 = jnp.float32
BF = jnp.bfloat16
C0 = 0.7978845608028654
C1 = 0.7978845608028654 * 0.044715

ROWS, COLS, CH = 32, 128, 128
RH, CHALO = 15, 16
WIDE = COLS + 2 * CHALO
PAD = 8

HALO = (14, 12, 8, 0)
SIDES = (32, 16)
SPANS = (
    ((0, 192), (0, 192), (8, 184), (16, 176)),
    ((0, 160), (0, 160), (8, 152), (16, 144)),
)
DHALO = (2, 3, 8, 0)
DSIDE = (16, 16, 8, 0)

VMEM = pl.BlockSpec(memory_space=pltpu.VMEM)
SMEM = pl.BlockSpec(memory_space=pltpu.SMEM)
ANY = pl.BlockSpec(memory_space=pl.ANY)


def sds(shape, dtype):
    return jax.ShapeDtypeStruct(shape, dtype)


def gelu_parts(half, want_slope):
    square = half * half
    t = jnp.tanh(half * (BF(2 * C0) + BF(8 * C1) * square))
    half_t = half * t
    hidden = half + half_t
    if not want_slope:
        return hidden, None
    slope = (BF(0.5) + BF(0.5) * t) + (half - half_t * t) * (BF(C0) + BF(12 * C1) * square)
    return hidden, slope


def rows_of(kernel, scale):
    return [jnp.broadcast_to(kernel[t : t + 1, :] * scale, (8, CH))[None] for t in range(9)]


def tap_sum(src, row, col, width, dilate, sign, taps, which, start=None):
    total = start
    for i in which:
        for j in (-1, 0, 1):
            at = col + sign * j * dilate
            piece = src[row + sign * i * dilate, at : at + width, :].reshape(width // 8, 8, CH)
            piece = piece * taps[(i + 1) * 3 + j + 1]
            total = piece if total is None else total + piece
    return total


def chunks(low, high, size):
    out = []
    while low < high:
        out.append((low, min(size, high - low)))
        low += size
    return out


def pull_back(upstream, weight):
    return lax.dot_general(
        upstream.reshape(-1, CH), weight, (((1,), (1,)), ((), ())), preferred_element_type=F32
    )


def grad_of(hidden, upstream):
    return lax.dot_general(
        hidden.reshape(-1, CH),
        upstream.reshape(-1, CH),
        (((0,), (0,)), ((), ())),
        preferred_element_type=F32,
    )


INNER = (0, 2, 6)
DSKIP = (4, 3, 0)


def act_rows(src, taps, seg, layer, r, number, want_slope, h_buf, h_at, slope_buf, slope_at, hid_own):
    low, high = SPANS[seg][layer]
    first = SIDES[seg] - DSIDE[layer] - low
    for q in range(number):
        parts = []
        for c, width in chunks(low, high, 32):
            half = tap_sum(src, RH + r + q, PAD + c, width, 2**layer, 1, taps, (-1, 0, 1))
            parts.append(gelu_parts(half.reshape(width, CH).astype(BF), want_slope))
        hidden = jnp.concatenate([p[0] for p in parts], 0)
        h_buf[h_at + q] = hidden
        if hid_own is not None:
            own = hidden.astype(F32)[SIDES[seg] - low : SIDES[seg] - low + COLS]
            hid_own[h_at + q] = own.astype(BF)
        if want_slope:
            slope = jnp.concatenate([p[1] for p in parts], 0)
            slope_buf[slope_at + q] = slope[first : first + COLS + 2 * DSIDE[layer]]


def mixed_rows(h_buf, h_at, src, r, step, seg, layer, weights):
    low, high = SPANS[seg][layer]
    mixed = jnp.dot(
        h_buf[pl.ds(h_at, step)].reshape(step * (high - low), CH),
        weights[layer],
        preferred_element_type=F32,
    ).reshape(step, high - low, CH)
    return src[pl.ds(RH + r, step), PAD + low : PAD + high] + mixed


def fill_row(buf, row, at, pieces, r):
    for piece in pieces:
        width = piece.shape[1]
        buf[row, at : at + width] = piece[r].astype(F32)
        at += width


def clear_columns(ref, edges, seg):
    side = SIDES[seg]
    count = ref.shape[0]

    @pl.when(edges[2] == 1)
    def _():
        ref[:, PAD : PAD + side] = jnp.zeros((count, side, CH), F32)

    @pl.when(edges[3] == 1)
    def _():
        ref[:, PAD + side + COLS : PAD + 2 * side + COLS] = jnp.zeros((count, side, CH), F32)


def clear_rows(ref, edges, number):
    count, breadth = ref.shape[0], ref.shape[1]

    @pl.when(edges[0] == 1)
    def _():
        ref[0:number] = jnp.zeros((number, breadth, CH), F32)

    @pl.when(edges[1] == 1)
    def _():
        ref[count - number : count] = jnp.zeros((number, breadth, CH), F32)


def inner_kernel(seg, *refs):
    refs = list(refs)
    take = lambda n: [refs.pop(0) for _ in range(n)]
    edges = take(1)[0]
    pieces = take(1 if seg else 3)
    kernels, weights = take(2)
    hid_out, slope_out, x_all = take(3), take(3), take(1)[0]
    x_out = [x_all.at[pl.ds(o, n)] for o, n in ((0, 8), (8, 16), (24, 18))]
    x_bufs, h_bufs, slopes = take(4), take(3), take(3)
    hid_two, sem = take(2)

    def build(r, _):
        fill_row(x_bufs[0], RH + r, PAD, pieces, r)
        return 0

    lax.fori_loop(0, ROWS, build, 0)
    copies = []

    def send(src, dst, slot):
        copies.append(pltpu.make_async_copy(src, dst, sem.at[slot]))
        copies[-1].start()

    for layer in range(3):
        src, dst = x_bufs[layer], x_bufs[layer + 1]
        h_buf, slope_buf = h_bufs[layer], slopes[layer]
        low, high = SPANS[seg][layer]
        edge = INNER[layer]
        first, number = edge + 1, ROWS - 2 - 2 * edge
        group = (5, 2, 6)[layer]
        taps = rows_of(kernels[layer], 0.5)
        hid_own = hid_two if layer == 2 else None

        def body(it, _):
            at = group * it
            act_rows(
                src, taps, seg, layer, first + at, group, True, h_buf, at, slope_buf, at, hid_own
            )
            return 0

        lax.fori_loop(0, number // group, body, 0)
        rows = pl.ds(first, number)
        hid_src = hid_two if layer == 2 else h_buf.at[:, pl.ds(SIDES[seg] - low, COLS)]
        send(hid_src, hid_out[layer].at[rows], layer)
        send(slope_buf, slope_out[layer].at[pl.ds(DHALO[layer] + first, number)], 3 + layer)

        step = (15, 13, 9)[layer]

        def mix_body(it, _):
            at = it * step
            dst[pl.ds(RH + first + at, step), PAD + low : PAD + high] = mixed_rows(
                h_buf, at, src, first + at, step, seg, layer, weights
            )
            return 0

        lax.fori_loop(0, number // step, mix_body, 0)
        clear_columns(dst, edges, seg)
        depth = (4, 8, 18)[layer]
        send(dst.at[pl.ds(RH + first, depth)], x_out[layer].at[pl.ds(0, depth)], 6 + layer)
        if layer < 2:
            send(
                dst.at[pl.ds(RH + first + number - depth, depth)],
                x_out[layer].at[pl.ds(depth, depth)],
                9 + layer,
            )
    for copy in copies:
        copy.wait()


SLOPE_SHAPES = [(ROWS + 2 * DHALO[k], COLS + 2 * DSIDE[k], CH) for k in range(4)]


def x_wide(seg):
    return COLS + 2 * SIDES[seg] + 2 * PAD


def inner(seg, edges, pieces, kernels, weights):
    outs = [sds((ROWS, COLS, CH), BF)] * 3
    outs += [sds(s, BF) for s in SLOPE_SHAPES[:3]]
    outs += [sds((42, x_wide(seg), CH), F32)]
    numbers = [ROWS - 2 - 2 * e for e in INNER]
    breadth = [b - a for a, b in SPANS[seg]]
    scratch = [pltpu.VMEM((ROWS + 2 * RH, x_wide(seg), CH), F32)] * 4
    scratch += [pltpu.VMEM((numbers[k], breadth[k], CH), BF) for k in range(3)]
    scratch += [pltpu.VMEM((numbers[k], SLOPE_SHAPES[k][1], CH), BF) for k in range(3)]
    scratch += [pltpu.VMEM((numbers[2], COLS, CH), BF), pltpu.SemaphoreType.DMA((11,))]
    return pl.pallas_call(
        functools.partial(inner_kernel, seg),
        out_shape=outs,
        in_specs=[SMEM] + [VMEM] * (2 + len(pieces)),
        out_specs=[ANY] * 7,
        scratch_shapes=scratch,
        compiler_params=pltpu.CompilerParams(vmem_limit_bytes=52 * 2**20),
        cost_estimate=pl.CostEstimate(
            flops=4 * 2 * 3000 * CH * CH, bytes_accessed=12 * 2**20, transcendentals=0
        ),
        name="inner_last" if seg else "inner_first",
    )(edges, *pieces, kernels, weights)


def outer_kernel(seg, *refs):
    refs = list(refs)
    take = lambda n: [refs.pop(0) for _ in range(n)]
    edges = take(1)[0]
    pieces = take(1 if seg else 3)
    top, bottom, kernels, weights = take(4)
    if seg:
        cot = take(1)[0]
    x_all = take(1)[0]
    x_in = [x_all.at[pl.ds(o, n)] for o, n in ((0, 8), (8, 16), (24, 18))]
    take(6)
    if seg:
        out, pre, strip_left, strip_right, grad = take(5)
    else:
        x_out, up_out, down_out, hid_three, slope_three = take(5)
    hid_out, slope_out = take(3), take(3)
    x_bufs, h_bufs, slopes = take(4), take(4), take(4)
    hid_two, own_buf, sem = take(3)
    side = SIDES[seg]

    loads = []
    for layer in range(3):
        first = INNER[layer] + 1
        depth = (4, 8, 18)[layer]
        spots = [(first, 0)] if layer == 2 else [(first, 0), (ROWS - first - depth, depth)]
        for k, (r, at) in enumerate(spots):
            copy = pltpu.make_async_copy(
                x_in[layer].at[pl.ds(at, depth)],
                x_bufs[layer + 1].at[pl.ds(RH + r, depth)],
                sem.at[20 + 2 * layer + k],
            )
            copy.start()
            loads.append((layer, copy))

    for r in (0, 1, ROWS - 2, ROWS - 1):
        fill_row(x_bufs[0], RH + r, PAD, pieces, r)

    def build_ends(r, _):
        fill_row(x_bufs[0], r, PAD, [top], r)
        fill_row(x_bufs[0], RH + ROWS + r, PAD, [bottom], r)
        return 0

    lax.fori_loop(0, RH, build_ends, 0)
    copies = []

    def send(src, dst, slot):
        copies.append(pltpu.make_async_copy(src, dst, sem.at[slot]))
        copies[-1].start()

    for layer in range(3):
        src, dst = x_bufs[layer], x_bufs[layer + 1]
        h_buf, slope_buf = h_bufs[layer], slopes[layer]
        halo, edge, dhalo = HALO[layer], INNER[layer], DHALO[layer]
        low, high = SPANS[seg][layer]
        taps = rows_of(kernels[layer], 0.5)
        hid_own = hid_two if layer == 2 else None
        skip = DSKIP[layer]
        kept = 5 - skip

        if skip:

            def far_body(it, _):
                low_side = it >= skip
                at = jnp.where(low_side, 15 + 3 * kept + 3 * (it - skip), 3 * it)
                r = jnp.where(low_side, ROWS - 1 - edge - 15, -halo) + at
                act_rows(src, taps, seg, layer, r, 3, False, h_buf, at, None, 0, None)
                return 0

            lax.fori_loop(0, 2 * skip, far_body, 0)

        def near_body(it, _):
            low_side = it >= kept
            at = jnp.where(low_side, 15 + 3 * (it - kept), 3 * skip + 3 * it)
            r = jnp.where(low_side, ROWS - 1 - edge - 15, -halo) + at
            act_rows(src, taps, seg, layer, r, 3, True, h_buf, at, slope_buf, 3 * it, hid_own)
            return 0

        lax.fori_loop(0, 2 * kept, near_body, 0)

        whole = hid_two if layer == 2 else h_buf
        cols = pl.ds(0, COLS) if layer == 2 else pl.ds(side - low, COLS)
        send(whole.at[pl.ds(halo, edge + 1), cols], hid_out[layer].at[pl.ds(0, edge + 1)], layer)
        send(
            whole.at[pl.ds(15, edge + 1), cols],
            hid_out[layer].at[pl.ds(ROWS - 1 - edge, edge + 1)],
            3 + layer,
        )
        number = 3 * kept
        send(slope_buf.at[pl.ds(0, number)], slope_out[layer].at[pl.ds(0, number)], 6 + layer)
        send(
            slope_buf.at[pl.ds(number, number)],
            slope_out[layer].at[pl.ds(dhalo + ROWS - 1 - edge, number)],
            9 + layer,
        )
        for which, copy in loads:
            if which == layer:
                copy.wait()

        def mix_body(it, _):
            r = jnp.where(it == 0, -halo, ROWS - 1 - edge)
            dst[pl.ds(RH + r, 15), PAD + low : PAD + high] = mixed_rows(
                h_buf, 15 * it, src, r, 15, seg, layer, weights
            )
            return 0

        lax.fori_loop(0, 2, mix_body, 0)
        clear_rows(dst, edges, RH)
        clear_columns(dst, edges, seg)

    taps = rows_of(kernels[3], 0.5)

    def last_body(it, _):
        act_rows(
            x_bufs[3], taps, seg, 3, 4 * it, 4, True, h_bufs[3], 4 * it, slopes[3], 4 * it, None
        )
        return 0

    lax.fori_loop(0, ROWS // 4, last_body, 0)
    if not seg:
        send(h_bufs[3].at[:, pl.ds(CHALO, COLS)], hid_three, 12)
        send(slopes[3], slope_three, 13)

    def last_mix(it, _):
        at = 16 * it
        value = mixed_rows(h_bufs[3], at, x_bufs[3], at, 16, seg, 3, weights)
        own_buf[pl.ds(at, 16)] = value.astype(BF)
        return 0

    lax.fori_loop(0, 2, last_mix, 0)
    if seg:
        send(own_buf, out, 14)
        total = jnp.zeros((CH, CH), F32)
        edge_cols = []
        for b in range(2):
            rows = slice(16 * b, 16 * b + 16)
            up = cot[rows]
            total = total + grad_of(h_bufs[3][rows], up)
            pulled = pull_back(up, weights[3])
            value = pulled.reshape(16, COLS, CH) * slopes[3][rows].astype(F32)
            value = value.astype(BF)
            pre[rows] = value
            strip_left[rows] = value[:, :CHALO]
            strip_right[rows] = value[:, COLS - CHALO :]
            edge_cols.append(up.astype(F32))
        pack_edges(strip_left, strip_right, edge_cols)
        grad[...] = total
    else:
        zeros = jnp.zeros((ROWS, CHALO, CH), BF)

        @pl.when(edges[2] == 1)
        def _():
            own_buf[:, 0:CHALO] = zeros

        @pl.when(edges[3] == 1)
        def _():
            own_buf[:, CHALO + COLS : WIDE] = zeros

        send(own_buf, x_out, 14)
        send(own_buf.at[pl.ds(0, RH)], up_out, 15)
        send(own_buf.at[pl.ds(ROWS - RH, RH)], down_out, 16)
    for copy in copies:
        copy.wait()


def pack_edges(strip_left, strip_right, halves):
    first, second = halves
    strip_left[ROWS : ROWS + 16] = jnp.concatenate([first[:, :8], second[:, :8]], 1).astype(BF)
    strip_right[ROWS : ROWS + 16] = jnp.concatenate(
        [first[:, COLS - 8 :], second[:, COLS - 8 :]], 1
    ).astype(BF)


def outer(seg, edges, pieces, top, bottom, kernels, weights, begun, extra=()):
    block = sds((ROWS, COLS, CH), BF)
    strip = sds((ROWS + 16, CHALO, CH), BF)
    if seg:
        outs = [block, block, strip, strip, sds((CH, CH), F32)]
        specs = [ANY] + [VMEM] * 4
    else:
        ends_shape = sds((RH, WIDE, CH), BF)
        outs = [sds((ROWS, WIDE, CH), BF), ends_shape, ends_shape, block, block]
        specs = [ANY] * 5
    shift = len(outs)
    outs = outs + [sds(a.shape, BF) for a in begun[:6]]
    specs = specs + [ANY] * 6
    args = (edges, *pieces, top, bottom, kernels, weights, *extra, *begun[6:], *begun[:6])
    breadth = [b - a for a, b in SPANS[seg]]
    scratch = [pltpu.VMEM((ROWS + 2 * RH, x_wide(seg), CH), F32)] * 4
    heights = [30, 30, 30, ROWS]
    scratch += [pltpu.VMEM((heights[k], breadth[k], CH), BF) for k in range(4)]
    tall = [6 * (5 - DSKIP[k]) for k in range(3)] + [ROWS]
    scratch += [pltpu.VMEM((tall[k], SLOPE_SHAPES[k][1], CH), BF) for k in range(4)]
    scratch += [pltpu.VMEM((30, COLS, CH), BF), pltpu.VMEM((ROWS, breadth[3], CH), BF)]
    scratch += [pltpu.SemaphoreType.DMA((26,))]
    return pl.pallas_call(
        functools.partial(outer_kernel, seg),
        out_shape=outs,
        in_specs=[SMEM] + [VMEM] * (len(args) - 8) + [ANY] * 7,
        out_specs=specs,
        scratch_shapes=scratch,
        input_output_aliases={len(args) - 6 + k: shift + k for k in range(6)},
        compiler_params=pltpu.CompilerParams(vmem_limit_bytes=52 * 2**20),
        cost_estimate=pl.CostEstimate(
            flops=4 * 2 * 5000 * CH * CH, bytes_accessed=12 * 2**20, transcendentals=0
        ),
        name="outer_last" if seg else "outer_first",
    )(*args)


def pool_kernel(feature, cot, x_last, weight, out, back, grad):
    total = None
    for b in range(ROWS // STRIDE):
        rows = slice(STRIDE * b, STRIDE * (b + 1))

        def block_sum(ref):
            value = ref[STRIDE * b].astype(F32)
            for r in range(1, STRIDE):
                value = value + ref[STRIDE * b + r].astype(F32)
            return value.reshape(COLS // STRIDE, STRIDE, CH).sum(axis=1)

        pooled = (block_sum(feature) * (1.0 / (STRIDE * STRIDE))).astype(BF)
        block_cot = block_sum(cot).astype(BF)
        coarse = jnp.dot(pooled, weight[...], preferred_element_type=F32)
        value = x_last[rows].astype(F32).reshape(STRIDE, COLS // STRIDE, STRIDE, CH)
        value = value + coarse[:, None, :][None]
        out[rows] = value.reshape(STRIDE, COLS, CH).astype(BF)
        back[b] = pull_back(block_cot, weight[...]) * (1.0 / (STRIDE * STRIDE))
        part = grad_of(pooled, block_cot)
        total = part if total is None else total + part
    grad[...] = total


def pool(feature, cot, x_last, weight):
    small = sds((ROWS // STRIDE, COLS // STRIDE, CH), F32)
    return pl.pallas_call(
        pool_kernel,
        out_shape=[sds((ROWS, COLS, CH), BF), small, sds((CH, CH), F32)],
        in_specs=[VMEM] * 4,
        out_specs=[VMEM] * 3,
        compiler_params=pltpu.CompilerParams(vmem_limit_bytes=16 * 2**20),
        cost_estimate=pl.CostEstimate(flops=10**9, bytes_accessed=4 * 2**20, transcendentals=0),
        name="pool",
    )(feature, cot, x_last, weight)


BASE = 8


def fill_pre(buf, row, pre, from_left, from_right, r):
    buf[row, 0:16] = from_left[r].astype(F32)
    buf[row, 16:144] = pre[r].astype(F32)
    buf[row, 144:160] = from_right[r].astype(F32)


def base_row(base, from_left, from_right, r, half):
    side = slice(8 * half, 8 * half + 8)
    return jnp.concatenate(
        [
            from_left[ROWS + r].astype(F32)[side],
            base[r + 16 * half].astype(F32),
            from_right[ROWS + r].astype(F32)[side],
        ],
        0,
    )


def row_taps(buf, r, taps, which, low=8, high=152):
    parts = []
    for c, width in chunks(low, high, 32):
        parts.append(tap_sum(buf, r, c, width, 8, -1, taps, which).reshape(width, CH))
    return jnp.concatenate(parts, 0)


def ends_kernel(pre, from_left, from_right, base, kernel, up, down, buf):
    taps = rows_of(kernel, 1.0)

    def build(r, _):
        fill_pre(buf, r, pre, from_left, from_right, r)
        fill_pre(buf, 16 + r, pre, from_left, from_right, 16 + r)
        return 0

    lax.fori_loop(0, 16, build, 0)
    zeros = jnp.zeros((8, CH), F32)

    def one(r, half, which):
        value = row_taps(buf, r + 16 * half, taps, which)
        value = value + base_row(base, from_left, from_right, r, half)
        return jnp.concatenate([zeros, value, zeros], 0).astype(BF)

    def body(r, _):
        up[r] = one(r, 0, (-1, 0))
        down[r] = one(ROWS - 23 + r, 1, (0, 1))
        return 0

    lax.fori_loop(0, 7, body, 0)

    def body_pre(r, _):
        up[7 + r] = buf[r].astype(BF)
        down[7 + r] = buf[ROWS - 8 + r].astype(BF)
        return 0

    lax.fori_loop(0, 8, body_pre, 0)


def ends(pre, from_left, from_right, base, kernel):
    strip = sds((RH, WIDE, CH), BF)
    return pl.pallas_call(
        ends_kernel,
        out_shape=[strip, strip],
        in_specs=[VMEM] * 5,
        out_specs=[VMEM] * 2,
        scratch_shapes=[pltpu.VMEM((ROWS, WIDE, CH), F32)],
        compiler_params=pltpu.CompilerParams(vmem_limit_bytes=20 * 2**20),
        cost_estimate=pl.CostEstimate(flops=10**8, bytes_accessed=6 * 2**20, transcendentals=0),
        name="ends",
    )(pre, from_left, from_right, base, kernel)


def own_kernel(pre, from_left, from_right, base, kernel, out, buf):
    taps = rows_of(kernel, 1.0)

    def build(r, _):
        fill_pre(buf, r, pre, from_left, from_right, r)
        fill_pre(buf, 16 + r, pre, from_left, from_right, 16 + r)
        return 0

    lax.fori_loop(0, 16, build, 0)

    def one(r, half, which):
        value = row_taps(buf, r + 16 * half, taps, which)
        out[r + 16 * half] = value + base_row(base, from_left, from_right, r, half)

    def body_edge(r, _):
        one(r, 0, (-1, 0))
        one(r + 8, 1, (0, 1))
        return 0

    def body_middle(r, _):
        one(r + 8, 0, (-1, 0, 1))
        one(r, 1, (-1, 0, 1))
        return 0

    lax.fori_loop(0, 8, body_edge, 0)
    lax.fori_loop(0, 8, body_middle, 0)


def own_part(pre, from_left, from_right, base, kernel):
    return pl.pallas_call(
        own_kernel,
        out_shape=sds((ROWS, UWIDE, CH), F32),
        in_specs=[VMEM] * 5,
        out_specs=VMEM,
        scratch_shapes=[pltpu.VMEM((ROWS, WIDE, CH), F32)],
        compiler_params=pltpu.CompilerParams(vmem_limit_bytes=20 * 2**20),
        cost_estimate=pl.CostEstimate(
            flops=2 * 10**9, bytes_accessed=6 * 2**20, transcendentals=0
        ),
        name="own_part",
    )(pre, from_left, from_right, base, kernel)


UHALO = 7
UWIDE = COLS + 16


def backward_kernel(last, *refs):
    refs = list(refs)
    take = lambda n: [refs.pop(0) for _ in range(n)]
    edges, pre, from_left, from_right, top, bottom = take(6)
    kernels, weights = take(2)
    count = 3 if last else 4
    if last:
        back = take(1)[0]
    part_in = take(1)[0]
    slope_in = take(count)
    if last:
        hid_in = take(count)
        out, grads = take(2)
    else:
        up_out, pre_out, strip_left, strip_right = take(4)
        held_out = take(count)
    buf, ups = take(2)
    slopes = take(count)
    hids = take(count)
    sem = take(1)[0]

    copies = []
    for k in range(count):
        copies.append([pltpu.make_async_copy(slope_in[k], slopes[k], sem.at[2 * k])])
        if last:
            copies[-1].append(pltpu.make_async_copy(hid_in[k], hids[k], sem.at[2 * k + 1]))
        else:
            copies[-1].append(pltpu.make_async_copy(hids[k], held_out[k], sem.at[2 * k + 1]))
        copies[-1][0].start()
        if last:
            copies[-1][1].start()

    part_copy = pltpu.make_async_copy(
        part_in, ups.at[pl.ds(UHALO, ROWS)], sem.at[2 * count]
    )
    part_copy.start()

    def build(r, _):
        fill_pre(buf, BASE + r, pre, from_left, from_right, r)
        fill_pre(buf, BASE + 24 + r, pre, from_left, from_right, 24 + r)
        return 0

    lax.fori_loop(0, 8, build, 0)

    def build_pre(r, _):
        buf[r] = top[7 + r].astype(F32)
        buf[BASE + ROWS + r] = bottom[7 + r].astype(F32)
        return 0

    lax.fori_loop(0, 8, build_pre, 0)

    def build_ups(r, _):
        ups[r] = top[r].astype(F32)[8:152]
        ups[UHALO + ROWS + r] = bottom[r].astype(F32)[8:152]
        return 0

    lax.fori_loop(0, 7, build_ups, 0)

    def add_taps(r, low, high, dilate, taps, which, extra=None):
        for c, width in chunks(low, high, 32):
            start = ups[UHALO + r, c - 8 : c - 8 + width].reshape(width // 8, 8, CH)
            total = tap_sum(buf, BASE + r, c, width, dilate, -1, taps, which, start)
            if extra is not None:
                total = total + extra[(c - low) // 8 : (c - low + width) // 8][:, None, :]
                out[r, c - low : c - low + width] = total.reshape(width, CH).astype(BF)
            else:
                ups[UHALO + r, c - 8 : c - 8 + width] = total.reshape(width, CH)

    taps = rows_of(kernels[3], 1.0)

    part_copy.wait()

    def first_upper(r, _):
        add_taps(r, 8, 152, 8, taps, (1,))
        add_taps(24 + r, 8, 152, 8, taps, (-1,))
        return 0

    lax.fori_loop(0, 8, first_upper, 0)

    def first_ends(r, _):
        add_taps(r - 7, 8, 152, 8, taps, (-1,))
        add_taps(ROWS + r, 8, 152, 8, taps, (1,))
        return 0

    lax.fori_loop(0, 7, first_ends, 0)

    for k, layer in enumerate((2, 1, 0)):
        dilate = 2**layer
        halo = (1, 3, 7)[layer]
        copies[k][0].wait()
        if last:
            copies[k][1].wait()
        step = (ROWS + 2 * halo) // 2
        skip = DHALO[layer] - halo

        def pull_body(it, _):
            at = it * step
            up = ups[pl.ds(UHALO - halo + at, step)].astype(BF)
            pulled = pull_back(up, weights[layer]).reshape(step, UWIDE, CH)
            slope = slopes[k][pl.ds(skip + at, step)].astype(F32)
            slope = slope[:, DSIDE[layer] - 8 : DSIDE[layer] - 8 + UWIDE]
            buf[pl.ds(BASE - halo + at, step), 8:152] = pulled * slope
            return 0

        lax.fori_loop(0, 2, pull_body, 0)
        clear_rows(buf, edges, 8)
        zeros = jnp.zeros((ROWS + 16, CHALO, CH), F32)

        @pl.when(edges[2] == 1)
        def _():
            buf[:, 0:CHALO] = zeros

        @pl.when(edges[3] == 1)
        def _():
            buf[:, CHALO + COLS : WIDE] = zeros

        total = jnp.zeros((CH, CH), F32)
        for b in range(2):
            up = ups[UHALO + 16 * b : UHALO + 16 * b + 16, 8:136].astype(BF)
            if last:
                total = total + grad_of(hids[k][16 * b : 16 * b + 16], up)
            else:
                hids[k][16 * b : 16 * b + 16] = up
        if last:
            grads[k] = total
        else:
            copies[k][1].start()

        taps = rows_of(kernels[layer], 1.0)
        reach = (0, 1, 3)[layer]
        low, high = ((16, 144), (8, 152), (8, 152))[layer]

        def tap_body(it, _):
            for q in range(2):
                r = 2 * it + q - reach
                if last and layer == 0:
                    add_taps(r, low, high, dilate, taps, (-1, 0, 1), back[r // STRIDE])
                else:
                    add_taps(r, low, high, dilate, taps, (-1, 0, 1))
            return 0

        if layer == 1:
            lax.fori_loop(0, (ROWS + 2) // 2, tap_body, 0)
        else:
            lax.fori_loop(0, (ROWS + 2 * reach) // 2, tap_body, 0)

    if not last:
        copies[3][0].wait()
        edge_cols = []
        for b in range(2):
            rows = slice(16 * b, 16 * b + 16)
            value = ups[UHALO + 16 * b : UHALO + 16 * b + 16, 8:136]
            up_out[rows] = value
            up = value.astype(BF)
            hids[3][rows] = up
            pulled = pull_back(up, weights[3])
            value = (pulled.reshape(16, COLS, CH) * slopes[3][rows].astype(F32)).astype(BF)
            pre_out[rows] = value
            strip_left[rows] = value[:, :CHALO]
            strip_right[rows] = value[:, COLS - CHALO :]
            edge_cols.append(ups[UHALO + 16 * b : UHALO + 16 * b + 16, 8:136])
        pack_edges(strip_left, strip_right, edge_cols)
        copies[3][1].start()
        for k in range(count):
            copies[k][1].wait()


def backward(last, edges, pre, sides, part, ends_in, kernels, weights, slopes, hids=(), back=()):
    count = len(slopes)
    block = sds((ROWS, COLS, CH), BF)
    if last:
        outs = [block, sds((count, CH, CH), F32)]
    else:
        strip = sds((ROWS + 16, CHALO, CH), BF)
        outs = [sds((ROWS, COLS, CH), F32), block, strip, strip] + [block] * count
    scratch = [
        pltpu.VMEM((ROWS + 16, WIDE, CH), F32),
        pltpu.VMEM((ROWS + 2 * UHALO, UWIDE, CH), F32),
    ]
    scratch += [pltpu.VMEM(a.shape, BF) for a in slopes]
    scratch += [pltpu.VMEM((ROWS, COLS, CH), BF)] * count
    scratch += [pltpu.SemaphoreType.DMA((2 * count + 1,))]
    args = (edges, pre, *sides, *ends_in, kernels, weights, *back)
    return pl.pallas_call(
        functools.partial(backward_kernel, last),
        out_shape=outs,
        in_specs=[SMEM] + [VMEM] * (len(args) - 1) + [ANY] * (1 + count + len(hids)),
        out_specs=[VMEM] * len(outs) if last else [VMEM] * 4 + [ANY] * count,
        scratch_shapes=scratch,
        compiler_params=pltpu.CompilerParams(vmem_limit_bytes=30 * 2**20),
        cost_estimate=pl.CostEstimate(
            flops=7 * 2 * 5000 * CH * CH, bytes_accessed=14 * 2**20, transcendentals=0
        ),
        name="backward_last" if last else "backward_first",
    )(*args, part, *slopes, *hids)


def late_kernel(*refs):
    count = (len(refs) - 2) // 4
    ins, grads = refs[: 2 * count], refs[2 * count]
    bufs, sem = refs[2 * count + 1 : -1], refs[-1]
    copies = [pltpu.make_async_copy(a, b, sem.at[k]) for k, (a, b) in enumerate(zip(ins, bufs))]
    for copy in copies:
        copy.start()
    for k in range(count):
        copies[2 * k].wait()
        copies[2 * k + 1].wait()
        total = jnp.zeros((CH, CH), F32)
        for b in range(2):
            rows = slice(16 * b, 16 * b + 16)
            total = total + grad_of(bufs[2 * k][rows], bufs[2 * k + 1][rows])
        grads[k] = total


def late_grads(hids, held):
    args = [a for pair in zip(hids, held) for a in pair]
    return pl.pallas_call(
        late_kernel,
        out_shape=sds((len(hids), CH, CH), F32),
        in_specs=[ANY] * len(args),
        out_specs=VMEM,
        scratch_shapes=[pltpu.VMEM((ROWS, COLS, CH), BF)] * len(args)
        + [pltpu.SemaphoreType.DMA((len(args),))],
        compiler_params=pltpu.CompilerParams(vmem_limit_bytes=20 * 2**20),
        cost_estimate=pl.CostEstimate(
            flops=4 * 2 * 4096 * CH * CH, bytes_accessed=8 * 2**20, transcendentals=0
        ),
        name="late_grads",
    )(*args)


def exchange(to_before, to_after, axis):
    ends_at = lax.axis_size(axis) - 1
    forth = [(i, i + 1) for i in range(ends_at)]
    back = [(i + 1, i) for i in range(ends_at)]
    return lax.ppermute(to_after, axis, forth), lax.ppermute(to_before, axis, back)


def local(features_in, cotangent, depth_kernels, point_weights, coarse_weight):
    row, col = lax.axis_index("rows"), lax.axis_index("cols")
    row_end, col_end = lax.axis_size("rows") - 1, lax.axis_size("cols") - 1
    edges = jnp.stack([row == 0, row == row_end, col == 0, col == col_end]).astype(jnp.int32)
    kernels = depth_kernels.astype(F32)

    left, right = exchange(
        features_in[:, : SIDES[0]], features_in[:, COLS - SIDES[0] :], "cols"
    )
    wide = lambda rows: jnp.concatenate([left[rows], features_in[rows], right[rows]], axis=1)
    top, bottom = exchange(wide(slice(0, RH)), wide(slice(ROWS - RH, ROWS)), "rows")
    pieces = (left, features_in, right)
    begun = inner(0, edges, pieces, kernels[:3], point_weights[:3])
    x_mid, x_up, x_down, hid_three, slope_three, *kept = outer(
        0, edges, pieces, top, bottom, kernels[:4], point_weights[:4], begun
    )
    hid_low, slope_low = kept[:3] + [hid_three], kept[3:] + [slope_three]
    top, bottom = exchange(x_up, x_down, "rows")
    begun = inner(1, edges, (x_mid,), kernels[4:7], point_weights[4:7])
    x_last, pre, strip_left, strip_right, grad_top, *kept = outer(
        1, edges, (x_mid,), top, bottom, kernels[4:], point_weights[4:], begun,
        (cotangent,),
    )
    hid_high, slope_high = kept[:3], kept[3:]

    order = lambda things: [things[2], things[1], things[0]]
    sides = exchange(strip_left, strip_right, "cols")
    rows_in = exchange(*ends(pre, *sides, cotangent, kernels[7]), "rows")
    part = own_part(pre, *sides, cotangent, kernels[7])
    upstream, pre, strip_left, strip_right, *held = backward(
        False, edges, pre, sides, part, rows_in,
        kernels[4:], jnp.concatenate([point_weights[4:7], point_weights[3:4]]),
        order(slope_high) + [slope_low[3]],
    )
    sides = exchange(strip_left, strip_right, "cols")
    rows_in = exchange(*ends(pre, *sides, upstream, kernels[3]), "rows")
    output, back, coarse_grad = pool(features_in, cotangent, x_last, coarse_weight)
    grad_mid = late_grads(order(hid_high) + [hid_low[3]], held)
    later, back, grad_mid = lax.optimization_barrier((upstream, back, grad_mid))
    part = own_part(pre, *sides, later, kernels[3])
    input_grad, grad_low = backward(
        True, edges, pre, sides, part, rows_in,
        kernels[:4], point_weights[:3], order(slope_low), order(hid_low), (back,),
    )

    grads = [grad_low[2], grad_low[1], grad_low[0], grad_mid[3], grad_mid[2], grad_mid[1]]
    grads = jnp.stack(grads + [grad_mid[0], grad_top, coarse_grad]).astype(BF)
    shares = lax.all_to_all(grads, "rows", 1, 0, tiled=True)
    summed = shares.reshape(-1, grads.shape[0], CH * 4).astype(F32).sum(axis=0)
    parts = lax.all_gather(summed.astype(BF), "cols", axis=0, tiled=False)
    weight_grads = parts.astype(F32).sum(axis=0).reshape(grads.shape[0], 4, CH)
    return (output, input_grad, weight_grads)


def solution(mesh):
    in_specs = (P("rows", "cols", None), P("rows", "cols", None), P(), P(), P())
    out_specs = (P("rows", "cols", None), P("rows", "cols", None), P(None, "rows", None))
    return jax.shard_map(local, mesh=mesh, in_specs=in_specs, out_specs=out_specs, check_vma=False)
```

```python
import functools

import jax
import jax.numpy as jnp
from jax import lax
from jax.experimental import pallas as pl
from jax.experimental.pallas import tpu as pltpu
from jax.sharding import PartitionSpec as P

STRIDE = 8
F32 = jnp.float32
BF = jnp.bfloat16
C0 = 0.7978845608028654
C1 = 0.7978845608028654 * 0.044715

ROWS, COLS, CH = 32, 128, 128
RH, CHALO = 15, 16
WIDE = COLS + 2 * CHALO
PAD = 8

HALO = (14, 12, 8, 0)
SIDES = (32, 16)
SPANS = (
    ((0, 192), (0, 192), (8, 184), (16, 176)),
    ((0, 160), (0, 160), (8, 152), (16, 144)),
)
DHALO = (2, 3, 8, 0)
DSIDE = (16, 16, 8, 0)

VMEM = pl.BlockSpec(memory_space=pltpu.VMEM)
SMEM = pl.BlockSpec(memory_space=pltpu.SMEM)
ANY = pl.BlockSpec(memory_space=pl.ANY)


def sds(shape, dtype):
    return jax.ShapeDtypeStruct(shape, dtype)


def gelu_parts(half, want_slope):
    square = half * half
    t = jnp.tanh(half * (BF(2 * C0) + BF(8 * C1) * square))
    half_t = half * t
    hidden = half + half_t
    if not want_slope:
        return hidden, None
    slope = (BF(0.5) + BF(0.5) * t) + (half - half_t * t) * (BF(C0) + BF(12 * C1) * square)
    return hidden, slope


def rows_of(kernel, scale):
    return [jnp.broadcast_to(kernel[t : t + 1, :] * scale, (8, CH))[None] for t in range(9)]


def tap_sum(src, row, col, width, dilate, sign, taps, which, start=None):
    total = start
    for i in which:
        for j in (-1, 0, 1):
            at = col + sign * j * dilate
            piece = src[row + sign * i * dilate, at : at + width, :].reshape(width // 8, 8, CH)
            piece = piece * taps[(i + 1) * 3 + j + 1]
            total = piece if total is None else total + piece
    return total


def chunks(low, high, size):
    out = []
    while low < high:
        out.append((low, min(size, high - low)))
        low += size
    return out


def pull_back(upstream, weight):
    return lax.dot_general(
        upstream.reshape(-1, CH), weight, (((1,), (1,)), ((), ())), preferred_element_type=F32
    )


def grad_of(hidden, upstream):
    return lax.dot_general(
        hidden.reshape(-1, CH),
        upstream.reshape(-1, CH),
        (((0,), (0,)), ((), ())),
        preferred_element_type=F32,
    )


INNER = (0, 2, 6)
DSKIP = (4, 3, 0)


def act_rows(src, taps, seg, layer, r, number, want_slope, h_buf, h_at, slope_buf, slope_at, hid_own):
    low, high = SPANS[seg][layer]
    first = SIDES[seg] - DSIDE[layer] - low
    for q in range(number):
        parts = []
        for c, width in chunks(low, high, 32):
            half = tap_sum(src, RH + r + q, PAD + c, width, 2**layer, 1, taps, (-1, 0, 1))
            parts.append(gelu_parts(half.reshape(width, CH).astype(BF), want_slope))
        hidden = jnp.concatenate([p[0] for p in parts], 0)
        h_buf[h_at + q] = hidden
        if hid_own is not None:
            own = hidden.astype(F32)[SIDES[seg] - low : SIDES[seg] - low + COLS]
            hid_own[h_at + q] = own.astype(BF)
        if want_slope:
            slope = jnp.concatenate([p[1] for p in parts], 0)
            slope_buf[slope_at + q] = slope[first : first + COLS + 2 * DSIDE[layer]]


def mixed_rows(h_buf, h_at, src, r, step, seg, layer, weights):
    low, high = SPANS[seg][layer]
    mixed = jnp.dot(
        h_buf[pl.ds(h_at, step)].reshape(step * (high - low), CH),
        weights[layer],
        preferred_element_type=F32,
    ).reshape(step, high - low, CH)
    return src[pl.ds(RH + r, step), PAD + low : PAD + high] + mixed


def fill_row(buf, row, at, pieces, r):
    for piece in pieces:
        width = piece.shape[1]
        buf[row, at : at + width] = piece[r].astype(F32)
        at += width


def clear_columns(ref, edges, seg):
    side = SIDES[seg]
    count = ref.shape[0]

    @pl.when(edges[2] == 1)
    def _():
        ref[:, PAD : PAD + side] = jnp.zeros((count, side, CH), F32)

    @pl.when(edges[3] == 1)
    def _():
        ref[:, PAD + side + COLS : PAD + 2 * side + COLS] = jnp.zeros((count, side, CH), F32)


def clear_rows(ref, edges, number):
    count, breadth = ref.shape[0], ref.shape[1]

    @pl.when(edges[0] == 1)
    def _():
        ref[0:number] = jnp.zeros((number, breadth, CH), F32)

    @pl.when(edges[1] == 1)
    def _():
        ref[count - number : count] = jnp.zeros((number, breadth, CH), F32)


def inner_kernel(seg, *refs):
    refs = list(refs)
    take = lambda n: [refs.pop(0) for _ in range(n)]
    edges = take(1)[0]
    pieces = take(1 if seg else 3)
    kernels, weights = take(2)
    hid_out, slope_out, x_all = take(3), take(3), take(1)[0]
    x_out = [x_all.at[pl.ds(o, n)] for o, n in ((0, 8), (8, 16), (24, 18))]
    x_bufs, h_bufs, slopes = take(4), take(3), take(3)
    hid_two, sem = take(2)

    def build(r, _):
        fill_row(x_bufs[0], RH + r, PAD, pieces, r)
        return 0

    lax.fori_loop(0, ROWS, build, 0)
    copies = []

    def send(src, dst, slot):
        copies.append(pltpu.make_async_copy(src, dst, sem.at[slot]))
        copies[-1].start()

    for layer in range(3):
        src, dst = x_bufs[layer], x_bufs[layer + 1]
        h_buf, slope_buf = h_bufs[layer], slopes[layer]
        low, high = SPANS[seg][layer]
        edge = INNER[layer]
        first, number = edge + 1, ROWS - 2 - 2 * edge
        group = (5, 2, 6)[layer]
        taps = rows_of(kernels[layer], 0.5)
        hid_own = hid_two if layer == 2 else None

        def body(it, _):
            at = group * it
            act_rows(
                src, taps, seg, layer, first + at, group, True, h_buf, at, slope_buf, at, hid_own
            )
            return 0

        lax.fori_loop(0, number // group, body, 0)
        rows = pl.ds(first, number)
        hid_src = hid_two if layer == 2 else h_buf.at[:, pl.ds(SIDES[seg] - low, COLS)]
        send(hid_src, hid_out[layer].at[rows], layer)
        send(slope_buf, slope_out[layer].at[pl.ds(DHALO[layer] + first, number)], 3 + layer)

        step = (15, 13, 9)[layer]

        def mix_body(it, _):
            at = it * step
            dst[pl.ds(RH + first + at, step), PAD + low : PAD + high] = mixed_rows(
                h_buf, at, src, first + at, step, seg, layer, weights
            )
            return 0

        lax.fori_loop(0, number // step, mix_body, 0)
        clear_columns(dst, edges, seg)
        depth = (4, 8, 18)[layer]
        send(dst.at[pl.ds(RH + first, depth)], x_out[layer].at[pl.ds(0, depth)], 6 + layer)
        if layer < 2:
            send(
                dst.at[pl.ds(RH + first + number - depth, depth)],
                x_out[layer].at[pl.ds(depth, depth)],
                9 + layer,
            )
    for copy in copies:
        copy.wait()


SLOPE_SHAPES = [(ROWS + 2 * DHALO[k], COLS + 2 * DSIDE[k], CH) for k in range(4)]


def x_wide(seg):
    return COLS + 2 * SIDES[seg] + 2 * PAD


def inner(seg, edges, pieces, kernels, weights):
    outs = [sds((ROWS, COLS, CH), BF)] * 3
    outs += [sds(s, BF) for s in SLOPE_SHAPES[:3]]
    outs += [sds((42, x_wide(seg), CH), F32)]
    numbers = [ROWS - 2 - 2 * e for e in INNER]
    breadth = [b - a for a, b in SPANS[seg]]
    scratch = [pltpu.VMEM((ROWS + 2 * RH, x_wide(seg), CH), F32)] * 4
    scratch += [pltpu.VMEM((numbers[k], breadth[k], CH), BF) for k in range(3)]
    scratch += [pltpu.VMEM((numbers[k], SLOPE_SHAPES[k][1], CH), BF) for k in range(3)]
    scratch += [pltpu.VMEM((numbers[2], COLS, CH), BF), pltpu.SemaphoreType.DMA((11,))]
    return pl.pallas_call(
        functools.partial(inner_kernel, seg),
        out_shape=outs,
        in_specs=[SMEM] + [VMEM] * (2 + len(pieces)),
        out_specs=[ANY] * 7,
        scratch_shapes=scratch,
        compiler_params=pltpu.CompilerParams(vmem_limit_bytes=52 * 2**20),
        cost_estimate=pl.CostEstimate(
            flops=4 * 2 * 3000 * CH * CH, bytes_accessed=12 * 2**20, transcendentals=0
        ),
        name="inner_last" if seg else "inner_first",
    )(edges, *pieces, kernels, weights)


def outer_kernel(seg, *refs):
    refs = list(refs)
    take = lambda n: [refs.pop(0) for _ in range(n)]
    edges = take(1)[0]
    pieces = take(1 if seg else 3)
    top, bottom, kernels, weights = take(4)
    if seg:
        cot = take(1)[0]
    x_all = take(1)[0]
    x_in = [x_all.at[pl.ds(o, n)] for o, n in ((0, 8), (8, 16), (24, 18))]
    take(6)
    if seg:
        out, pre, strip_left, strip_right, hid_three = take(5)
    else:
        x_out, up_out, down_out, hid_three, slope_three = take(5)
    hid_out, slope_out = take(3), take(3)
    x_bufs, h_bufs, slopes = take(4), take(4), take(4)
    hid_two, own_buf, sem = take(3)
    side = SIDES[seg]

    loads = []
    for layer in range(3):
        first = INNER[layer] + 1
        depth = (4, 8, 18)[layer]
        spots = [(first, 0)] if layer == 2 else [(first, 0), (ROWS - first - depth, depth)]
        for k, (r, at) in enumerate(spots):
            copy = pltpu.make_async_copy(
                x_in[layer].at[pl.ds(at, depth)],
                x_bufs[layer + 1].at[pl.ds(RH + r, depth)],
                sem.at[20 + 2 * layer + k],
            )
            copy.start()
            loads.append((layer, copy))

    for r in (0, 1, ROWS - 2, ROWS - 1):
        fill_row(x_bufs[0], RH + r, PAD, pieces, r)

    def build_ends(r, _):
        fill_row(x_bufs[0], r, PAD, [top], r)
        fill_row(x_bufs[0], RH + ROWS + r, PAD, [bottom], r)
        return 0

    lax.fori_loop(0, RH, build_ends, 0)
    copies = []

    def send(src, dst, slot):
        copies.append(pltpu.make_async_copy(src, dst, sem.at[slot]))
        copies[-1].start()

    for layer in range(3):
        src, dst = x_bufs[layer], x_bufs[layer + 1]
        h_buf, slope_buf = h_bufs[layer], slopes[layer]
        halo, edge, dhalo = HALO[layer], INNER[layer], DHALO[layer]
        low, high = SPANS[seg][layer]
        taps = rows_of(kernels[layer], 0.5)
        hid_own = hid_two if layer == 2 else None
        skip = DSKIP[layer]
        kept = 5 - skip

        if skip:

            def far_body(it, _):
                low_side = it >= skip
                at = jnp.where(low_side, 15 + 3 * kept + 3 * (it - skip), 3 * it)
                r = jnp.where(low_side, ROWS - 1 - edge - 15, -halo) + at
                act_rows(src, taps, seg, layer, r, 3, False, h_buf, at, None, 0, None)
                return 0

            lax.fori_loop(0, 2 * skip, far_body, 0)

        def near_body(it, _):
            low_side = it >= kept
            at = jnp.where(low_side, 15 + 3 * (it - kept), 3 * skip + 3 * it)
            r = jnp.where(low_side, ROWS - 1 - edge - 15, -halo) + at
            act_rows(src, taps, seg, layer, r, 3, True, h_buf, at, slope_buf, 3 * it, hid_own)
            return 0

        lax.fori_loop(0, 2 * kept, near_body, 0)

        whole = hid_two if layer == 2 else h_buf
        cols = pl.ds(0, COLS) if layer == 2 else pl.ds(side - low, COLS)
        send(whole.at[pl.ds(halo, edge + 1), cols], hid_out[layer].at[pl.ds(0, edge + 1)], layer)
        send(
            whole.at[pl.ds(15, edge + 1), cols],
            hid_out[layer].at[pl.ds(ROWS - 1 - edge, edge + 1)],
            3 + layer,
        )
        number = 3 * kept
        send(slope_buf.at[pl.ds(0, number)], slope_out[layer].at[pl.ds(0, number)], 6 + layer)
        send(
            slope_buf.at[pl.ds(number, number)],
            slope_out[layer].at[pl.ds(dhalo + ROWS - 1 - edge, number)],
            9 + layer,
        )
        for which, copy in loads:
            if which == layer:
                copy.wait()

        def mix_body(it, _):
            r = jnp.where(it == 0, -halo, ROWS - 1 - edge)
            dst[pl.ds(RH + r, 15), PAD + low : PAD + high] = mixed_rows(
                h_buf, 15 * it, src, r, 15, seg, layer, weights
            )
            return 0

        lax.fori_loop(0, 2, mix_body, 0)
        clear_rows(dst, edges, RH)
        clear_columns(dst, edges, seg)

    taps = rows_of(kernels[3], 0.5)

    def last_body(it, _):
        act_rows(
            x_bufs[3], taps, seg, 3, 4 * it, 4, True, h_bufs[3], 4 * it, slopes[3], 4 * it, None
        )
        return 0

    lax.fori_loop(0, ROWS // 4, last_body, 0)
    if seg:
        send(h_bufs[3], hid_three, 12)
    else:
        send(h_bufs[3].at[:, pl.ds(CHALO, COLS)], hid_three, 12)
        send(slopes[3], slope_three, 13)

    def last_mix(it, _):
        at = 16 * it
        value = mixed_rows(h_bufs[3], at, x_bufs[3], at, 16, seg, 3, weights)
        own_buf[pl.ds(at, 16)] = value.astype(BF)
        return 0

    lax.fori_loop(0, 2, last_mix, 0)
    if seg:
        send(own_buf, out, 14)
        edge_cols = []
        for b in range(2):
            rows = slice(16 * b, 16 * b + 16)
            up = cot[rows]
            pulled = pull_back(up, weights[3])
            value = pulled.reshape(16, COLS, CH) * slopes[3][rows].astype(F32)
            value = value.astype(BF)
            pre[rows] = value
            strip_left[rows] = value[:, :CHALO]
            strip_right[rows] = value[:, COLS - CHALO :]
            edge_cols.append(up.astype(F32))
        pack_edges(strip_left, strip_right, edge_cols)
    else:
        zeros = jnp.zeros((ROWS, CHALO, CH), BF)

        @pl.when(edges[2] == 1)
        def _():
            own_buf[:, 0:CHALO] = zeros

        @pl.when(edges[3] == 1)
        def _():
            own_buf[:, CHALO + COLS : WIDE] = zeros

        send(own_buf, x_out, 14)
        send(own_buf.at[pl.ds(0, RH)], up_out, 15)
        send(own_buf.at[pl.ds(ROWS - RH, RH)], down_out, 16)
    for copy in copies:
        copy.wait()


def pack_edges(strip_left, strip_right, halves):
    first, second = halves
    strip_left[ROWS : ROWS + 16] = jnp.concatenate([first[:, :8], second[:, :8]], 1).astype(BF)
    strip_right[ROWS : ROWS + 16] = jnp.concatenate(
        [first[:, COLS - 8 :], second[:, COLS - 8 :]], 1
    ).astype(BF)


def outer(seg, edges, pieces, top, bottom, kernels, weights, begun, extra=()):
    block = sds((ROWS, COLS, CH), BF)
    strip = sds((ROWS + 16, CHALO, CH), BF)
    if seg:
        outs = [block, block, strip, strip, block]
        specs = [ANY] + [VMEM] * 3 + [ANY]
    else:
        ends_shape = sds((RH, WIDE, CH), BF)
        outs = [sds((ROWS, WIDE, CH), BF), ends_shape, ends_shape, block, block]
        specs = [ANY] * 5
    shift = len(outs)
    outs = outs + [sds(a.shape, BF) for a in begun[:6]]
    specs = specs + [ANY] * 6
    args = (edges, *pieces, top, bottom, kernels, weights, *extra, *begun[6:], *begun[:6])
    breadth = [b - a for a, b in SPANS[seg]]
    scratch = [pltpu.VMEM((ROWS + 2 * RH, x_wide(seg), CH), F32)] * 4
    heights = [30, 30, 30, ROWS]
    scratch += [pltpu.VMEM((heights[k], breadth[k], CH), BF) for k in range(4)]
    tall = [6 * (5 - DSKIP[k]) for k in range(3)] + [ROWS]
    scratch += [pltpu.VMEM((tall[k], SLOPE_SHAPES[k][1], CH), BF) for k in range(4)]
    scratch += [pltpu.VMEM((30, COLS, CH), BF), pltpu.VMEM((ROWS, breadth[3], CH), BF)]
    scratch += [pltpu.SemaphoreType.DMA((26,))]
    return pl.pallas_call(
        functools.partial(outer_kernel, seg),
        out_shape=outs,
        in_specs=[SMEM] + [VMEM] * (len(args) - 8) + [ANY] * 7,
        out_specs=specs,
        scratch_shapes=scratch,
        input_output_aliases={len(args) - 6 + k: shift + k for k in range(6)},
        compiler_params=pltpu.CompilerParams(vmem_limit_bytes=52 * 2**20),
        cost_estimate=pl.CostEstimate(
            flops=4 * 2 * 5000 * CH * CH, bytes_accessed=12 * 2**20, transcendentals=0
        ),
        name="outer_last" if seg else "outer_first",
    )(*args)


def pool_kernel(feature, cot, x_last, weight, out, back, grad):
    total = None
    for b in range(ROWS // STRIDE):
        rows = slice(STRIDE * b, STRIDE * (b + 1))

        def block_sum(ref):
            value = ref[STRIDE * b].astype(F32)
            for r in range(1, STRIDE):
                value = value + ref[STRIDE * b + r].astype(F32)
            return value.reshape(COLS // STRIDE, STRIDE, CH).sum(axis=1)

        pooled = (block_sum(feature) * (1.0 / (STRIDE * STRIDE))).astype(BF)
        block_cot = block_sum(cot).astype(BF)
        coarse = jnp.dot(pooled, weight[...], preferred_element_type=F32)
        value = x_last[rows].astype(F32).reshape(STRIDE, COLS // STRIDE, STRIDE, CH)
        value = value + coarse[:, None, :][None]
        out[rows] = value.reshape(STRIDE, COLS, CH).astype(BF)
        back[b] = pull_back(block_cot, weight[...]) * (1.0 / (STRIDE * STRIDE))
        part = grad_of(pooled, block_cot)
        total = part if total is None else total + part
    grad[...] = total


def pool(feature, cot, x_last, weight):
    small = sds((ROWS // STRIDE, COLS // STRIDE, CH), F32)
    return pl.pallas_call(
        pool_kernel,
        out_shape=[sds((ROWS, COLS, CH), BF), small, sds((CH, CH), F32)],
        in_specs=[VMEM] * 4,
        out_specs=[VMEM] * 3,
        compiler_params=pltpu.CompilerParams(vmem_limit_bytes=16 * 2**20),
        cost_estimate=pl.CostEstimate(flops=10**9, bytes_accessed=4 * 2**20, transcendentals=0),
        name="pool",
    )(feature, cot, x_last, weight)


BASE = 8


def fill_pre(buf, row, pre, from_left, from_right, r):
    buf[row, 0:16] = from_left[r].astype(F32)
    buf[row, 16:144] = pre[r].astype(F32)
    buf[row, 144:160] = from_right[r].astype(F32)


def base_row(base, from_left, from_right, r, half):
    side = slice(8 * half, 8 * half + 8)
    return jnp.concatenate(
        [
            from_left[ROWS + r].astype(F32)[side],
            base[r + 16 * half].astype(F32),
            from_right[ROWS + r].astype(F32)[side],
        ],
        0,
    )


def row_taps(buf, r, taps, which, low=8, high=152):
    parts = []
    for c, width in chunks(low, high, 32):
        parts.append(tap_sum(buf, r, c, width, 8, -1, taps, which).reshape(width, CH))
    return jnp.concatenate(parts, 0)


def ends_kernel(pre, from_left, from_right, base, kernel, up, down, buf):
    taps = rows_of(kernel, 1.0)

    def build(r, _):
        fill_pre(buf, r, pre, from_left, from_right, r)
        fill_pre(buf, 16 + r, pre, from_left, from_right, 16 + r)
        return 0

    lax.fori_loop(0, 16, build, 0)
    zeros = jnp.zeros((8, CH), F32)

    def one(r, half, which):
        value = row_taps(buf, r + 16 * half, taps, which)
        value = value + base_row(base, from_left, from_right, r, half)
        return jnp.concatenate([zeros, value, zeros], 0).astype(BF)

    def body(r, _):
        up[r] = one(r, 0, (-1, 0))
        down[r] = one(ROWS - 23 + r, 1, (0, 1))
        return 0

    lax.fori_loop(0, 7, body, 0)

    def body_pre(r, _):
        up[7 + r] = buf[r].astype(BF)
        down[7 + r] = buf[ROWS - 8 + r].astype(BF)
        return 0

    lax.fori_loop(0, 8, body_pre, 0)


def ends(pre, from_left, from_right, base, kernel):
    strip = sds((RH, WIDE, CH), BF)
    return pl.pallas_call(
        ends_kernel,
        out_shape=[strip, strip],
        in_specs=[VMEM] * 5,
        out_specs=[VMEM] * 2,
        scratch_shapes=[pltpu.VMEM((ROWS, WIDE, CH), F32)],
        compiler_params=pltpu.CompilerParams(vmem_limit_bytes=20 * 2**20),
        cost_estimate=pl.CostEstimate(flops=10**8, bytes_accessed=6 * 2**20, transcendentals=0),
        name="ends",
    )(pre, from_left, from_right, base, kernel)


def own_kernel(pre, from_left, from_right, base, kernel, out, buf):
    taps = rows_of(kernel, 1.0)

    def build(r, _):
        fill_pre(buf, r, pre, from_left, from_right, r)
        fill_pre(buf, 16 + r, pre, from_left, from_right, 16 + r)
        return 0

    lax.fori_loop(0, 16, build, 0)

    def one(r, half, which):
        value = row_taps(buf, r + 16 * half, taps, which)
        out[r + 16 * half] = value + base_row(base, from_left, from_right, r, half)

    def body_edge(r, _):
        one(r, 0, (-1, 0))
        one(r + 8, 1, (0, 1))
        return 0

    def body_middle(r, _):
        one(r + 8, 0, (-1, 0, 1))
        one(r, 1, (-1, 0, 1))
        return 0

    lax.fori_loop(0, 8, body_edge, 0)
    lax.fori_loop(0, 8, body_middle, 0)


def own_part(pre, from_left, from_right, base, kernel):
    return pl.pallas_call(
        own_kernel,
        out_shape=sds((ROWS, UWIDE, CH), F32),
        in_specs=[VMEM] * 5,
        out_specs=VMEM,
        scratch_shapes=[pltpu.VMEM((ROWS, WIDE, CH), F32)],
        compiler_params=pltpu.CompilerParams(vmem_limit_bytes=20 * 2**20),
        cost_estimate=pl.CostEstimate(
            flops=2 * 10**9, bytes_accessed=6 * 2**20, transcendentals=0
        ),
        name="own_part",
    )(pre, from_left, from_right, base, kernel)


UHALO = 7
UWIDE = COLS + 16


def backward_kernel(last, *refs):
    refs = list(refs)
    take = lambda n: [refs.pop(0) for _ in range(n)]
    edges, pre, from_left, from_right, top, bottom = take(6)
    kernels, weights = take(2)
    count = 3 if last else 4
    if last:
        back = take(1)[0]
    part_in = take(1)[0]
    slope_in = take(count)
    if last:
        hid_in = take(count)
        out, grads = take(2)
    else:
        up_out, pre_out, strip_left, strip_right = take(4)
        held_out = take(count)
    buf, ups = take(2)
    slopes = take(count)
    hids = take(count)
    sem = take(1)[0]

    copies = []
    for k in range(count):
        copies.append([pltpu.make_async_copy(slope_in[k], slopes[k], sem.at[2 * k])])
        if last:
            copies[-1].append(pltpu.make_async_copy(hid_in[k], hids[k], sem.at[2 * k + 1]))
        else:
            copies[-1].append(pltpu.make_async_copy(hids[k], held_out[k], sem.at[2 * k + 1]))
        copies[-1][0].start()
        if last:
            copies[-1][1].start()

    part_copy = pltpu.make_async_copy(
        part_in, ups.at[pl.ds(UHALO, ROWS)], sem.at[2 * count]
    )
    part_copy.start()

    def build(r, _):
        fill_pre(buf, BASE + r, pre, from_left, from_right, r)
        fill_pre(buf, BASE + 24 + r, pre, from_left, from_right, 24 + r)
        return 0

    lax.fori_loop(0, 8, build, 0)

    def build_pre(r, _):
        buf[r] = top[7 + r].astype(F32)
        buf[BASE + ROWS + r] = bottom[7 + r].astype(F32)
        return 0

    lax.fori_loop(0, 8, build_pre, 0)

    def build_ups(r, _):
        ups[r] = top[r].astype(F32)[8:152]
        ups[UHALO + ROWS + r] = bottom[r].astype(F32)[8:152]
        return 0

    lax.fori_loop(0, 7, build_ups, 0)

    def add_taps(r, low, high, dilate, taps, which, extra=None):
        for c, width in chunks(low, high, 32):
            start = ups[UHALO + r, c - 8 : c - 8 + width].reshape(width // 8, 8, CH)
            total = tap_sum(buf, BASE + r, c, width, dilate, -1, taps, which, start)
            if extra is not None:
                total = total + extra[(c - low) // 8 : (c - low + width) // 8][:, None, :]
                out[r, c - low : c - low + width] = total.reshape(width, CH).astype(BF)
            else:
                ups[UHALO + r, c - 8 : c - 8 + width] = total.reshape(width, CH)

    taps = rows_of(kernels[3], 1.0)

    part_copy.wait()

    def first_upper(r, _):
        add_taps(r, 8, 152, 8, taps, (1,))
        add_taps(24 + r, 8, 152, 8, taps, (-1,))
        return 0

    lax.fori_loop(0, 8, first_upper, 0)

    def first_ends(r, _):
        add_taps(r - 7, 8, 152, 8, taps, (-1,))
        add_taps(ROWS + r, 8, 152, 8, taps, (1,))
        return 0

    lax.fori_loop(0, 7, first_ends, 0)

    for k, layer in enumerate((2, 1, 0)):
        dilate = 2**layer
        halo = (1, 3, 7)[layer]
        copies[k][0].wait()
        if last:
            copies[k][1].wait()
        step = (ROWS + 2 * halo) // 2
        skip = DHALO[layer] - halo

        def pull_body(it, _):
            at = it * step
            up = ups[pl.ds(UHALO - halo + at, step)].astype(BF)
            pulled = pull_back(up, weights[layer]).reshape(step, UWIDE, CH)
            slope = slopes[k][pl.ds(skip + at, step)].astype(F32)
            slope = slope[:, DSIDE[layer] - 8 : DSIDE[layer] - 8 + UWIDE]
            buf[pl.ds(BASE - halo + at, step), 8:152] = pulled * slope
            return 0

        lax.fori_loop(0, 2, pull_body, 0)
        clear_rows(buf, edges, 8)
        zeros = jnp.zeros((ROWS + 16, CHALO, CH), F32)

        @pl.when(edges[2] == 1)
        def _():
            buf[:, 0:CHALO] = zeros

        @pl.when(edges[3] == 1)
        def _():
            buf[:, CHALO + COLS : WIDE] = zeros

        total = jnp.zeros((CH, CH), F32)
        for b in range(2):
            up = ups[UHALO + 16 * b : UHALO + 16 * b + 16, 8:136].astype(BF)
            if last:
                total = total + grad_of(hids[k][16 * b : 16 * b + 16], up)
            else:
                hids[k][16 * b : 16 * b + 16] = up
        if last:
            grads[k] = total
        else:
            copies[k][1].start()

        taps = rows_of(kernels[layer], 1.0)
        reach = (0, 1, 3)[layer]
        low, high = ((16, 144), (8, 152), (8, 152))[layer]

        def tap_body(it, _):
            for q in range(2):
                r = 2 * it + q - reach
                if last and layer == 0:
                    add_taps(r, low, high, dilate, taps, (-1, 0, 1), back[r // STRIDE])
                else:
                    add_taps(r, low, high, dilate, taps, (-1, 0, 1))
            return 0

        if layer == 1:
            lax.fori_loop(0, (ROWS + 2) // 2, tap_body, 0)
        else:
            lax.fori_loop(0, (ROWS + 2 * reach) // 2, tap_body, 0)

    if not last:
        copies[3][0].wait()
        edge_cols = []
        for b in range(2):
            rows = slice(16 * b, 16 * b + 16)
            value = ups[UHALO + 16 * b : UHALO + 16 * b + 16, 8:136]
            up_out[rows] = value
            up = value.astype(BF)
            hids[3][rows] = up
            pulled = pull_back(up, weights[3])
            value = (pulled.reshape(16, COLS, CH) * slopes[3][rows].astype(F32)).astype(BF)
            pre_out[rows] = value
            strip_left[rows] = value[:, :CHALO]
            strip_right[rows] = value[:, COLS - CHALO :]
            edge_cols.append(ups[UHALO + 16 * b : UHALO + 16 * b + 16, 8:136])
        pack_edges(strip_left, strip_right, edge_cols)
        copies[3][1].start()
        for k in range(count):
            copies[k][1].wait()


def backward(last, edges, pre, sides, part, ends_in, kernels, weights, slopes, hids=(), back=()):
    count = len(slopes)
    block = sds((ROWS, COLS, CH), BF)
    if last:
        outs = [block, sds((count, CH, CH), F32)]
    else:
        strip = sds((ROWS + 16, CHALO, CH), BF)
        outs = [sds((ROWS, COLS, CH), F32), block, strip, strip] + [block] * count
    scratch = [
        pltpu.VMEM((ROWS + 16, WIDE, CH), F32),
        pltpu.VMEM((ROWS + 2 * UHALO, UWIDE, CH), F32),
    ]
    scratch += [pltpu.VMEM(a.shape, BF) for a in slopes]
    scratch += [pltpu.VMEM((ROWS, COLS, CH), BF)] * count
    scratch += [pltpu.SemaphoreType.DMA((2 * count + 1,))]
    args = (edges, pre, *sides, *ends_in, kernels, weights, *back)
    return pl.pallas_call(
        functools.partial(backward_kernel, last),
        out_shape=outs,
        in_specs=[SMEM] + [VMEM] * (len(args) - 1) + [ANY] * (1 + count + len(hids)),
        out_specs=[VMEM] * len(outs) if last else [VMEM] * 4 + [ANY] * count,
        scratch_shapes=scratch,
        compiler_params=pltpu.CompilerParams(vmem_limit_bytes=30 * 2**20),
        cost_estimate=pl.CostEstimate(
            flops=7 * 2 * 5000 * CH * CH, bytes_accessed=14 * 2**20, transcendentals=0
        ),
        name="backward_last" if last else "backward_first",
    )(*args, part, *slopes, *hids)


def late_kernel(*refs):
    count = (len(refs) - 2) // 4
    ins, grads = refs[: 2 * count], refs[2 * count]
    bufs, sem = refs[2 * count + 1 : -1], refs[-1]
    copies = [pltpu.make_async_copy(a, b, sem.at[k]) for k, (a, b) in enumerate(zip(ins, bufs))]
    for copy in copies:
        copy.start()
    for k in range(count):
        copies[2 * k].wait()
        copies[2 * k + 1].wait()
        total = jnp.zeros((CH, CH), F32)
        for b in range(2):
            rows = slice(16 * b, 16 * b + 16)
            total = total + grad_of(bufs[2 * k][rows], bufs[2 * k + 1][rows])
        grads[k] = total


def late_grads(hids, held):
    args = [a for pair in zip(hids, held) for a in pair]
    return pl.pallas_call(
        late_kernel,
        out_shape=sds((len(hids), CH, CH), F32),
        in_specs=[ANY] * len(args),
        out_specs=VMEM,
        scratch_shapes=[pltpu.VMEM((ROWS, COLS, CH), BF)] * len(args)
        + [pltpu.SemaphoreType.DMA((len(args),))],
        compiler_params=pltpu.CompilerParams(vmem_limit_bytes=20 * 2**20),
        cost_estimate=pl.CostEstimate(
            flops=5 * 2 * 4096 * CH * CH, bytes_accessed=8 * 2**20, transcendentals=0
        ),
        name="late_grads",
    )(*args)


def exchange(to_before, to_after, axis):
    ends_at = lax.axis_size(axis) - 1
    forth = [(i, i + 1) for i in range(ends_at)]
    back = [(i + 1, i) for i in range(ends_at)]
    return lax.ppermute(to_after, axis, forth), lax.ppermute(to_before, axis, back)


def local(features_in, cotangent, depth_kernels, point_weights, coarse_weight):
    row, col = lax.axis_index("rows"), lax.axis_index("cols")
    row_end, col_end = lax.axis_size("rows") - 1, lax.axis_size("cols") - 1
    edges = jnp.stack([row == 0, row == row_end, col == 0, col == col_end]).astype(jnp.int32)
    kernels = depth_kernels.astype(F32)

    left, right = exchange(
        features_in[:, : SIDES[0]], features_in[:, COLS - SIDES[0] :], "cols"
    )
    wide = lambda rows: jnp.concatenate([left[rows], features_in[rows], right[rows]], axis=1)
    top, bottom = exchange(wide(slice(0, RH)), wide(slice(ROWS - RH, ROWS)), "rows")
    pieces = (left, features_in, right)
    begun = inner(0, edges, pieces, kernels[:3], point_weights[:3])
    x_mid, x_up, x_down, hid_three, slope_three, *kept = outer(
        0, edges, pieces, top, bottom, kernels[:4], point_weights[:4], begun
    )
    hid_low, slope_low = kept[:3] + [hid_three], kept[3:] + [slope_three]
    top, bottom = exchange(x_up, x_down, "rows")
    begun = inner(1, edges, (x_mid,), kernels[4:7], point_weights[4:7])
    x_last, pre, strip_left, strip_right, hid_top, *kept = outer(
        1, edges, (x_mid,), top, bottom, kernels[4:], point_weights[4:], begun,
        (cotangent,),
    )
    hid_high, slope_high = kept[:3], kept[3:]

    order = lambda things: [things[2], things[1], things[0]]
    sides = exchange(strip_left, strip_right, "cols")
    rows_in = exchange(*ends(pre, *sides, cotangent, kernels[7]), "rows")
    part = own_part(pre, *sides, cotangent, kernels[7])
    upstream, pre, strip_left, strip_right, *held = backward(
        False, edges, pre, sides, part, rows_in,
        kernels[4:], jnp.concatenate([point_weights[4:7], point_weights[3:4]]),
        order(slope_high) + [slope_low[3]],
    )
    sides = exchange(strip_left, strip_right, "cols")
    rows_in = exchange(*ends(pre, *sides, upstream, kernels[3]), "rows")
    output, back, coarse_grad = pool(features_in, cotangent, x_last, coarse_weight)
    grad_mid = late_grads(
        order(hid_high) + [hid_low[3], hid_top], list(held) + [cotangent]
    )
    later, back, grad_mid = lax.optimization_barrier((upstream, back, grad_mid))
    part = own_part(pre, *sides, later, kernels[3])
    input_grad, grad_low = backward(
        True, edges, pre, sides, part, rows_in,
        kernels[:4], point_weights[:3], order(slope_low), order(hid_low), (back,),
    )

    grads = [grad_low[2], grad_low[1], grad_low[0], grad_mid[3], grad_mid[2], grad_mid[1]]
    grads = jnp.stack(grads + [grad_mid[0], grad_mid[4], coarse_grad]).astype(BF)
    shares = lax.all_to_all(grads, "rows", 1, 0, tiled=True)
    summed = shares.reshape(-1, grads.shape[0], CH * 4).astype(F32).sum(axis=0)
    parts = lax.all_gather(summed.astype(BF), "cols", axis=0, tiled=False)
    weight_grads = parts.astype(F32).sum(axis=0).reshape(grads.shape[0], 4, CH)
    return (output, input_grad, weight_grads)


def solution(mesh):
    in_specs = (P("rows", "cols", None), P("rows", "cols", None), P(), P(), P())
    out_specs = (P("rows", "cols", None), P("rows", "cols", None), P(None, "rows", None))
    return jax.shard_map(local, mesh=mesh, in_specs=in_specs, out_specs=out_specs, check_vma=False)
```
